128 devices in a mesh: dp: 16 (over x, z), tensor: 8 (over y, core).
Axes of the slice: x: 4, y: 4, z: 4, core: 2. Of those that a mesh axis runs over, the one named last changes fastest.
Arguments:
- tokens: bfloat16 [8192, 4096], P('dp', 'tensor'), may hold values from -6 to 6
- norm_gain: float32 [4096], replicated, may hold values from 0.1 to 1.9
- doc_ids: int32 [8192], P('dp'), may hold values from 0 to 8191, as said below
- panel_plan: int32 [256], P('dp'), may hold values from 0 to 255, as said below
- query_weight: bfloat16 [4096, 4096], P(None, 'tensor'), may hold values from -0.09375 to 0.09375
- key_weight: bfloat16 [4096, 1024], P(None, 'tensor'), may hold values from -0.09375 to 0.09375
- value_weight: bfloat16 [4096, 1024], P(None, 'tensor'), may hold values from -0.09375 to 0.09375
- out_weight: bfloat16 [4096, 4096], P('tensor'), may hold values from -0.5 to 0.5
- cotangent: bfloat16 [8192, 4096], P('dp', 'tensor'), may hold values from -6 to 6
Outputs:
- output: bfloat16 [8192, 4096], P('dp', 'tensor')
- grad_tokens: bfloat16 [8192, 4096], P('dp', 'tensor')
- grad_query: bfloat16 [4096, 4096], P(None, 'tensor')
- grad_key: bfloat16 [4096, 1024], P(None, 'tensor')
- grad_value: bfloat16 [4096, 1024], P(None, 'tensor')
The draws below stay inside these ranges and needn't reach their ends.
Inputs may be any that keep to these rules, and one draw needn't show every extreme that they name: A permutation: loader panel i goes to device panel_plan[i] // 16 of dp, into slot panel_plan[i] % 16; the 16 panels of one device of dp go to 16 different devices. `doc_ids`: in planned order each document is a run of consecutive rows inside one block of 512 rows, and its id is the planned row index of its first row; the last planned row is a document of its own.
All inputs are finite; a program needn't handle non-finite values.
Results may differ from the reference program's by a relative error of at most 0.02.
Values may be sent and summed in bfloat16 or wider, within the bound.
No kernel may reach another device: no remote copies, remote signals or barrier semaphores. Data moves between devices by JAX's collectives and lax.ppermute only.
A program may use at most 128 MiB of HBM per device.

```python
import jax
import jax.numpy as jnp
from jax import lax

D = 4096
HEADS = 32
KV_HEADS = 8
HD = 128
TOK_DEV = 512
PANELS_DEV = 16
PANEL = 32
TOKENS = 8192
PANELS = 256
N_DP = 16
N_TENSOR = 8


def planned_layout(key):
    shifts = jax.random.permutation(jax.random.fold_in(key, 101), N_DP)[:PANELS_DEV]
    outer_map = jax.random.permutation(jax.random.fold_in(key, 102), N_DP)
    inner_map = jax.random.permutation(jax.random.fold_in(key, 103), N_DP)
    targets = outer_map[(inner_map[:, None] + shifts[None, :]) % N_DP]
    scores = jax.random.randint(jax.random.fold_in(key, 104), (N_DP, PANELS_DEV), 0, 1 << 20)
    columns = jnp.arange(PANELS_DEV, dtype=jnp.int32)[None, :]
    scores = scores * PANELS_DEV + columns
    ranking = jnp.argsort(scores, axis=1).astype(jnp.int32)
    slot_ids = ranking[targets, columns]
    return (targets * PANELS_DEV + slot_ids).reshape(-1).astype(jnp.int32)


def draw_panel_plan(key, part):
    layout = planned_layout(key)
    return layout


def draw_doc_ids(key, part):
    layout = planned_layout(key)
    key = jax.random.fold_in(key, 5)
    exponents = jax.random.randint(jax.random.fold_in(key, 1), (N_DP, 1), 2, 9)
    random_ints = jax.random.randint(jax.random.fold_in(key, 2), (N_DP, TOK_DEV), 0, 1 << 12)
    ordinal = jnp.arange(TOK_DEV, dtype=jnp.int32)[None, :]
    block_index = jnp.arange(N_DP, dtype=jnp.int32)[:, None]
    starts = random_ints % jnp.left_shift(1, exponents) == 0
    starts = starts | (ordinal == 0)
    starts = starts | (ordinal == TOK_DEV - 1) & (block_index == N_DP - 1)
    firsts = lax.cummax(jnp.where(starts, ordinal, 0), axis=1)
    planned_ids = firsts + block_index * TOK_DEV
    panels = planned_ids.reshape(PANELS, PANEL)
    return panels[layout].reshape(-1).astype(jnp.int32)


def block_levels(own_key, extent, cuts, smallest, top_value):
    level = 1.0
    for axis_at, parts in cuts:
        steps = jax.random.uniform(jax.random.fold_in(jax.random.fold_in(own_key, 6), axis_at), (parts,), jnp.float32, smallest / len(cuts), top_value / len(cuts))
        level = level * jnp.repeat(jnp.exp(steps), extent[axis_at] // parts).reshape((-1,) + (1,) * (len(extent) - 1 - axis_at))
    return level


def bell_draw(own_key, extent, deviation, most, split=(), kind=jnp.bfloat16):
    entries = deviation * jax.random.normal(own_key, extent, jnp.float32)
    if split:
        entries = entries * block_levels(own_key, extent, split, -0.22, 0.18)
    return jnp.clip(entries, -most, most).astype(kind)


def setup_inputs(seed: int = 0) -> dict:
    streams_of = jax.random.split(jax.random.key(seed), 10)
    return {
        "tokens": bell_draw(streams_of[0], (TOKENS, D), 1.0, 6.0, ((0, 16), (1, 8))),
        "norm_gain": jnp.clip(1.0 + 0.18 * jax.random.normal(streams_of[1], (D,), jnp.float32), 0.1, 1.9),
        "doc_ids": draw_doc_ids(jax.random.fold_in(streams_of[9], 71), 0),
        "panel_plan": draw_panel_plan(jax.random.fold_in(streams_of[9], 71), 0),
        "query_weight": bell_draw(streams_of[4], (D, HEADS * HD), D ** -0.5, 0.09375, ((1, 8),)),
        "key_weight": bell_draw(streams_of[5], (D, KV_HEADS * HD), D ** -0.5, 0.09375, ((1, 8),)),
        "value_weight": bell_draw(streams_of[6], (D, KV_HEADS * HD), D ** -0.5, 0.09375, ((1, 8),)),
        "out_weight": bell_draw(streams_of[7], (HEADS * HD, D), HD ** -0.5, 0.5, ((0, 8),)),
        "cotangent": bell_draw(streams_of[8], (TOKENS, D), 1.0, 6.0, ((0, 16), (1, 8))),
    }


NORM_EPSILON = 1e-05
ROPE_THETA = 500000.0
EXACT_PRECISION = lax.Precision.HIGHEST

def to_half(values):
    return lax.optimization_barrier(values.astype(jnp.bfloat16))

def rotate_half(values):
    half_width = values.shape[-1] // 2
    return jnp.concatenate([-values[..., half_width:], values[..., :half_width]], axis=-1)

def rotate(values, cosine, sine_table):
    return values * cosine + rotate_half(values) * sine_table

def rotate_back(values, cosine, sine_table):
    return values * cosine - rotate_half(values) * sine_table

def rotary_tables(positions):
    half_width = HD // 2
    frequency = ROPE_THETA ** (-2.0 * jnp.arange(half_width, dtype=jnp.float32) / HD)
    angles = positions.astype(jnp.float32)[:, None] * frequency[None, :]
    angles = jnp.concatenate([angles, angles], axis=1)
    return (jnp.cos(angles)[:, None, :], jnp.sin(angles)[:, None, :])

def attend(queries, key_rows, values, allowed):
    row_count = queries.shape[0]
    grouped = queries.astype(jnp.float32).reshape(row_count, KV_HEADS, -1, HD)
    scores = jnp.einsum('qkgd,skd->kgqs', grouped, key_rows.astype(jnp.float32), precision=EXACT_PRECISION) * HD ** (-0.5)
    weights = jnp.where(allowed, jnp.exp(scores), 0.0)
    shares = weights / lax.optimization_barrier(jnp.sum(weights, axis=-1, keepdims=True))
    rounded = to_half(shares).astype(jnp.float32)
    attended = jnp.einsum('kgqs,skd->qkgd', rounded, values.astype(jnp.float32), precision=EXACT_PRECISION)
    return (to_half(attended.reshape(row_count, -1)), shares, rounded)

def attend_back(grad_attended, queries, key_rows, values, shares, rounded, cosine, sine_table):
    row_count = queries.shape[0]
    grouped = queries.astype(jnp.float32).reshape(row_count, KV_HEADS, -1, HD)
    grouped_grad = grad_attended.astype(jnp.float32).reshape(row_count, KV_HEADS, -1, HD)
    key_heads = key_rows.astype(jnp.float32)
    value_heads = values.astype(jnp.float32)
    share_grad = jnp.einsum('qkgd,skd->kgqs', grouped_grad, value_heads, precision=EXACT_PRECISION)
    row_dot = lax.optimization_barrier(jnp.sum(share_grad * shares, axis=-1, keepdims=True))
    dscore = to_half(shares * (share_grad - row_dot) * HD ** (-0.5)).astype(jnp.float32)
    value_grad = jnp.einsum('kgqs,qkgd->skd', rounded, grouped_grad, precision=EXACT_PRECISION)
    query_grad = jnp.einsum('kgqs,skd->qkgd', dscore, key_heads, precision=EXACT_PRECISION).reshape(row_count, HEADS, HD)
    key_grad = jnp.einsum('kgqs,qkgd->skd', dscore, grouped, precision=EXACT_PRECISION)
    query_grad = to_half(rotate_back(query_grad, cosine, sine_table)).reshape(row_count, -1)
    key_grad = to_half(rotate_back(key_grad, cosine, sine_table)).reshape(row_count, -1)
    return (query_grad, key_grad, to_half(value_grad).reshape(row_count, -1))

def reference(tokens, norm_gain, doc_ids, panel_plan, query_weight, key_weight, value_weight, out_weight, cotangent):
    inverse_plan = jnp.zeros((PANELS,), jnp.int32).at[panel_plan].set(jnp.arange(PANELS, dtype=jnp.int32))

    def planned(array):
        shaped = array.reshape((PANELS, PANEL) + array.shape[1:])
        return shaped[inverse_plan].reshape((N_DP, TOK_DEV) + array.shape[1:])
    out_groups = out_weight.astype(jnp.float32).reshape(N_TENSOR, -1, D)
    query_groups = query_weight.astype(jnp.float32).reshape(D, N_TENSOR, -1)
    key_groups = key_weight.astype(jnp.float32).reshape(D, N_TENSOR, -1)
    value_groups = value_weight.astype(jnp.float32).reshape(D, N_TENSOR, -1)

    def block_pass(totals, inputs):
        block_tokens, block_cot, block_docs, first_row = inputs
        widened = block_tokens.astype(jnp.float32)
        inverse = lax.rsqrt(lax.optimization_barrier(jnp.mean(widened * widened, axis=1, keepdims=True)) + NORM_EPSILON)
        scaled = widened * inverse
        normed = to_half(scaled * norm_gain)
        ordinal = jnp.arange(TOK_DEV, dtype=jnp.int32)
        cosine, sine_table = rotary_tables(first_row + ordinal - block_docs)
        queries = jnp.dot(normed, query_weight, preferred_element_type=jnp.float32).reshape(TOK_DEV, HEADS, HD)
        queries = to_half(rotate(queries, cosine, sine_table))
        key_rows = jnp.dot(normed, key_weight, preferred_element_type=jnp.float32).reshape(TOK_DEV, KV_HEADS, HD)
        key_rows = to_half(rotate(key_rows, cosine, sine_table))
        values = to_half(jnp.dot(normed, value_weight, preferred_element_type=jnp.float32)).reshape(TOK_DEV, KV_HEADS, HD)
        allowed = (block_docs[:, None] == block_docs[None, :]) & (ordinal[None, :] <= ordinal[:, None])
        attended, shares, rounded = attend(queries, key_rows, values, allowed)
        head_terms = jnp.einsum('rnc,ncd->nrd', attended.astype(jnp.float32).reshape(TOK_DEV, N_TENSOR, -1), out_groups, precision=EXACT_PRECISION)
        output_rows = to_half(widened + lax.optimization_barrier(jnp.sum(to_half(head_terms).astype(jnp.float32), axis=0)))
        grad_attended = to_half(jnp.dot(block_cot, out_weight.T, preferred_element_type=jnp.float32))
        query_grad, key_grad, value_grad = attend_back(grad_attended, queries, key_rows, values, shares, rounded, cosine, sine_table)
        dn_terms = jnp.einsum('rnc,dnc->nrd', query_grad.astype(jnp.float32).reshape(TOK_DEV, N_TENSOR, -1), query_groups, precision=EXACT_PRECISION)
        dn_terms = dn_terms + jnp.einsum('rnc,dnc->nrd', key_grad.astype(jnp.float32).reshape(TOK_DEV, N_TENSOR, -1), key_groups, precision=EXACT_PRECISION)
        dn_terms = dn_terms + jnp.einsum('rnc,dnc->nrd', value_grad.astype(jnp.float32).reshape(TOK_DEV, N_TENSOR, -1), value_groups, precision=EXACT_PRECISION)
        dnormed = lax.optimization_barrier(jnp.sum(to_half(dn_terms).astype(jnp.float32), axis=0))
        dscaled = dnormed * norm_gain
        mean_term = lax.optimization_barrier(jnp.mean(dscaled * scaled, axis=1, keepdims=True))
        grad_rows = to_half(block_cot.astype(jnp.float32) + inverse * (dscaled - scaled * mean_term))
        totals = (totals[0] + to_half(jnp.dot(normed.T, query_grad, preferred_element_type=jnp.float32)).astype(jnp.float32), totals[1] + to_half(jnp.dot(normed.T, key_grad, preferred_element_type=jnp.float32)).astype(jnp.float32), totals[2] + to_half(jnp.dot(normed.T, value_grad, preferred_element_type=jnp.float32)).astype(jnp.float32))
        return (totals, (output_rows, grad_rows))
    initial = (jnp.zeros((D, HEADS * HD), jnp.float32), jnp.zeros((D, KV_HEADS * HD), jnp.float32), jnp.zeros((D, KV_HEADS * HD), jnp.float32))
    firsts = jnp.arange(N_DP, dtype=jnp.int32) * TOK_DEV
    totals, (outputs, grads) = lax.scan(block_pass, initial, (planned(tokens), planned(cotangent), planned(doc_ids), firsts))

    def unplan(blocks):
        return blocks.reshape(PANELS, PANEL, D)[panel_plan].reshape(TOKENS, D)
    scale = TOKENS ** (-0.5)
    return (unplan(outputs), unplan(grads), (totals[0] * scale).astype(jnp.bfloat16), (totals[1] * scale).astype(jnp.bfloat16), (totals[2] * scale).astype(jnp.bfloat16))
```

```python
import functools

import jax
import jax.numpy as jnp
from jax import lax
from jax.experimental import pallas as pl
from jax.experimental.pallas import tpu as pltpu
from jax.sharding import Mesh
from jax.sharding import PartitionSpec as P

HD = 128
NORM_EPSILON = 1e-05
ROPE_THETA = 500000.0
SCORE_SCALE = HD ** (-0.5)
STEPS = (0, -1, 1, 2)
BF = jnp.bfloat16
F32 = jnp.float32
VMEM_LIMIT = 48 * 1024 * 1024


def params():
    return pltpu.CompilerParams(vmem_limit_bytes=VMEM_LIMIT)


def cost(flops, moved):
    return pl.CostEstimate(flops=int(flops), bytes_accessed=int(moved), transcendentals=0)


def nn(a, b):
    return lax.dot_general(a, b, (((1,), (0,)), ((), ())), preferred_element_type=F32)


def nt(a, b):
    return lax.dot_general(a, b, (((1,), (1,)), ((), ())), preferred_element_type=F32)


def place_kernel(plan_ref, rows_ref, out_ref):
    count = rows_ref.shape[0]
    for panel in range(count):
        out_ref[plan_ref[panel] // count] = rows_ref[panel]


def place(plan, panels):
    return pl.pallas_call(
        place_kernel,
        out_shape=jax.ShapeDtypeStruct(panels.shape, panels.dtype),
        in_specs=[
            pl.BlockSpec(memory_space=pltpu.SMEM),
            pl.BlockSpec(memory_space=pltpu.VMEM),
        ],
        out_specs=pl.BlockSpec(memory_space=pltpu.VMEM),
        compiler_params=params(),
        cost_estimate=cost(0, 2 * panels.size * 2),
        name="place",
    )(plan, panels)


def place_meta_kernel(plan_ref, rows_ref, docs_ref, out_ref):
    count, rows, width = rows_ref.shape
    for panel in range(count):
        target = plan_ref[panel] // count
        slot = plan_ref[panel] % count
        out_ref[target, :, :width] = rows_ref[panel]
        doc = docs_ref[panel]
        high = (doc // 128).astype(F32)
        low = (doc % 128).astype(F32)
        lane = lax.broadcasted_iota(jnp.int32, (rows, 128), 1)
        extra = jnp.where(lane == 0, high, 0.0)
        extra = jnp.where(lane == 1, low, extra)
        extra = jnp.where(lane == 2, slot.astype(F32), extra)
        out_ref[target, :, width:] = extra.astype(BF)


def place_meta(plan, panels, docs):
    count, rows, width = panels.shape
    return pl.pallas_call(
        place_meta_kernel,
        out_shape=jax.ShapeDtypeStruct((count, rows, width + 128), panels.dtype),
        in_specs=[
            pl.BlockSpec(memory_space=pltpu.SMEM),
            pl.BlockSpec(memory_space=pltpu.VMEM),
            pl.BlockSpec(memory_space=pltpu.VMEM),
        ],
        out_specs=pl.BlockSpec(memory_space=pltpu.VMEM),
        compiler_params=params(),
        cost_estimate=cost(0, 2 * panels.size * 2),
        name="place_meta",
    )(plan, panels, docs.reshape(count, rows, 1))


def project_kernel(
    idx_ref, mine_ref, other_ref, gain_ref, wq_ref, wk_ref, wv_ref,
    turned_ref, raw_ref, inverse_ref, acc_ref, squares_ref,
):
    step = pl.program_id(0)
    last = pl.num_programs(0) - 1
    width = mine_ref.shape[2]

    @pl.when(step == 0)
    def _():
        acc_ref[...] = jnp.zeros_like(acc_ref)
        squares_ref[...] = jnp.zeros_like(squares_ref)

    def work(piece):
        wide = piece.astype(F32)
        squares_ref[...] += jnp.sum(wide * wide, axis=1, keepdims=True)
        gained = (wide * gain_ref[0]).astype(BF)
        turned_ref[0] = gained.T
        q_cols = wq_ref.shape[1]
        kv_cols = wk_ref.shape[1]
        acc_ref[:, :q_cols] += nn(gained, wq_ref[...])
        acc_ref[:, q_cols : q_cols + kv_cols] += nn(gained, wk_ref[...])
        acc_ref[:, q_cols + kv_cols :] += nn(gained, wv_ref[...])

    half = pl.num_programs(0) // 2

    @pl.when(step < half)
    def _():
        work(mine_ref[0])

    @pl.when(step >= half)
    def _():
        work(other_ref[0])

    @pl.when(step == last)
    def _():
        features = width * (last + 1)
        inverse = lax.rsqrt(squares_ref[...] / features + NORM_EPSILON)
        inverse_ref[...] = inverse
        raw_ref[...] = acc_ref[...] * inverse


def project(idx, mine, other, gain, wq, wk, wv):
    parts, rows, width = mine.shape
    pieces = 2 * parts
    cols = wq.shape[1] + wk.shape[1] + wv.shape[1]
    grid_spec = pltpu.PrefetchScalarGridSpec(
        num_scalar_prefetch=1,
        grid=(pieces,),
        in_specs=[
            pl.BlockSpec((1, rows, width), lambda j, idx: (jnp.minimum(j, parts - 1), 0, 0)),
            pl.BlockSpec((1, rows, width), lambda j, idx: (jnp.maximum(j - parts, 0), 0, 0)),
            pl.BlockSpec((1, 1, width), lambda j, idx: (idx[j], 0, 0)),
            pl.BlockSpec((width, wq.shape[1]), lambda j, idx: (idx[j], 0)),
            pl.BlockSpec((width, wk.shape[1]), lambda j, idx: (idx[j], 0)),
            pl.BlockSpec((width, wv.shape[1]), lambda j, idx: (idx[j], 0)),
        ],
        out_specs=[
            pl.BlockSpec((1, width, rows), lambda j, idx: (j, 0, 0)),
            pl.BlockSpec((rows, cols), lambda j, idx: (0, 0)),
            pl.BlockSpec((rows, 1), lambda j, idx: (0, 0)),
        ],
        scratch_shapes=[pltpu.VMEM((rows, cols), F32), pltpu.VMEM((rows, 1), F32)],
    )
    return pl.pallas_call(
        project_kernel,
        grid_spec=grid_spec,
        out_shape=[
            jax.ShapeDtypeStruct((pieces, width, rows), BF),
            jax.ShapeDtypeStruct((rows, cols), F32),
            jax.ShapeDtypeStruct((rows, 1), F32),
        ],
        compiler_params=params(),
        cost_estimate=cost(2 * rows * width * pieces * cols, 2 * pieces * width * (2 * rows + cols)),
        name="project",
    )(idx, mine, other, gain.reshape(pieces, 1, width), wq, wk, wv)


def attend_kernel(
    q_raw_ref, k_raw_ref, v_raw_ref, cosine_ref, sine_ref, where_col_ref, where_row_ref,
    q_ref, k_ref, k_turned_ref, v_ref, shares_ref, attended_ref, v_turned_ref,
):
    cosine = cosine_ref[...]
    sine = sine_ref[...]

    def rotate(u):
        return u * cosine + pltpu.roll(u, HD // 2, 1) * sine

    @pl.when(pl.program_id(0) == 0)
    def _():
        key = rotate(k_raw_ref[...])
        k_ref[...] = key.astype(BF)
        k_turned_ref[...] = key.T.astype(BF)
        v_ref[...] = v_raw_ref[...].astype(BF)
        v_turned_ref[...] = v_raw_ref[...].T.astype(BF)

    query = rotate(q_raw_ref[...]).astype(BF)
    q_ref[...] = query
    scores = nt(k_ref[...], query) * SCORE_SCALE
    doc_s = where_col_ref[:, 0:1]
    at_s = where_col_ref[:, 1:2]
    doc_g = where_row_ref[0:1, :]
    at_g = where_row_ref[1:2, :]
    allowed = (doc_s == doc_g) & (at_s <= at_g)
    weights = jnp.where(allowed, jnp.exp(scores), 0.0)
    total = jnp.sum(weights, axis=0, keepdims=True)
    shares = (weights * (1.0 / total)).astype(BF)
    shares_ref[0] = shares
    attended_ref[...] = nn(v_turned_ref[...], shares).T.astype(BF)


def attend(raw, cosine, sine, where_col, where_row):
    rows = raw.shape[0]
    heads = raw.shape[1] // HD - 2
    whole = lambda shape: pl.BlockSpec(shape, lambda h: (0,) * len(shape))
    head = pl.BlockSpec((rows, HD), lambda h: (0, h))
    return pl.pallas_call(
        attend_kernel,
        grid=(heads,),
        in_specs=[
            head,
            pl.BlockSpec((rows, HD), lambda h: (0, heads)),
            pl.BlockSpec((rows, HD), lambda h: (0, heads + 1)),
            whole((rows, HD)),
            whole((rows, HD)),
            whole(where_col.shape),
            whole(where_row.shape),
        ],
        out_specs=[
            head,
            whole((rows, HD)),
            whole((HD, rows)),
            whole((rows, HD)),
            pl.BlockSpec((1, rows, rows), lambda h: (h, 0, 0)),
            head,
        ],
        out_shape=[
            jax.ShapeDtypeStruct((rows, heads * HD), BF),
            jax.ShapeDtypeStruct((rows, HD), BF),
            jax.ShapeDtypeStruct((HD, rows), BF),
            jax.ShapeDtypeStruct((rows, HD), BF),
            jax.ShapeDtypeStruct((heads, rows, rows), BF),
            jax.ShapeDtypeStruct((rows, heads * HD), BF),
        ],
        scratch_shapes=[pltpu.VMEM((HD, rows), BF)],
        compiler_params=params(),
        cost_estimate=cost(4 * heads * rows * rows * HD, 2 * heads * rows * rows),
        name="attend",
    )(raw, raw, raw, cosine, sine, where_col, where_row)


def back_kernel(
    idx_ref, mine_ref, other_ref, wo_ref, q_ref, k_ref, k_turned_ref, v_ref, shares_ref,
    raw_ref, inverse_ref, cosine_ref, sine_ref,
    grad_ref, scaled_ref, dots_ref, acc_ref, *, scale,
):
    step = pl.program_id(0)
    last = pl.num_programs(0) - 1
    half = pl.num_programs(0) // 2

    @pl.when(step == 0)
    def _():
        acc_ref[...] = jnp.zeros_like(acc_ref)

    @pl.when(step < half)
    def _():
        acc_ref[...] += nt(mine_ref[0], wo_ref[...])

    @pl.when(step >= half)
    def _():
        acc_ref[...] += nt(other_ref[0], wo_ref[...])

    @pl.when(step == last)
    def _():
        cosine = cosine_ref[...]
        sine = sine_ref[...]
        heads = shares_ref.shape[0]
        rows = q_ref.shape[0]
        factor = inverse_ref[...] * scale
        ones = jnp.ones((8, HD), F32)
        dots_ref[...] = jnp.zeros_like(dots_ref)

        def rotate_back(u):
            return u * cosine - pltpu.roll(u, HD // 2, 1) * sine

        def emit(at, grad):
            cols = slice(at * HD, (at + 1) * HD)
            rounded = grad.astype(BF)
            grad_ref[:, cols] = rounded
            scaled_ref[:, cols] = (grad * factor).astype(BF)
            product = rounded.astype(F32) * raw_ref[:, cols]
            dots_ref[...] += lax.dot_general(
                ones, product, (((1,), (1,)), ((), ())),
                preferred_element_type=F32, precision=lax.Precision.HIGHEST,
            )

        key_grad = jnp.zeros((rows, HD), F32)
        value_grad = jnp.zeros((rows, HD), F32)
        for h in range(heads):
            cols = slice(h * HD, (h + 1) * HD)
            grad_attended = acc_ref[:, cols].astype(BF)
            shares = shares_ref[h]
            share_grad = nt(v_ref[...], grad_attended)
            wide = shares.astype(F32)
            row_dot = jnp.sum(share_grad * wide, axis=0, keepdims=True)
            dscore = (wide * (share_grad - row_dot) * SCORE_SCALE).astype(BF)
            key_grad += nn(dscore, q_ref[:, cols])
            value_grad += nn(shares, grad_attended)
            emit(h, rotate_back(nn(k_turned_ref[...], dscore).T))
        emit(heads, rotate_back(key_grad))
        emit(heads + 1, value_grad)


def back(idx, mine, other, wo, q, k, k_turned, v, shares, raw, inverse, cosine, sine, scale):
    parts, rows, width = mine.shape
    cols = wo.shape[0]
    whole = lambda array: pl.BlockSpec(array.shape, lambda j, idx: (0,) * array.ndim)
    grid_spec = pltpu.PrefetchScalarGridSpec(
        num_scalar_prefetch=1,
        grid=(2 * parts,),
        in_specs=[
            pl.BlockSpec((1, rows, width), lambda j, idx: (jnp.minimum(j, parts - 1), 0, 0)),
            pl.BlockSpec((1, rows, width), lambda j, idx: (jnp.maximum(j - parts, 0), 0, 0)),
            pl.BlockSpec((cols, width), lambda j, idx: (0, idx[j])),
        ]
        + [whole(a) for a in (q, k, k_turned, v, shares, raw, inverse, cosine, sine)],
        out_specs=[
            pl.BlockSpec(raw.shape, lambda j, idx: (0, 0)),
            pl.BlockSpec(raw.shape, lambda j, idx: (0, 0)),
            pl.BlockSpec((8, rows), lambda j, idx: (0, 0)),
        ],
        scratch_shapes=[pltpu.VMEM((rows, cols), F32)],
    )
    return pl.pallas_call(
        functools.partial(back_kernel, scale=scale),
        grid_spec=grid_spec,
        out_shape=[
            jax.ShapeDtypeStruct(raw.shape, BF),
            jax.ShapeDtypeStruct(raw.shape, BF),
            jax.ShapeDtypeStruct((8, rows), F32),
        ],
        compiler_params=params(),
        cost_estimate=cost(
            4 * parts * rows * width * cols + 8 * cols * rows * rows, 4 * parts * width * (rows + cols)
        ),
        name="back",
    )(idx, mine, other, wo, q, k, k_turned, v, shares, raw, inverse, cosine, sine)


def weight_grad_kernel(idx_ref, turned_ref, scaled_ref, q_ref, k_ref, v_ref):
    turned = turned_ref[0]
    q_cols = q_ref.shape[1]
    kv_cols = k_ref.shape[1]
    q_ref[...] = nn(turned, scaled_ref[:, :q_cols]).astype(BF)
    both = nn(turned, scaled_ref[:, q_cols:]).astype(BF)
    k_ref[...] = both[:, :kv_cols]
    v_ref[...] = both[:, kv_cols:]


def weight_grad(idx, turned, scaled, q_cols, kv_cols):
    pieces, width, rows = turned.shape
    widths = (q_cols, kv_cols, kv_cols)
    grid_spec = pltpu.PrefetchScalarGridSpec(
        num_scalar_prefetch=1,
        grid=(pieces,),
        in_specs=[
            pl.BlockSpec((1, width, rows), lambda j, idx: (j, 0, 0)),
            pl.BlockSpec(scaled.shape, lambda j, idx: (0, 0)),
        ],
        out_specs=[pl.BlockSpec((width, w), lambda j, idx: (idx[j], 0)) for w in widths],
    )
    return pl.pallas_call(
        weight_grad_kernel,
        grid_spec=grid_spec,
        out_shape=[jax.ShapeDtypeStruct((pieces * width, w), BF) for w in widths],
        compiler_params=params(),
        cost_estimate=cost(
            2 * pieces * width * rows * sum(widths), 2 * pieces * width * (rows + sum(widths))
        ),
        name="weight_grad",
    )(idx, turned, scaled)


def out_term_kernel(idx_ref, attended_ref, wo_ref, out_ref):
    out_ref[0] = nn(attended_ref[...], wo_ref[...]).astype(BF)


def out_terms(idx, attended, wo, width):
    rows, cols = attended.shape
    parts = idx.shape[0]
    grid_spec = pltpu.PrefetchScalarGridSpec(
        num_scalar_prefetch=1,
        grid=(parts,),
        in_specs=[
            pl.BlockSpec((rows, cols), lambda j, idx: (0, 0)),
            pl.BlockSpec((cols, width), lambda j, idx: (0, idx[j])),
        ],
        out_specs=pl.BlockSpec((1, rows, width), lambda j, idx: (j, 0, 0)),
    )
    return pl.pallas_call(
        out_term_kernel,
        grid_spec=grid_spec,
        out_shape=jax.ShapeDtypeStruct((parts, rows, width), BF),
        compiler_params=params(),
        cost_estimate=cost(2 * parts * rows * cols * width, 2 * parts * width * (rows + cols)),
        name="out_terms",
    )(idx, attended, wo)


def input_term_kernel(idx_ref, grad_ref, dots_ref, wq_ref, wk_ref, wv_ref, out_ref):
    q_cols = wq_ref.shape[1]
    kv_cols = wk_ref.shape[1]
    rows = grad_ref.shape[0]
    term = nt(grad_ref[:, :q_cols], wq_ref[...])
    term += nt(grad_ref[:, q_cols : q_cols + kv_cols], wk_ref[...])
    term += nt(grad_ref[:, q_cols + kv_cols :], wv_ref[...])
    out_ref[0, :rows] = term.astype(BF)
    dots = dots_ref[0:1, :]
    high = dots.astype(BF).astype(F32)
    line = lax.broadcasted_iota(jnp.int32, (16, dots.shape[1]), 0)
    extra = jnp.where(line == 0, high, jnp.where(line == 1, dots - high, 0.0))
    out_ref[0, rows:] = extra.astype(BF)


def input_terms(idx, grad, dots, wq, wk, wv, width):
    rows, cols = grad.shape
    parts = idx.shape[0]
    grid_spec = pltpu.PrefetchScalarGridSpec(
        num_scalar_prefetch=1,
        grid=(parts,),
        in_specs=[
            pl.BlockSpec((rows, cols), lambda j, idx: (0, 0)),
            pl.BlockSpec(dots.shape, lambda j, idx: (0, 0)),
        ]
        + [pl.BlockSpec((width, w.shape[1]), lambda j, idx: (idx[j], 0)) for w in (wq, wk, wv)],
        out_specs=pl.BlockSpec((1, rows + 16, width), lambda j, idx: (j, 0, 0)),
    )
    return pl.pallas_call(
        input_term_kernel,
        grid_spec=grid_spec,
        out_shape=jax.ShapeDtypeStruct((parts, rows + 16, width), BF),
        compiler_params=params(),
        cost_estimate=cost(2 * parts * rows * cols * width, 2 * parts * width * (rows + cols)),
        name="input_terms",
    )(idx, grad, dots, wq, wk, wv)


def shift(array, step):
    size = lax.axis_size("y")
    return lax.ppermute(array, "y", [(i, (i + step) % size) for i in range(size)])


def swap(array):
    return lax.ppermute(array, "core", [(0, 1), (1, 0)])


def gather_pieces(piece):
    half = piece.shape[0] // 2
    below = shift(piece, 1)
    above = shift(piece, -1)
    far_top = shift(below[:half], 1)
    far_end = shift(above[half:], -1)
    mine = jnp.stack([piece, below, above, jnp.concatenate([far_top, far_end], axis=0)])
    return mine, swap(mine)


def sum_pieces(other_terms, mine_terms):
    wide = lambda a: a.astype(F32)
    sums = (wide(mine_terms) + wide(swap(other_terms))).astype(BF)
    rows = sums.shape[1]
    half = rows // 32 * 16
    relay_top = shift(sums[3, :half], 1)
    relay_end = shift(sums[3, half:], -1)
    up = jnp.concatenate([(wide(sums[2, :half]) + wide(relay_top)).astype(BF), sums[2, half:]], axis=0)
    down = jnp.concatenate([sums[1, :half], (wide(sums[1, half:]) + wide(relay_end)).astype(BF)], axis=0)
    return wide(sums[0]) + wide(shift(up, 1)) + wide(shift(down, -1))


def exchange(panels):
    return lax.all_to_all(panels, ("x", "z"), split_axis=0, concat_axis=0, tiled=True)


def per_device(
    tokens, norm_gain, doc_ids, panel_plan, wq, wk, wv, wo, cotangent,
):
    y, core = lax.axis_index("y"), lax.axis_index("core")
    ys, cores = lax.axis_size("y"), lax.axis_size("core")
    block = lax.axis_index("x") * lax.axis_size("z") + lax.axis_index("z")
    dp = lax.axis_size("x") * lax.axis_size("z")
    count = panel_plan.shape[0]
    rows, width = tokens.shape
    panel = rows // count
    features = norm_gain.shape[0]

    around = (y + jnp.array(STEPS, jnp.int32)) % ys
    idx_mine = around * cores + core
    idx_other = around * cores + (1 - core)
    idx = jnp.concatenate([idx_mine, idx_other])

    here_tokens = exchange(place(panel_plan, tokens.reshape(count, panel, width))).reshape(rows, width)
    arrived = exchange(
        place_meta(panel_plan, cotangent.reshape(count, panel, width), doc_ids.reshape(count, panel))
    )
    here_cot = arrived[:, :, :width].reshape(rows, width)
    meta = arrived[:, :, width : width + 3].reshape(rows, 3).astype(jnp.int32)
    docs = meta[:, 0] * 128 + meta[:, 1]
    at = block * rows + meta[:, 2] * panel + jnp.arange(rows, dtype=jnp.int32) % panel
    positions = (at - docs).astype(F32)
    frequency = ROPE_THETA ** (-2.0 * jnp.arange(HD // 2, dtype=F32) / HD)
    angles = positions[:, None] * frequency[None, :]
    cosine, sine = jnp.cos(angles), jnp.sin(angles)
    cosine = jnp.concatenate([cosine, cosine], axis=1)
    sine = jnp.concatenate([-sine, sine], axis=1)
    where_row = jnp.stack([docs, at])
    where_col = where_row.T

    tok_mine, tok_other = gather_pieces(here_tokens)
    cot_mine, cot_other = gather_pieces(here_cot)
    turned, raw, inverse = project(idx, tok_mine, tok_other, norm_gain, wq, wk, wv)
    q, k, k_turned, v, shares, attended = attend(raw, cosine, sine, where_col, where_row)

    out_sum = sum_pieces(
        out_terms(idx_other, attended, wo, width), out_terms(idx_mine, attended, wo, width)
    )
    output_rows = (here_tokens.astype(F32) + out_sum).astype(BF)

    scale = (rows * dp) ** (-0.5)
    grad, scaled, dots = back(
        idx, cot_mine, cot_other, wo, q, k, k_turned, v, shares, raw, inverse, cosine, sine, scale
    )
    grads = weight_grad(idx, turned, scaled, wq.shape[1], wk.shape[1])
    grad_query, grad_key, grad_value = lax.psum(tuple(grads), ("x", "z"))

    in_sum = sum_pieces(
        input_terms(idx_other, grad, dots, wq, wk, wv, width),
        input_terms(idx_mine, grad, dots, wq, wk, wv, width),
    )
    mean_term = ((in_sum[rows] + in_sum[rows + 1]) / features)[:, None]
    own = y * cores + core
    own_gain = lax.dynamic_slice_in_dim(norm_gain, own * width, width, 0)
    own_scaled = here_tokens.astype(F32) * inverse
    grad_rows = here_cot.astype(F32) + inverse * (in_sum[:rows] * own_gain - own_scaled * mean_term)
    grad_rows = grad_rows.astype(BF)

    targets = panel_plan // count
    output = exchange(output_rows.reshape(dp, panel, width))[targets].reshape(rows, width)
    grad_tokens = exchange(grad_rows.reshape(dp, panel, width))[targets].reshape(rows, width)
    return output, grad_tokens, grad_query, grad_key, grad_value


def solution(mesh):
    axes = ("x", "z", "y", "core")
    split = Mesh(mesh.devices.reshape(4, 4, 4, 2), axes)
    dp, tensor = ("x", "z"), ("y", "core")
    in_specs = (
        P(dp, tensor),
        P(),
        P(dp),
        P(dp),
        P(None, tensor),
        P(None, tensor),
        P(None, tensor),
        P(tensor, None),
        P(dp, tensor),
    )
    out_specs = (
        P(dp, tensor),
        P(dp, tensor),
        P(None, tensor),
        P(None, tensor),
        P(None, tensor),
    )
    return jax.shard_map(
        per_device, mesh=split, in_specs=in_specs, out_specs=out_specs, check_vma=False
    )
```

```python
import functools

import jax
import jax.numpy as jnp
from jax import lax
from jax.experimental import pallas as pl
from jax.experimental.pallas import tpu as pltpu
from jax.sharding import Mesh
from jax.sharding import PartitionSpec as P

HD = 128
NORM_EPSILON = 1e-05
ROPE_THETA = 500000.0
SCORE_SCALE = HD ** (-0.5)
STEPS = (0, -1, 1, 2)
BF = jnp.bfloat16
F32 = jnp.float32
VMEM_LIMIT = 56 * 1024 * 1024


def params():
    return pltpu.CompilerParams(vmem_limit_bytes=VMEM_LIMIT)


def cost(flops, moved):
    return pl.CostEstimate(flops=int(flops), bytes_accessed=int(moved), transcendentals=0)


def nn(a, b):
    return lax.dot_general(a, b, (((1,), (0,)), ((), ())), preferred_element_type=F32)


def nt(a, b):
    return lax.dot_general(a, b, (((1,), (1,)), ((), ())), preferred_element_type=F32)


def place_kernel(plan_ref, rows_ref, out_ref):
    count = rows_ref.shape[0]
    for panel in range(count):
        out_ref[plan_ref[panel] // count] = rows_ref[panel]


def place(plan, panels):
    return pl.pallas_call(
        place_kernel,
        out_shape=jax.ShapeDtypeStruct(panels.shape, panels.dtype),
        in_specs=[
            pl.BlockSpec(memory_space=pltpu.SMEM),
            pl.BlockSpec(memory_space=pltpu.VMEM),
        ],
        out_specs=pl.BlockSpec(memory_space=pltpu.VMEM),
        compiler_params=params(),
        cost_estimate=cost(0, 2 * panels.size * 2),
        name="place",
    )(plan, panels)


def place_meta_kernel(plan_ref, rows_ref, docs_ref, out_ref):
    count, rows, width = rows_ref.shape
    for panel in range(count):
        target = plan_ref[panel] // count
        slot = plan_ref[panel] % count
        out_ref[target, :, :width] = rows_ref[panel]
        doc = docs_ref[panel]
        high = (doc // 128).astype(F32)
        low = (doc % 128).astype(F32)
        lane = lax.broadcasted_iota(jnp.int32, (rows, 128), 1)
        extra = jnp.where(lane == 0, high, 0.0)
        extra = jnp.where(lane == 1, low, extra)
        extra = jnp.where(lane == 2, slot.astype(F32), extra)
        out_ref[target, :, width:] = extra.astype(BF)


def place_meta(plan, panels, docs):
    count, rows, width = panels.shape
    return pl.pallas_call(
        place_meta_kernel,
        out_shape=jax.ShapeDtypeStruct((count, rows, width + 128), panels.dtype),
        in_specs=[
            pl.BlockSpec(memory_space=pltpu.SMEM),
            pl.BlockSpec(memory_space=pltpu.VMEM),
            pl.BlockSpec(memory_space=pltpu.VMEM),
        ],
        out_specs=pl.BlockSpec(memory_space=pltpu.VMEM),
        compiler_params=params(),
        cost_estimate=cost(0, 2 * panels.size * 2),
        name="place_meta",
    )(plan, panels, docs.reshape(count, rows, 1))


NEAR = tuple((step, other) for step in range(3) for other in (0, 1))
FAR = ((3, 0), (3, 1))

SMEM_SPEC = pl.BlockSpec(memory_space=pltpu.SMEM)
HBM_SPEC = pl.BlockSpec(memory_space=pltpu.HBM)


def whole(shape):
    return pl.BlockSpec(tuple(shape), lambda j: (0,) * len(shape))


def part_of(idx_ref, step, other, width):
    at = idx_ref[step] + (idx_ref[4] if not other else 1 - idx_ref[4])
    return pl.ds(pl.multiple_of(at * width, width), width)


class Copies:
    def __init__(self, sems):
        self.sems = sems
        self.count = 0

    def start(self, source, target):
        copy = pltpu.make_async_copy(source, target, self.sems.at[self.count])
        self.count += 1
        copy.start()
        return copy


def fetch_near(copies, pieces, buffer):
    return [[copies.start(pieces[3 * o + s], buffer.at[n])] for n, (s, o) in enumerate(NEAR)]


def fetch_far(copies, pieces, buffer):
    half = buffer.shape[1] // 2
    return [
        [
            copies.start(pieces[2 * n], buffer.at[n, :half]),
            copies.start(pieces[2 * n + 1], buffer.at[n, half:]),
        ]
        for n in range(2)
    ]


def project_steps(
    idx_ref, places, arrivals, copies, buffer, gain_ref, weights, held, turned_ref, raw_ref, fresh
):
    rows, width = buffer.shape[1:]
    for n, (step, other) in enumerate(places):
        part = part_of(idx_ref, step, other, width)
        for ref, target in zip(weights, held):
            arrivals[n].append(copies.start(ref.at[part], target.at[n]))
    squares = jnp.zeros((rows, 1), F32)
    for n, (step, other) in enumerate(places):
        core = idx_ref[4] if not other else 1 - idx_ref[4]
        for copy in arrivals[n]:
            copy.wait()
        wide = buffer[n].astype(F32)
        squares += jnp.sum(wide * wide, axis=1, keepdims=True)
        gained = (wide * gain_ref[pl.ds(idx_ref[step] + core, 1)]).astype(BF)
        turned_ref[step % 3, pl.ds(pl.multiple_of(core * width, width), width)] = gained.T
        at = 0
        for target in held:
            cols = slice(at, at + target.shape[2])
            at += target.shape[2]
            if fresh and n == 0:
                raw_ref[:, cols] = nn(gained, target[n])
            else:
                raw_ref[:, cols] += nn(gained, target[n])
    return squares


def project_near_kernel(*refs):
    idx_ref, pieces = refs[0], refs[1:7]
    gain_ref, wq, wk, wv, turned_ref, raw_ref, squares_ref, buffer, hq, hk, hv, sems = refs[7:]
    copies = Copies(sems)
    arrivals = fetch_near(copies, pieces, buffer)
    squares = project_steps(
        idx_ref, NEAR, arrivals, copies, buffer, gain_ref, (wq, wk, wv), (hq, hk, hv),
        turned_ref, raw_ref, True,
    )
    squares_ref[...] = jnp.broadcast_to(squares, squares_ref.shape)


def project_near(idx, pieces, gain, wq, wk, wv):
    rows, width = pieces[0].shape
    weights = (wq, wk, wv)
    cols = sum(w.shape[1] for w in weights)
    shapes = [
        jax.ShapeDtypeStruct((3, 2 * width, rows), BF),
        jax.ShapeDtypeStruct((rows, cols), F32),
        jax.ShapeDtypeStruct((rows, HD), F32),
    ]
    return pl.pallas_call(
        project_near_kernel,
        grid=(1,),
        in_specs=[SMEM_SPEC] + [HBM_SPEC] * 6 + [whole(gain.shape)] + [HBM_SPEC] * 3,
        out_specs=[whole(a.shape) for a in shapes],
        out_shape=shapes,
        scratch_shapes=[pltpu.VMEM((6, rows, width), BF)]
        + [pltpu.VMEM((6, width, w.shape[1]), BF) for w in weights]
        + [pltpu.SemaphoreType.DMA((24,))],
        compiler_params=params(),
        cost_estimate=cost(12 * rows * width * cols, 12 * width * (2 * rows + cols)),
        name="project_near",
    )(idx, *pieces, gain, *weights)


def attend_kernel(*refs):
    idx_ref, pieces = refs[0], refs[1:5]
    (
        gain_ref, wq, wk, wv, near_raw_ref, near_squares_ref,
        cosine_ref, sine_ref, where_col_ref, where_row_ref,
        turned_ref, raw_ref, inverse_ref, q_ref, k_ref, k_turned_ref, v_ref, shares_ref, attended_ref,
        buffer, hq, hk, hv, sems,
    ) = refs[5:]
    rows, width = buffer.shape[1:]
    copies = Copies(sems)
    arrivals = fetch_far(copies, pieces, buffer)
    raw_ref[...] = near_raw_ref[...]
    squares = project_steps(
        idx_ref, FAR, arrivals, copies, buffer, gain_ref, (wq, wk, wv), (hq, hk, hv),
        turned_ref, raw_ref, False,
    )
    features = wq.shape[0]
    inverse = lax.rsqrt((squares + near_squares_ref[:, 0:1]) / features + NORM_EPSILON)
    inverse_ref[...] = jnp.broadcast_to(inverse, inverse_ref.shape)
    raw_ref[...] = raw_ref[...] * inverse

    cosine = cosine_ref[...]
    sine = sine_ref[...]
    heads = shares_ref.shape[0]

    def rotate(u):
        return u * cosine + pltpu.roll(u, HD // 2, 1) * sine

    key = rotate(raw_ref[:, heads * HD : (heads + 1) * HD])
    k_ref[...] = key.astype(BF)
    k_turned_ref[...] = key.T.astype(BF)
    value = raw_ref[:, (heads + 1) * HD :]
    v_ref[...] = value.astype(BF)
    v_turned = value.T.astype(BF)
    doc_s = where_col_ref[:, 0:1]
    at_s = where_col_ref[:, 1:2]
    doc_g = where_row_ref[0:1, :]
    at_g = where_row_ref[1:2, :]
    allowed = (doc_s == doc_g) & (at_s <= at_g)
    for h in range(heads):
        cols = slice(h * HD, (h + 1) * HD)
        query = rotate(raw_ref[:, cols]).astype(BF)
        q_ref[:, cols] = query
        scores = nt(k_ref[...], query) * SCORE_SCALE
        weights = jnp.where(allowed, jnp.exp(scores), 0.0)
        total = jnp.sum(weights, axis=0, keepdims=True)
        shares = (weights * (1.0 / total)).astype(BF)
        shares_ref[h] = shares
        attended_ref[:, cols] = nn(v_turned, shares).T.astype(BF)


def attend(idx, pieces, gain, wq, wk, wv, near_raw, near_squares, cosine, sine, where_col, where_row):
    width = pieces[0].shape[1]
    rows, cols = near_raw.shape
    weights = (wq, wk, wv)
    heads = wq.shape[1] // HD
    shapes = [
        jax.ShapeDtypeStruct((1, 2 * width, rows), BF),
        jax.ShapeDtypeStruct((rows, cols), F32),
        jax.ShapeDtypeStruct((rows, HD), F32),
        jax.ShapeDtypeStruct((rows, heads * HD), BF),
        jax.ShapeDtypeStruct((rows, HD), BF),
        jax.ShapeDtypeStruct((HD, rows), BF),
        jax.ShapeDtypeStruct((rows, HD), BF),
        jax.ShapeDtypeStruct((heads, rows, rows), BF),
        jax.ShapeDtypeStruct((rows, heads * HD), BF),
    ]
    extras = (near_raw, near_squares, cosine, sine, where_col, where_row)
    return pl.pallas_call(
        attend_kernel,
        grid=(1,),
        in_specs=[SMEM_SPEC] + [HBM_SPEC] * 4 + [whole(gain.shape)] + [HBM_SPEC] * 3
        + [whole(a.shape) for a in extras],
        out_specs=[whole(a.shape) for a in shapes],
        out_shape=shapes,
        scratch_shapes=[pltpu.VMEM((2, rows, width), BF)]
        + [pltpu.VMEM((2, width, w.shape[1]), BF) for w in weights]
        + [pltpu.SemaphoreType.DMA((10,))],
        compiler_params=params(),
        cost_estimate=cost(
            4 * rows * width * cols + 4 * heads * rows * rows * HD, 4 * width * (2 * rows + cols)
        ),
        name="attend",
    )(idx, *pieces, gain, *weights, *extras)


def back_near_kernel(*refs):
    idx_ref, pieces = refs[0], refs[1:7]
    wo_ref, acc_ref, buffer, held, sems = refs[7:]
    width = buffer.shape[2]
    copies = Copies(sems)
    arrivals = fetch_near(copies, pieces, buffer)
    for n, (step, other) in enumerate(NEAR):
        part = part_of(idx_ref, step, other, width)
        arrivals[n].append(copies.start(wo_ref.at[:, part], held.at[n]))
    for n in range(len(NEAR)):
        for copy in arrivals[n]:
            copy.wait()
        if n == 0:
            acc_ref[...] = nt(buffer[n], held[n])
        else:
            acc_ref[...] += nt(buffer[n], held[n])


def back_near(idx, pieces, wo):
    rows, width = pieces[0].shape
    cols = wo.shape[0]
    return pl.pallas_call(
        back_near_kernel,
        grid=(1,),
        in_specs=[SMEM_SPEC] + [HBM_SPEC] * 7,
        out_specs=whole((rows, cols)),
        out_shape=jax.ShapeDtypeStruct((rows, cols), F32),
        scratch_shapes=[
            pltpu.VMEM((6, rows, width), BF),
            pltpu.VMEM((6, cols, width), BF),
            pltpu.SemaphoreType.DMA((12,)),
        ],
        compiler_params=params(),
        cost_estimate=cost(12 * rows * width * cols, 12 * width * (rows + cols)),
        name="back_near",
    )(idx, *pieces, wo)


def back_kernel(*refs, scale):
    idx_ref, pieces = refs[0], refs[1:5]
    inputs = refs[5:17]
    grad_ref, dots_ref, gq_ref, gk_ref, gv_ref = refs[17:22]
    buffer, held, scaled_ref, gq, gk, gv, sems = refs[22:29]
    targets = refs[29:]
    wo_ref, near_ref, far_turned, near_turned = inputs[:4]
    copies = Copies(sems)
    arrivals = fetch_far(copies, pieces, buffer)
    rows, width = buffer.shape[1:]
    for n, (step, other) in enumerate(FAR):
        part = part_of(idx_ref, step, other, width)
        arrivals[n].append(copies.start(wo_ref.at[:, part], held.at[n]))
    acc_ref, turned_ref = targets[:2]
    acc_copy = copies.start(near_ref, acc_ref)
    loads = [copies.start(source, target) for source, target in zip(inputs[4:], targets[2:])]
    turned_loads = [
        copies.start(near_turned, turned_ref.at[:3]),
        copies.start(far_turned, turned_ref.at[3:]),
    ]
    q_ref, k_ref, k_turned_ref, v_ref, shares_ref, raw_ref, inverse_ref, rotary_ref = targets[2:]
    acc_copy.wait()
    for n in range(2):
        for copy in arrivals[n]:
            copy.wait()
        acc_ref[...] += nt(buffer[n], held[n])
    for copy in loads:
        copy.wait()

    cosine = rotary_ref[0]
    sine = rotary_ref[1]
    heads = shares_ref.shape[0]
    factor = inverse_ref[:, 0:1] * scale

    def rotate_back(u):
        return u * cosine - pltpu.roll(u, HD // 2, 1) * sine

    products = jnp.zeros((rows, HD), F32)

    def emit(at, grad):
        cols = slice(at * HD, (at + 1) * HD)
        rounded = grad.astype(BF)
        grad_ref[:, cols] = rounded
        scaled_ref[:, cols] = (grad * factor).astype(BF)
        return rounded.astype(F32) * raw_ref[:, cols]

    parts = turned_ref.shape[0]
    outs = []

    def send(held_ref, out_ref, at):
        tall = turned_ref.shape[1]
        wide = held_ref.shape[2]
        for j in range(parts):
            held_ref[j] = nn(turned_ref[j], scaled_ref[:, at : at + wide]).astype(BF)
            start = pl.multiple_of(idx_ref[j] * width, tall)
            outs.append(copies.start(held_ref.at[j], out_ref.at[pl.ds(start, tall)]))

    key_grad = jnp.zeros((rows, HD), F32)
    value_grad = jnp.zeros((rows, HD), F32)
    for h in range(heads):
        cols = slice(h * HD, (h + 1) * HD)
        grad_attended = acc_ref[:, cols].astype(BF)
        shares = shares_ref[h]
        share_grad = nt(v_ref[...], grad_attended)
        wide = shares.astype(F32)
        row_dot = jnp.sum(share_grad * wide, axis=0, keepdims=True)
        dscore = (wide * (share_grad - row_dot) * SCORE_SCALE).astype(BF)
        key_grad += nn(dscore, q_ref[:, cols])
        value_grad += nn(shares, grad_attended)
        products += emit(h, rotate_back(nn(k_turned_ref[...], dscore).T))
    products += emit(heads, rotate_back(key_grad))
    products += emit(heads + 1, value_grad)
    for copy in turned_loads:
        copy.wait()
    send(gq, gq_ref, 0)
    kv = gk.shape[2]
    for j in range(parts):
        both = nn(turned_ref[j], scaled_ref[:, heads * HD :]).astype(BF)
        gk[j] = both[:, :kv]
        gv[j] = both[:, kv:]
        tall = turned_ref.shape[1]
        start = pl.multiple_of(idx_ref[j] * width, tall)
        outs.append(copies.start(gk.at[j], gk_ref.at[pl.ds(start, tall)]))
        outs.append(copies.start(gv.at[j], gv_ref.at[pl.ds(start, tall)]))
    dots_ref[...] = lax.dot_general(
        jnp.ones((8, HD), F32), products, (((1,), (1,)), ((), ())),
        preferred_element_type=F32, precision=lax.Precision.HIGHEST,
    )
    for copy in outs:
        copy.wait()


def back(idx, pieces, wo, near, far_turned, near_turned, q, k, k_turned, v, shares, raw, inverse, rotary, scale):
    width = pieces[0].shape[1]
    cols, features = wo.shape
    rows = near.shape[0]
    kv_cols = k.shape[1]
    inputs = (wo, near, far_turned, near_turned, q, k, k_turned, v, shares, raw, inverse, rotary)
    loaded = (q, k, k_turned, v, shares, raw, inverse, rotary)
    weight_shapes = [
        jax.ShapeDtypeStruct((features, w), BF) for w in (cols, kv_cols, kv_cols)
    ]
    shapes = [jax.ShapeDtypeStruct(raw.shape, BF), jax.ShapeDtypeStruct((8, rows), F32)]
    return pl.pallas_call(
        functools.partial(back_kernel, scale=scale),
        grid=(1,),
        in_specs=[SMEM_SPEC] + [HBM_SPEC] * 16,
        out_specs=[whole(a.shape) for a in shapes] + [HBM_SPEC] * 3,
        out_shape=shapes + weight_shapes,
        scratch_shapes=[
            pltpu.VMEM((2, rows, width), BF),
            pltpu.VMEM((2, cols, width), BF),
            pltpu.VMEM(raw.shape, BF),
        ]
        + [pltpu.VMEM((4, features // 4, w.shape[1]), BF) for w in weight_shapes]
        + [
            pltpu.SemaphoreType.DMA((40,)),
            pltpu.VMEM(near.shape, F32),
            pltpu.VMEM((4, features // 4, rows), BF),
        ]
        + [pltpu.VMEM(a.shape, a.dtype) for a in loaded],
        compiler_params=params(),
        cost_estimate=cost(
            4 * rows * width * cols + 8 * cols * rows * rows + 2 * rows * features * (cols + 2 * kv_cols),
            2 * features * (rows + cols),
        ),
        name="back",
    )(idx, *pieces, *inputs)


def out_term_kernel(idx_ref, _, attended_ref, wo_ref, out_ref):
    out_ref[0] = nn(attended_ref[...], wo_ref[...]).astype(BF)


def out_terms(idx, after, attended, wo, width):
    rows, cols = attended.shape
    parts = 4
    grid_spec = pltpu.PrefetchScalarGridSpec(
        num_scalar_prefetch=1,
        grid=(parts,),
        in_specs=[
            HBM_SPEC,
            pl.BlockSpec((rows, cols), lambda j, idx: (0, 0)),
            pl.BlockSpec((cols, width), lambda j, idx: (0, idx[j])),
        ],
        out_specs=pl.BlockSpec((1, rows, width), lambda j, idx: (j, 0, 0)),
    )
    return pl.pallas_call(
        out_term_kernel,
        grid_spec=grid_spec,
        out_shape=jax.ShapeDtypeStruct((parts, rows, width), BF),
        compiler_params=params(),
        cost_estimate=cost(40 * parts * rows * cols * width, 40 * parts * width * (rows + cols)),
        name="out_terms",
    )(idx, after, attended, wo)


def input_term_kernel(idx_ref, _, grad_ref, dots_ref, wq_ref, wk_ref, wv_ref, out_ref):
    q_cols = wq_ref.shape[1]
    kv_cols = wk_ref.shape[1]
    rows = grad_ref.shape[0]
    dots = dots_ref[0:1, :]
    high = dots.astype(BF).astype(F32)
    line = lax.broadcasted_iota(jnp.int32, (16, dots.shape[1]), 0)
    extra = jnp.where(line == 0, high, jnp.where(line == 1, dots - high, 0.0))
    term = nt(grad_ref[:, :q_cols], wq_ref[...])
    term += nt(grad_ref[:, q_cols : q_cols + kv_cols], wk_ref[...])
    term += nt(grad_ref[:, q_cols + kv_cols :], wv_ref[...])
    out_ref[0, :rows] = term.astype(BF)
    out_ref[0, rows:] = extra.astype(BF)


def input_terms(idx, after, grad, dots, wq, wk, wv, width):
    rows, cols = grad.shape
    parts = 4
    grid_spec = pltpu.PrefetchScalarGridSpec(
        num_scalar_prefetch=1,
        grid=(parts,),
        in_specs=[
            HBM_SPEC,
            pl.BlockSpec((rows, cols), lambda j, idx: (0, 0)),
            pl.BlockSpec(dots.shape, lambda j, idx: (0, 0)),
        ]
        + [
            pl.BlockSpec((width, w.shape[1]), lambda j, idx: (idx[j], 0))
            for w in (wq, wk, wv)
        ],
        out_specs=pl.BlockSpec((1, rows + 16, width), lambda j, idx: (j, 0, 0)),
    )
    return pl.pallas_call(
        input_term_kernel,
        grid_spec=grid_spec,
        out_shape=jax.ShapeDtypeStruct((parts, rows + 16, width), BF),
        compiler_params=params(),
        cost_estimate=cost(40 * parts * rows * cols * width, 40 * parts * width * (rows + cols)),
        name="input_terms",
    )(idx, after, grad, dots, wq, wk, wv)


def shift(array, step):
    size = lax.axis_size("y")
    return lax.ppermute(array, "y", [(i, (i + step) % size) for i in range(size)])


def swap(array):
    return lax.ppermute(array, "core", [(0, 1), (1, 0)])


def start_gather(piece):
    return piece, shift(piece, 1), shift(piece, -1)


def end_gather(piece, below, above):
    half = piece.shape[0] // 2
    far = (shift(below[:half], 1), shift(above[half:], -1))
    near = (piece, below, above)
    near = near + tuple(swap(a) for a in near)
    return near, far + tuple(swap(a) for a in far)


def sum_pieces(mine_terms, other_terms):
    wide = lambda a: a.astype(F32)
    sums = (wide(mine_terms) + wide(swap(other_terms))).astype(BF)
    rows = sums.shape[1]
    half = rows // 32 * 16
    relay_top = shift(sums[3, :half], 1)
    relay_end = shift(sums[3, half:], -1)
    up = jnp.concatenate([(wide(sums[2, :half]) + wide(relay_top)).astype(BF), sums[2, half:]], axis=0)
    down = jnp.concatenate([sums[1, :half], (wide(sums[1, half:]) + wide(relay_end)).astype(BF)], axis=0)
    return wide(sums[0]) + wide(shift(up, 1)) + wide(shift(down, -1))


def exchange(panels):
    return lax.all_to_all(panels, ("x", "z"), split_axis=0, concat_axis=0, tiled=True)


def per_device(
    tokens, norm_gain, doc_ids, panel_plan, wq, wk, wv, wo, cotangent,
):
    y, core = lax.axis_index("y"), lax.axis_index("core")
    ys, cores = lax.axis_size("y"), lax.axis_size("core")
    block = lax.axis_index("x") * lax.axis_size("z") + lax.axis_index("z")
    dp = lax.axis_size("x") * lax.axis_size("z")
    count = panel_plan.shape[0]
    rows, width = tokens.shape
    panel = rows // count
    features = norm_gain.shape[0]

    around = (y + jnp.array(STEPS, jnp.int32)) % ys
    idx = jnp.concatenate([around * cores, core[None]])

    here_tokens = exchange(place(panel_plan, tokens.reshape(count, panel, width))).reshape(rows, width)
    arrived = exchange(
        place_meta(panel_plan, cotangent.reshape(count, panel, width), doc_ids.reshape(count, panel))
    )
    here_cot = arrived[:, :, :width].reshape(rows, width)
    meta = arrived[:, :, width : width + 3].reshape(rows, 3).astype(jnp.int32)
    docs = meta[:, 0] * 128 + meta[:, 1]
    at = block * rows + meta[:, 2] * panel + jnp.arange(rows, dtype=jnp.int32) % panel
    positions = (at - docs).astype(F32)
    frequency = ROPE_THETA ** (-2.0 * jnp.arange(HD // 2, dtype=F32) / HD)
    angles = positions[:, None] * frequency[None, :]
    cosine, sine = jnp.cos(angles), jnp.sin(angles)
    cosine = jnp.concatenate([cosine, cosine], axis=1)
    sine = jnp.concatenate([-sine, sine], axis=1)
    where_row = jnp.stack([docs, at])
    where_col = where_row.T

    tok_near = start_gather(here_tokens)
    cot_near = start_gather(here_cot)
    tok_pieces = end_gather(*tok_near)
    gain = norm_gain.reshape(features // width, width)
    near_turned, near_raw, near_squares = project_near(idx, tok_pieces[0], gain, wq, wk, wv)
    cot_near, near_raw = lax.optimization_barrier((cot_near, near_raw))
    cot_pieces = end_gather(*cot_near)
    far_turned, raw, inverse, q, k, k_turned, v, shares, attended = attend(
        idx, tok_pieces[1], gain, wq, wk, wv, near_raw, near_squares, cosine, sine, where_col, where_row
    )

    scale = (rows * dp) ** (-0.5)
    cot_nears, shares = lax.optimization_barrier((cot_pieces[0], shares))
    near = back_near(idx, cot_nears, wo)
    rotary = jnp.stack([cosine, sine])
    grad, dots, *grads = back(
        idx, cot_pieces[1], wo, near, far_turned, near_turned, q, k, k_turned, v, shares,
        raw, inverse, rotary, scale,
    )
    grad_query, grad_key, grad_value = lax.psum(tuple(grads), ("x", "z"))

    after = swap(dots)
    idx_mine, idx_other = around * cores + core, around * cores + (1 - core)
    out_sum = sum_pieces(
        *[out_terms(i, after, attended, wo, width) for i in (idx_mine, idx_other)]
    )
    output_rows = (here_tokens.astype(F32) + out_sum).astype(BF)
    in_sum = sum_pieces(
        *[input_terms(i, after, grad, dots, wq, wk, wv, width) for i in (idx_mine, idx_other)]
    )
    inverse = inverse[:, 0:1]
    mean_term = ((in_sum[rows] + in_sum[rows + 1]) / features)[:, None]
    own = y * cores + core
    own_gain = lax.dynamic_slice_in_dim(norm_gain, own * width, width, 0)
    own_scaled = here_tokens.astype(F32) * inverse
    grad_rows = here_cot.astype(F32) + inverse * (in_sum[:rows] * own_gain - own_scaled * mean_term)
    grad_rows = grad_rows.astype(BF)

    targets = panel_plan // count
    output = exchange(output_rows.reshape(dp, panel, width))[targets].reshape(rows, width)
    grad_tokens = exchange(grad_rows.reshape(dp, panel, width))[targets].reshape(rows, width)
    return output, grad_tokens, grad_query, grad_key, grad_value


def solution(mesh):
    axes = ("x", "z", "y", "core")
    split = Mesh(mesh.devices.reshape(4, 4, 4, 2), axes)
    dp, tensor = ("x", "z"), ("y", "core")
    in_specs = (
        P(dp, tensor),
        P(),
        P(dp),
        P(dp),
        P(None, tensor),
        P(None, tensor),
        P(None, tensor),
        P(tensor, None),
        P(dp, tensor),
    )
    out_specs = (
        P(dp, tensor),
        P(dp, tensor),
        P(None, tensor),
        P(None, tensor),
        P(None, tensor),
    )
    return jax.shard_map(
        per_device, mesh=split, in_specs=in_specs, out_specs=out_specs, check_vma=False
    )
```

```python
import functools

import jax
import jax.numpy as jnp
from jax import lax
from jax.experimental import pallas as pl
from jax.experimental.pallas import tpu as pltpu
from jax.sharding import Mesh
from jax.sharding import PartitionSpec as P

HD = 128
NORM_EPSILON = 1e-05
ROPE_THETA = 500000.0
SCORE_SCALE = HD ** (-0.5)
STEPS = (0, -1, 1, 2)
BF = jnp.bfloat16
F32 = jnp.float32
VMEM_LIMIT = 56 * 1024 * 1024


def params():
    return pltpu.CompilerParams(vmem_limit_bytes=VMEM_LIMIT)


def cost(flops, moved):
    return pl.CostEstimate(flops=int(flops), bytes_accessed=int(moved), transcendentals=0)


def nn(a, b):
    return lax.dot_general(a, b, (((1,), (0,)), ((), ())), preferred_element_type=F32)


def nt(a, b):
    return lax.dot_general(a, b, (((1,), (1,)), ((), ())), preferred_element_type=F32)


def place_kernel(plan_ref, rows_ref, out_ref):
    count = rows_ref.shape[0]
    for panel in range(count):
        out_ref[plan_ref[panel] // count] = rows_ref[panel]


def place(plan, panels):
    return pl.pallas_call(
        place_kernel,
        out_shape=jax.ShapeDtypeStruct(panels.shape, panels.dtype),
        in_specs=[
            pl.BlockSpec(memory_space=pltpu.SMEM),
            pl.BlockSpec(memory_space=pltpu.VMEM),
        ],
        out_specs=pl.BlockSpec(memory_space=pltpu.VMEM),
        compiler_params=params(),
        cost_estimate=cost(0, 2 * panels.size * 2),
        name="place",
    )(plan, panels)


def place_meta_kernel(plan_ref, rows_ref, docs_ref, out_ref):
    count, rows, width = rows_ref.shape
    for panel in range(count):
        target = plan_ref[panel] // count
        slot = plan_ref[panel] % count
        out_ref[target, :, :width] = rows_ref[panel]
        doc = docs_ref[panel]
        high = (doc // 128).astype(F32)
        low = (doc % 128).astype(F32)
        lane = lax.broadcasted_iota(jnp.int32, (rows, 128), 1)
        extra = jnp.where(lane == 0, high, 0.0)
        extra = jnp.where(lane == 1, low, extra)
        extra = jnp.where(lane == 2, slot.astype(F32), extra)
        out_ref[target, :, width:] = extra.astype(BF)


def place_meta(plan, panels, docs):
    count, rows, width = panels.shape
    return pl.pallas_call(
        place_meta_kernel,
        out_shape=jax.ShapeDtypeStruct((count, rows, width + 128), panels.dtype),
        in_specs=[
            pl.BlockSpec(memory_space=pltpu.SMEM),
            pl.BlockSpec(memory_space=pltpu.VMEM),
            pl.BlockSpec(memory_space=pltpu.VMEM),
        ],
        out_specs=pl.BlockSpec(memory_space=pltpu.VMEM),
        compiler_params=params(),
        cost_estimate=cost(0, 2 * panels.size * 2),
        name="place_meta",
    )(plan, panels, docs.reshape(count, rows, 1))


NEAR = tuple((step, other) for step in range(3) for other in (0, 1))
FAR = ((3, 0), (3, 1))

SMEM_SPEC = pl.BlockSpec(memory_space=pltpu.SMEM)
HBM_SPEC = pl.BlockSpec(memory_space=pltpu.HBM)


def whole(shape):
    return pl.BlockSpec(tuple(shape), lambda j: (0,) * len(shape))


def part_of(idx_ref, step, other, width):
    at = idx_ref[step] + (idx_ref[4] if not other else 1 - idx_ref[4])
    return pl.ds(pl.multiple_of(at * width, width), width)


class Copies:
    def __init__(self, sems):
        self.sems = sems
        self.count = 0

    def start(self, source, target):
        copy = pltpu.make_async_copy(source, target, self.sems.at[self.count])
        self.count += 1
        copy.start()
        return copy


def fetch_near(copies, pieces, buffer):
    return [[copies.start(pieces[3 * o + s], buffer.at[n])] for n, (s, o) in enumerate(NEAR)]


def fetch_far(copies, pieces, buffer):
    half = buffer.shape[1] // 2
    return [
        [
            copies.start(pieces[2 * n], buffer.at[n, :half]),
            copies.start(pieces[2 * n + 1], buffer.at[n, half:]),
        ]
        for n in range(2)
    ]


def project_steps(
    idx_ref, places, arrivals, copies, buffer, gain_ref, weights, held, turned_ref, raw_ref, fresh
):
    rows, width = buffer.shape[1:]
    for n, (step, other) in enumerate(places):
        part = part_of(idx_ref, step, other, width)
        for ref, target in zip(weights, held):
            arrivals[n].append(copies.start(ref.at[part], target.at[n]))
    squares = jnp.zeros((rows, 1), F32)
    for n, (step, other) in enumerate(places):
        core = idx_ref[4] if not other else 1 - idx_ref[4]
        for copy in arrivals[n]:
            copy.wait()
        wide = buffer[n].astype(F32)
        squares += jnp.sum(wide * wide, axis=1, keepdims=True)
        gained = (wide * gain_ref[pl.ds(idx_ref[step] + core, 1)]).astype(BF)
        turned_ref[step % 3, pl.ds(pl.multiple_of(core * width, width), width)] = gained.T
        at = 0
        for target in held:
            cols = slice(at, at + target.shape[2])
            at += target.shape[2]
            if fresh and n == 0:
                raw_ref[:, cols] = nn(gained, target[n])
            else:
                raw_ref[:, cols] += nn(gained, target[n])
    return squares


def project_near_kernel(*refs):
    idx_ref, pieces = refs[0], refs[1:7]
    gain_ref, wq, wk, wv, turned_ref, raw_ref, squares_ref, buffer, hq, hk, hv, sems = refs[7:]
    copies = Copies(sems)
    arrivals = fetch_near(copies, pieces, buffer)
    squares = project_steps(
        idx_ref, NEAR, arrivals, copies, buffer, gain_ref, (wq, wk, wv), (hq, hk, hv),
        turned_ref, raw_ref, True,
    )
    squares_ref[...] = jnp.broadcast_to(squares, squares_ref.shape)


def project_near(idx, pieces, gain, wq, wk, wv):
    rows, width = pieces[0].shape
    weights = (wq, wk, wv)
    cols = sum(w.shape[1] for w in weights)
    shapes = [
        jax.ShapeDtypeStruct((3, 2 * width, rows), BF),
        jax.ShapeDtypeStruct((rows, cols), F32),
        jax.ShapeDtypeStruct((rows, HD), F32),
    ]
    return pl.pallas_call(
        project_near_kernel,
        grid=(1,),
        in_specs=[SMEM_SPEC] + [HBM_SPEC] * 6 + [whole(gain.shape)] + [HBM_SPEC] * 3,
        out_specs=[whole(a.shape) for a in shapes],
        out_shape=shapes,
        scratch_shapes=[pltpu.VMEM((6, rows, width), BF)]
        + [pltpu.VMEM((6, width, w.shape[1]), BF) for w in weights]
        + [pltpu.SemaphoreType.DMA((24,))],
        compiler_params=params(),
        cost_estimate=cost(12 * rows * width * cols, 12 * width * (2 * rows + cols)),
        name="project_near",
    )(idx, *pieces, gain, *weights)


def attend_kernel(*refs):
    idx_ref, pieces = refs[0], refs[1:5]
    (
        gain_ref, wq, wk, wv, near_raw_ref, near_squares_ref,
        cosine_ref, sine_ref, where_col_ref, where_row_ref,
        turned_ref, raw_ref, inverse_ref, q_ref, k_ref, k_turned_ref, v_ref, shares_ref, attended_ref,
        buffer, hq, hk, hv, sems,
    ) = refs[5:]
    rows, width = buffer.shape[1:]
    copies = Copies(sems)
    arrivals = fetch_far(copies, pieces, buffer)
    raw_ref[...] = near_raw_ref[...]
    squares = project_steps(
        idx_ref, FAR, arrivals, copies, buffer, gain_ref, (wq, wk, wv), (hq, hk, hv),
        turned_ref, raw_ref, False,
    )
    features = wq.shape[0]
    inverse = lax.rsqrt((squares + near_squares_ref[:, 0:1]) / features + NORM_EPSILON)
    inverse_ref[...] = jnp.broadcast_to(inverse, inverse_ref.shape)
    raw_ref[...] = raw_ref[...] * inverse

    cosine = cosine_ref[...]
    sine = sine_ref[...]
    heads = shares_ref.shape[0]

    def rotate(u):
        return u * cosine + pltpu.roll(u, HD // 2, 1) * sine

    key = rotate(raw_ref[:, heads * HD : (heads + 1) * HD])
    k_ref[...] = key.astype(BF)
    k_turned_ref[...] = key.T.astype(BF)
    value = raw_ref[:, (heads + 1) * HD :]
    v_ref[...] = value.astype(BF)
    v_turned = value.T.astype(BF)
    doc_s = where_col_ref[:, 0:1]
    at_s = where_col_ref[:, 1:2]
    doc_g = where_row_ref[0:1, :]
    at_g = where_row_ref[1:2, :]
    allowed = (doc_s == doc_g) & (at_s <= at_g)
    for h in range(heads):
        cols = slice(h * HD, (h + 1) * HD)
        query = rotate(raw_ref[:, cols]).astype(BF)
        q_ref[:, cols] = query
        scores = nt(k_ref[...], query) * SCORE_SCALE
        weights = jnp.where(allowed, jnp.exp(scores), 0.0)
        total = jnp.sum(weights, axis=0, keepdims=True)
        shares = (weights * (1.0 / total)).astype(BF)
        shares_ref[h] = shares
        attended_ref[:, cols] = nn(v_turned, shares).T.astype(BF)


def attend(idx, pieces, gain, wq, wk, wv, near_raw, near_squares, cosine, sine, where_col, where_row):
    width = pieces[0].shape[1]
    rows, cols = near_raw.shape
    weights = (wq, wk, wv)
    heads = wq.shape[1] // HD
    shapes = [
        jax.ShapeDtypeStruct((1, 2 * width, rows), BF),
        jax.ShapeDtypeStruct((rows, cols), F32),
        jax.ShapeDtypeStruct((rows, HD), F32),
        jax.ShapeDtypeStruct((rows, heads * HD), BF),
        jax.ShapeDtypeStruct((rows, HD), BF),
        jax.ShapeDtypeStruct((HD, rows), BF),
        jax.ShapeDtypeStruct((rows, HD), BF),
        jax.ShapeDtypeStruct((heads, rows, rows), BF),
        jax.ShapeDtypeStruct((rows, heads * HD), BF),
    ]
    extras = (near_raw, near_squares, cosine, sine, where_col, where_row)
    return pl.pallas_call(
        attend_kernel,
        grid=(1,),
        in_specs=[SMEM_SPEC] + [HBM_SPEC] * 4 + [whole(gain.shape)] + [HBM_SPEC] * 3
        + [whole(a.shape) for a in extras],
        out_specs=[whole(a.shape) for a in shapes],
        out_shape=shapes,
        scratch_shapes=[pltpu.VMEM((2, rows, width), BF)]
        + [pltpu.VMEM((2, width, w.shape[1]), BF) for w in weights]
        + [pltpu.SemaphoreType.DMA((10,))],
        compiler_params=params(),
        cost_estimate=cost(
            4 * rows * width * cols + 4 * heads * rows * rows * HD, 4 * width * (2 * rows + cols)
        ),
        name="attend",
    )(idx, *pieces, gain, *weights, *extras)


def back_near_kernel(*refs):
    idx_ref, pieces = refs[0], refs[1:7]
    wo_ref, acc_ref, buffer, held, sems = refs[7:]
    width = buffer.shape[2]
    copies = Copies(sems)
    arrivals = fetch_near(copies, pieces, buffer)
    for n, (step, other) in enumerate(NEAR):
        part = part_of(idx_ref, step, other, width)
        arrivals[n].append(copies.start(wo_ref.at[:, part], held.at[n]))
    for n in range(len(NEAR)):
        for copy in arrivals[n]:
            copy.wait()
        if n == 0:
            acc_ref[...] = nt(buffer[n], held[n])
        else:
            acc_ref[...] += nt(buffer[n], held[n])


def back_near(idx, pieces, wo):
    rows, width = pieces[0].shape
    cols = wo.shape[0]
    return pl.pallas_call(
        back_near_kernel,
        grid=(1,),
        in_specs=[SMEM_SPEC] + [HBM_SPEC] * 7,
        out_specs=whole((rows, cols)),
        out_shape=jax.ShapeDtypeStruct((rows, cols), F32),
        scratch_shapes=[
            pltpu.VMEM((6, rows, width), BF),
            pltpu.VMEM((6, cols, width), BF),
            pltpu.SemaphoreType.DMA((12,)),
        ],
        compiler_params=params(),
        cost_estimate=cost(12 * rows * width * cols, 12 * width * (rows + cols)),
        name="back_near",
    )(idx, *pieces, wo)


def back_kernel(*refs, scale):
    idx_ref, pieces = refs[0], refs[1:5]
    inputs = refs[5:17]
    grad_ref, dots_ref, gq_ref, gk_ref, gv_ref = refs[17:22]
    buffer, held, scaled_ref, gq, gk, gv, sems = refs[22:29]
    targets = refs[29:]
    wo_ref, near_ref, far_turned, near_turned = inputs[:4]
    copies = Copies(sems)
    arrivals = fetch_far(copies, pieces, buffer)
    rows, width = buffer.shape[1:]
    for n, (step, other) in enumerate(FAR):
        part = part_of(idx_ref, step, other, width)
        arrivals[n].append(copies.start(wo_ref.at[:, part], held.at[n]))
    acc_ref, turned_ref = targets[:2]
    acc_copy = copies.start(near_ref, acc_ref)
    loads = [copies.start(source, target) for source, target in zip(inputs[4:], targets[2:])]
    turned_loads = [
        copies.start(near_turned, turned_ref.at[:3]),
        copies.start(far_turned, turned_ref.at[3:]),
    ]
    q_ref, k_ref, k_turned_ref, v_ref, shares_ref, raw_ref, inverse_ref, rotary_ref = targets[2:]
    acc_copy.wait()
    for n in range(2):
        for copy in arrivals[n]:
            copy.wait()
        acc_ref[...] += nt(buffer[n], held[n])
    for copy in loads:
        copy.wait()

    cosine = rotary_ref[0]
    sine = rotary_ref[1]
    heads = shares_ref.shape[0]
    factor = inverse_ref[:, 0:1] * scale

    def rotate_back(u):
        return u * cosine - pltpu.roll(u, HD // 2, 1) * sine

    products = jnp.zeros((rows, HD), F32)

    def emit(at, grad):
        cols = slice(at * HD, (at + 1) * HD)
        rounded = grad.astype(BF)
        grad_ref[:, cols] = rounded
        scaled_ref[:, cols] = (grad * factor).astype(BF)
        return rounded.astype(F32) * raw_ref[:, cols]

    parts = turned_ref.shape[0]
    outs = []

    def send(held_ref, out_ref, at):
        tall = turned_ref.shape[1]
        wide = held_ref.shape[2]
        for j in range(parts):
            held_ref[j] = nn(turned_ref[j], scaled_ref[:, at : at + wide]).astype(BF)
            start = pl.multiple_of(idx_ref[j] * width, tall)
            outs.append(copies.start(held_ref.at[j], out_ref.at[pl.ds(start, tall)]))

    key_grad = jnp.zeros((rows, HD), F32)
    value_grad = jnp.zeros((rows, HD), F32)
    for h in range(heads):
        cols = slice(h * HD, (h + 1) * HD)
        grad_attended = acc_ref[:, cols].astype(BF)
        shares = shares_ref[h]
        share_grad = nt(v_ref[...], grad_attended)
        wide = shares.astype(F32)
        row_dot = jnp.sum(share_grad * wide, axis=0, keepdims=True)
        dscore = (wide * (share_grad - row_dot) * SCORE_SCALE).astype(BF)
        key_grad += nn(dscore, q_ref[:, cols])
        value_grad += nn(shares, grad_attended)
        products += emit(h, rotate_back(nn(k_turned_ref[...], dscore).T))
    products += emit(heads, rotate_back(key_grad))
    products += emit(heads + 1, value_grad)
    for copy in turned_loads:
        copy.wait()
    send(gq, gq_ref, 0)
    kv = gk.shape[2]
    for j in range(parts):
        both = nn(turned_ref[j], scaled_ref[:, heads * HD :]).astype(BF)
        gk[j] = both[:, :kv]
        gv[j] = both[:, kv:]
        tall = turned_ref.shape[1]
        start = pl.multiple_of(idx_ref[j] * width, tall)
        outs.append(copies.start(gk.at[j], gk_ref.at[pl.ds(start, tall)]))
        outs.append(copies.start(gv.at[j], gv_ref.at[pl.ds(start, tall)]))
    dots_ref[...] = lax.dot_general(
        jnp.ones((8, HD), F32), products, (((1,), (1,)), ((), ())),
        preferred_element_type=F32, precision=lax.Precision.HIGHEST,
    )
    for copy in outs:
        copy.wait()


def back(idx, pieces, wo, near, far_turned, near_turned, q, k, k_turned, v, shares, raw, inverse, rotary, scale):
    width = pieces[0].shape[1]
    cols, features = wo.shape
    rows = near.shape[0]
    kv_cols = k.shape[1]
    inputs = (wo, near, far_turned, near_turned, q, k, k_turned, v, shares, raw, inverse, rotary)
    loaded = (q, k, k_turned, v, shares, raw, inverse, rotary)
    weight_shapes = [
        jax.ShapeDtypeStruct((features, w), BF) for w in (cols, kv_cols, kv_cols)
    ]
    shapes = [jax.ShapeDtypeStruct(raw.shape, BF), jax.ShapeDtypeStruct((8, rows), F32)]
    return pl.pallas_call(
        functools.partial(back_kernel, scale=scale),
        grid=(1,),
        in_specs=[SMEM_SPEC] + [HBM_SPEC] * 16,
        out_specs=[whole(a.shape) for a in shapes] + [HBM_SPEC] * 3,
        out_shape=shapes + weight_shapes,
        scratch_shapes=[
            pltpu.VMEM((2, rows, width), BF),
            pltpu.VMEM((2, cols, width), BF),
            pltpu.VMEM(raw.shape, BF),
        ]
        + [pltpu.VMEM((4, features // 4, w.shape[1]), BF) for w in weight_shapes]
        + [
            pltpu.SemaphoreType.DMA((40,)),
            pltpu.VMEM(near.shape, F32),
            pltpu.VMEM((4, features // 4, rows), BF),
        ]
        + [pltpu.VMEM(a.shape, a.dtype) for a in loaded],
        compiler_params=params(),
        cost_estimate=cost(
            4 * rows * width * cols + 8 * cols * rows * rows + 2 * rows * features * (cols + 2 * kv_cols),
            2 * features * (rows + cols),
        ),
        name="back",
    )(idx, *pieces, *inputs)


def out_term_kernel(idx_ref, _, attended_ref, wo_ref, out_ref):
    out_ref[0] = nn(attended_ref[...], wo_ref[...]).astype(BF)


def out_terms(idx, after, attended, wo, width):
    rows, cols = attended.shape
    parts = 4
    grid_spec = pltpu.PrefetchScalarGridSpec(
        num_scalar_prefetch=1,
        grid=(parts,),
        in_specs=[
            HBM_SPEC,
            pl.BlockSpec((rows, cols), lambda j, idx: (0, 0)),
            pl.BlockSpec((cols, width), lambda j, idx: (0, idx[j])),
        ],
        out_specs=pl.BlockSpec((1, rows, width), lambda j, idx: (j, 0, 0)),
    )
    return pl.pallas_call(
        out_term_kernel,
        grid_spec=grid_spec,
        out_shape=jax.ShapeDtypeStruct((parts, rows, width), BF),
        compiler_params=params(),
        cost_estimate=cost(40 * parts * rows * cols * width, 40 * parts * width * (rows + cols)),
        name="out_terms",
    )(idx, after, attended, wo)


def input_term_kernel(idx_ref, _, grad_ref, dots_ref, wq_ref, wk_ref, wv_ref, out_ref):
    q_cols = wq_ref.shape[1]
    kv_cols = wk_ref.shape[1]
    rows = grad_ref.shape[0]
    dots = dots_ref[0:1, :]
    high = dots.astype(BF).astype(F32)
    line = lax.broadcasted_iota(jnp.int32, (16, dots.shape[1]), 0)
    extra = jnp.where(line == 0, high, jnp.where(line == 1, dots - high, 0.0))
    term = nt(grad_ref[:, :q_cols], wq_ref[...])
    term += nt(grad_ref[:, q_cols : q_cols + kv_cols], wk_ref[...])
    term += nt(grad_ref[:, q_cols + kv_cols :], wv_ref[...])
    out_ref[0, :rows] = term.astype(BF)
    out_ref[0, rows:] = extra.astype(BF)


def input_terms(idx, after, grad, dots, wq, wk, wv, width):
    rows, cols = grad.shape
    parts = 4
    grid_spec = pltpu.PrefetchScalarGridSpec(
        num_scalar_prefetch=1,
        grid=(parts,),
        in_specs=[
            HBM_SPEC,
            pl.BlockSpec((rows, cols), lambda j, idx: (0, 0)),
            pl.BlockSpec(dots.shape, lambda j, idx: (0, 0)),
        ]
        + [
            pl.BlockSpec((width, w.shape[1]), lambda j, idx: (idx[j], 0))
            for w in (wq, wk, wv)
        ],
        out_specs=pl.BlockSpec((1, rows + 16, width), lambda j, idx: (j, 0, 0)),
    )
    return pl.pallas_call(
        input_term_kernel,
        grid_spec=grid_spec,
        out_shape=jax.ShapeDtypeStruct((parts, rows + 16, width), BF),
        compiler_params=params(),
        cost_estimate=cost(40 * parts * rows * cols * width, 40 * parts * width * (rows + cols)),
        name="input_terms",
    )(idx, after, grad, dots, wq, wk, wv)


def shift(array, step, axis="y"):
    size = lax.axis_size(axis)
    return lax.ppermute(array, axis, [(i, (i + step) % size) for i in range(size)])


def swap(array):
    return lax.ppermute(array, "core", [(0, 1), (1, 0)])


def gather_near(piece):
    return piece, shift(piece, 1), shift(piece, -1)


def gather_far(near):
    _, below, above = near
    half = below.shape[0] // 2
    return shift(below[:half], 1), shift(above[half:], -1)


def both_cores(pieces):
    return tuple(pieces) + tuple(swap(a) for a in pieces)


def sum_pieces(mine_terms, other_terms):
    wide = lambda a: a.astype(F32)
    sums = (wide(mine_terms) + wide(swap(other_terms))).astype(BF)
    rows = sums.shape[1]
    half = rows // 32 * 16
    relay_top = shift(sums[3, :half], 1)
    relay_end = shift(sums[3, half:], -1)
    up = jnp.concatenate([(wide(sums[2, :half]) + wide(relay_top)).astype(BF), sums[2, half:]], axis=0)
    down = jnp.concatenate([sums[1, :half], (wide(sums[1, half:]) + wide(relay_end)).astype(BF)], axis=0)
    return wide(sums[0]) + wide(shift(up, 1)) + wide(shift(down, -1))


def exchange(panels):
    return lax.all_to_all(panels, ("x", "z"), split_axis=0, concat_axis=0, tiled=True)


def per_device(
    tokens, norm_gain, doc_ids, panel_plan, wq, wk, wv, wo, cotangent,
):
    y, core = lax.axis_index("y"), lax.axis_index("core")
    ys, cores = lax.axis_size("y"), lax.axis_size("core")
    block = lax.axis_index("x") * lax.axis_size("z") + lax.axis_index("z")
    dp = lax.axis_size("x") * lax.axis_size("z")
    count = panel_plan.shape[0]
    rows, width = tokens.shape
    panel = rows // count
    features = norm_gain.shape[0]

    around = (y + jnp.array(STEPS, jnp.int32)) % ys
    steps = jnp.array(STEPS, jnp.int32)
    idx = jnp.concatenate(
        [around * cores, core[None], (lax.axis_index("x") + steps) % 4, (lax.axis_index("z") + steps) % 4]
    )

    here_tokens = exchange(place(panel_plan, tokens.reshape(count, panel, width))).reshape(rows, width)
    arrived = exchange(
        place_meta(panel_plan, cotangent.reshape(count, panel, width), doc_ids.reshape(count, panel))
    )
    here_cot = arrived[:, :, :width].reshape(rows, width)
    meta = arrived[:, :, width : width + 3].reshape(rows, 3).astype(jnp.int32)
    docs = meta[:, 0] * 128 + meta[:, 1]
    at = block * rows + meta[:, 2] * panel + jnp.arange(rows, dtype=jnp.int32) % panel
    positions = (at - docs).astype(F32)
    frequency = ROPE_THETA ** (-2.0 * jnp.arange(HD // 2, dtype=F32) / HD)
    angles = positions[:, None] * frequency[None, :]
    cosine, sine = jnp.cos(angles), jnp.sin(angles)
    cosine = jnp.concatenate([cosine, cosine], axis=1)
    sine = jnp.concatenate([-sine, sine], axis=1)
    where_row = jnp.stack([docs, at])
    where_col = where_row.T

    tok_near = gather_near(here_tokens)
    cot_near = gather_near(here_cot)
    tok_far = gather_far(tok_near)
    gain = norm_gain.reshape(features // width, width)
    near_turned, near_raw, near_squares = project_near(idx, both_cores(tok_near), gain, wq, wk, wv)
    tok_far, cot_near, near_raw = lax.optimization_barrier((tok_far, cot_near, near_raw))
    cot_far = gather_far(cot_near)
    far_turned, raw, inverse, q, k, k_turned, v, shares, attended = attend(
        idx, both_cores(tok_far), gain, wq, wk, wv, near_raw, near_squares, cosine, sine, where_col, where_row
    )

    scale = (rows * dp) ** (-0.5)
    cot_near, shares = lax.optimization_barrier((both_cores(cot_near), shares))
    near = back_near(idx, cot_near, wo)
    cot_far, near = lax.optimization_barrier((cot_far, near))
    rotary = jnp.stack([cosine, sine])
    grad, dots, *grads = back(
        idx, both_cores(cot_far), wo, near, far_turned, near_turned, q, k, k_turned, v, shares,
        raw, inverse, rotary, scale,
    )
    grad_query, grad_key, grad_value = lax.psum(tuple(grads), ("x", "z"))
    after = swap(dots)
    idx_mine, idx_other = around * cores + core, around * cores + (1 - core)
    out_sum = sum_pieces(
        *[out_terms(i, after, attended, wo, width) for i in (idx_mine, idx_other)]
    )
    output_rows = (here_tokens.astype(F32) + out_sum).astype(BF)
    in_sum = sum_pieces(
        *[input_terms(i, after, grad, dots, wq, wk, wv, width) for i in (idx_mine, idx_other)]
    )
    inverse = inverse[:, 0:1]
    mean_term = ((in_sum[rows] + in_sum[rows + 1]) / features)[:, None]
    own = y * cores + core
    own_gain = lax.dynamic_slice_in_dim(norm_gain, own * width, width, 0)
    own_scaled = here_tokens.astype(F32) * inverse
    grad_rows = here_cot.astype(F32) + inverse * (in_sum[:rows] * own_gain - own_scaled * mean_term)
    grad_rows = grad_rows.astype(BF)

    targets = panel_plan // count
    output = exchange(output_rows.reshape(dp, panel, width))[targets].reshape(rows, width)
    grad_tokens = exchange(grad_rows.reshape(dp, panel, width))[targets].reshape(rows, width)
    return output, grad_tokens, grad_query, grad_key, grad_value


def solution(mesh):
    axes = ("x", "z", "y", "core")
    split = Mesh(mesh.devices.reshape(4, 4, 4, 2), axes)
    dp, tensor = ("x", "z"), ("y", "core")
    in_specs = (
        P(dp, tensor),
        P(),
        P(dp),
        P(dp),
        P(None, tensor),
        P(None, tensor),
        P(None, tensor),
        P(tensor, None),
        P(dp, tensor),
    )
    out_specs = (
        P(dp, tensor),
        P(dp, tensor),
        P(None, tensor),
        P(None, tensor),
        P(None, tensor),
    )
    return jax.shard_map(
        per_device, mesh=split, in_specs=in_specs, out_specs=out_specs, check_vma=False
    )
```

```python
import functools

import jax
import jax.numpy as jnp
from jax import lax
from jax.experimental import pallas as pl
from jax.experimental.pallas import tpu as pltpu
from jax.sharding import Mesh
from jax.sharding import PartitionSpec as P

HD = 128
NORM_EPSILON = 1e-05
ROPE_THETA = 500000.0
SCORE_SCALE = HD ** (-0.5)
STEPS = (0, -1, 1, 2)
BF = jnp.bfloat16
F32 = jnp.float32
VMEM_LIMIT = 56 * 1024 * 1024


def params():
    return pltpu.CompilerParams(vmem_limit_bytes=VMEM_LIMIT)


def cost(flops, moved):
    return pl.CostEstimate(flops=int(flops), bytes_accessed=int(moved), transcendentals=0)


def nn(a, b):
    return lax.dot_general(a, b, (((1,), (0,)), ((), ())), preferred_element_type=F32)


def nt(a, b):
    return lax.dot_general(a, b, (((1,), (1,)), ((), ())), preferred_element_type=F32)


def place_kernel(plan_ref, rows_ref, out_ref):
    count = rows_ref.shape[0]
    for panel in range(count):
        out_ref[plan_ref[panel] // count] = rows_ref[panel]


def place(plan, panels):
    return pl.pallas_call(
        place_kernel,
        out_shape=jax.ShapeDtypeStruct(panels.shape, panels.dtype),
        in_specs=[
            pl.BlockSpec(memory_space=pltpu.SMEM),
            pl.BlockSpec(memory_space=pltpu.VMEM),
        ],
        out_specs=pl.BlockSpec(memory_space=pltpu.VMEM),
        compiler_params=params(),
        cost_estimate=cost(0, 2 * panels.size * 2),
        name="place",
    )(plan, panels)


def place_meta_kernel(plan_ref, rows_ref, docs_ref, out_ref):
    count, rows, width = rows_ref.shape
    for panel in range(count):
        target = plan_ref[panel] // count
        slot = plan_ref[panel] % count
        out_ref[target, :, :width] = rows_ref[panel]
        doc = docs_ref[panel]
        high = (doc // 128).astype(F32)
        low = (doc % 128).astype(F32)
        lane = lax.broadcasted_iota(jnp.int32, (rows, 128), 1)
        extra = jnp.where(lane == 0, high, 0.0)
        extra = jnp.where(lane == 1, low, extra)
        extra = jnp.where(lane == 2, slot.astype(F32), extra)
        out_ref[target, :, width:] = extra.astype(BF)


def place_meta(plan, panels, docs):
    count, rows, width = panels.shape
    return pl.pallas_call(
        place_meta_kernel,
        out_shape=jax.ShapeDtypeStruct((count, rows, width + 128), panels.dtype),
        in_specs=[
            pl.BlockSpec(memory_space=pltpu.SMEM),
            pl.BlockSpec(memory_space=pltpu.VMEM),
            pl.BlockSpec(memory_space=pltpu.VMEM),
        ],
        out_specs=pl.BlockSpec(memory_space=pltpu.VMEM),
        compiler_params=params(),
        cost_estimate=cost(0, 2 * panels.size * 2),
        name="place_meta",
    )(plan, panels, docs.reshape(count, rows, 1))


NEAR = tuple((step, other) for step in range(3) for other in (0, 1))
FAR = ((3, 0), (3, 1))

SMEM_SPEC = pl.BlockSpec(memory_space=pltpu.SMEM)
HBM_SPEC = pl.BlockSpec(memory_space=pltpu.HBM)


def whole(shape):
    return pl.BlockSpec(tuple(shape), lambda j: (0,) * len(shape))


def part_of(idx_ref, step, other, width):
    at = idx_ref[step] + (idx_ref[4] if not other else 1 - idx_ref[4])
    return pl.ds(pl.multiple_of(at * width, width), width)


class Copies:
    def __init__(self, sems):
        self.sems = sems
        self.count = 0

    def start(self, source, target):
        copy = pltpu.make_async_copy(source, target, self.sems.at[self.count])
        self.count += 1
        copy.start()
        return copy


def fetch_near(copies, pieces, buffer):
    return [[copies.start(pieces[3 * o + s], buffer.at[n])] for n, (s, o) in enumerate(NEAR)]


def fetch_far(copies, pieces, buffer):
    half = buffer.shape[1] // 2
    return [
        [
            copies.start(pieces[2 * n], buffer.at[n, :half]),
            copies.start(pieces[2 * n + 1], buffer.at[n, half:]),
        ]
        for n in range(2)
    ]


def project_steps(
    idx_ref, places, arrivals, copies, buffer, gain_ref, weights, held, stage, turned_ref, raw_ref, fresh
):
    rows, width = buffer.shape[1:]
    for n, (step, other) in enumerate(places):
        part = part_of(idx_ref, step, other, width)
        for ref, target in zip(weights, held):
            arrivals[n].append(copies.start(ref.at[part], target.at[n]))
    squares = jnp.zeros((rows, 1), F32)
    sent = []
    for n, (step, other) in enumerate(places):
        core = idx_ref[4] if not other else 1 - idx_ref[4]
        for copy in arrivals[n]:
            copy.wait()
        wide = buffer[n].astype(F32)
        squares += jnp.sum(wide * wide, axis=1, keepdims=True)
        gained = (wide * gain_ref[pl.ds(idx_ref[step] + core, 1)]).astype(BF)
        stage[n] = gained.T
        here = pl.ds(pl.multiple_of(core * width, width), width)
        sent.append(copies.start(stage.at[n], turned_ref.at[step % 3, here]))
        at = 0
        for target in held:
            cols = slice(at, at + target.shape[2])
            at += target.shape[2]
            if fresh and n == 0:
                raw_ref[:, cols] = nn(gained, target[n])
            else:
                raw_ref[:, cols] += nn(gained, target[n])
    return squares, sent


def project_near_kernel(*refs):
    idx_ref, pieces = refs[0], refs[1:7]
    gain_ref, wq, wk, wv, turned_ref, raw_ref, squares_ref, buffer, stage, hq, hk, hv, sems = refs[7:]
    copies = Copies(sems)
    arrivals = fetch_near(copies, pieces, buffer)
    squares, sent = project_steps(
        idx_ref, NEAR, arrivals, copies, buffer, gain_ref, (wq, wk, wv), (hq, hk, hv),
        stage, turned_ref, raw_ref, True,
    )
    squares_ref[...] = jnp.broadcast_to(squares, squares_ref.shape)
    for copy in sent:
        copy.wait()


def project_near(idx, pieces, gain, wq, wk, wv):
    rows, width = pieces[0].shape
    weights = (wq, wk, wv)
    cols = sum(w.shape[1] for w in weights)
    shapes = [
        jax.ShapeDtypeStruct((3, 2 * width, rows), BF),
        jax.ShapeDtypeStruct((rows, cols), F32),
        jax.ShapeDtypeStruct((rows, HD), F32),
    ]
    return pl.pallas_call(
        project_near_kernel,
        grid=(1,),
        in_specs=[SMEM_SPEC] + [HBM_SPEC] * 6 + [whole(gain.shape)] + [HBM_SPEC] * 3,
        out_specs=[HBM_SPEC] + [whole(a.shape) for a in shapes[1:]],
        out_shape=shapes,
        scratch_shapes=[pltpu.VMEM((6, rows, width), BF), pltpu.VMEM((6, width, rows), BF)]
        + [pltpu.VMEM((6, width, w.shape[1]), BF) for w in weights]
        + [pltpu.SemaphoreType.DMA((30,))],
        compiler_params=params(),
        cost_estimate=cost(12 * rows * width * cols, 12 * width * (2 * rows + cols)),
        name="project_near",
    )(idx, *pieces, gain, *weights)


def attend_kernel(*refs):
    idx_ref, pieces = refs[0], refs[1:5]
    (
        gain_ref, wq, wk, wv, near_raw_ref, near_squares_ref, rotary_ref, where_ref,
        turned_ref, inverse_ref, q_ref, k_ref, k_turned_ref, v_ref, shares_ref, attended_ref,
        raw_ref, shares_stage, buffer, stage, hq, hk, hv, sems,
    ) = refs[5:]
    rows, width = buffer.shape[1:]
    copies = Copies(sems)
    arrivals = fetch_far(copies, pieces, buffer)
    raw_ref[...] = near_raw_ref[...]
    squares, sent = project_steps(
        idx_ref, FAR, arrivals, copies, buffer, gain_ref, (wq, wk, wv), (hq, hk, hv),
        stage, turned_ref, raw_ref, False,
    )
    features = wq.shape[0]
    inverse = lax.rsqrt((squares + near_squares_ref[:, 0:1]) / features + NORM_EPSILON)
    inverse_ref[...] = jnp.broadcast_to(inverse, inverse_ref.shape)

    cosine = rotary_ref[0] * inverse
    sine = rotary_ref[1] * inverse
    heads = shares_stage.shape[0]

    def rotate(u):
        return u * cosine + pltpu.roll(u, HD // 2, 1) * sine

    key = rotate(raw_ref[:, heads * HD : (heads + 1) * HD])
    k_ref[...] = key.astype(BF)
    k_turned_ref[...] = key.T.astype(BF)
    value = raw_ref[:, (heads + 1) * HD :] * inverse
    v_ref[...] = value.astype(BF)
    v_turned = value.T.astype(BF)
    down = where_ref[...].T
    doc_s = down[:, 0:1]
    at_s = down[:, 1:2]
    doc_g = where_ref[0:1, :]
    at_g = where_ref[1:2, :]
    allowed = (doc_s == doc_g) & (at_s <= at_g)
    for h in range(heads):
        cols = slice(h * HD, (h + 1) * HD)
        query = rotate(raw_ref[:, cols]).astype(BF)
        q_ref[:, cols] = query
        scores = nt(k_ref[...], query) * SCORE_SCALE
        weights = jnp.where(allowed, jnp.exp(scores), 0.0)
        total = jnp.sum(weights, axis=0, keepdims=True)
        shares = (weights * (1.0 / total)).astype(BF)
        shares_stage[h] = shares
        sent.append(copies.start(shares_stage.at[h], shares_ref.at[h]))
        attended_ref[:, cols] = nn(v_turned, shares).T.astype(BF)
    for copy in sent:
        copy.wait()


def attend(idx, pieces, gain, wq, wk, wv, near_raw, near_squares, rotary, where):
    width = pieces[0].shape[1]
    rows, cols = near_raw.shape
    weights = (wq, wk, wv)
    heads = wq.shape[1] // HD
    shapes = [
        jax.ShapeDtypeStruct((1, 2 * width, rows), BF),
        jax.ShapeDtypeStruct((rows, HD), F32),
        jax.ShapeDtypeStruct((rows, heads * HD), BF),
        jax.ShapeDtypeStruct((rows, HD), BF),
        jax.ShapeDtypeStruct((HD, rows), BF),
        jax.ShapeDtypeStruct((rows, HD), BF),
        jax.ShapeDtypeStruct((heads, rows, rows), BF),
        jax.ShapeDtypeStruct((rows, heads * HD), BF),
    ]
    extras = (near_raw, near_squares, rotary, where)
    out_specs = [whole(a.shape) for a in shapes]
    out_specs[0] = out_specs[6] = HBM_SPEC
    return pl.pallas_call(
        attend_kernel,
        grid=(1,),
        in_specs=[SMEM_SPEC] + [HBM_SPEC] * 4 + [whole(gain.shape)] + [HBM_SPEC] * 3
        + [whole(a.shape) for a in extras],
        out_specs=out_specs,
        out_shape=shapes,
        scratch_shapes=[
            pltpu.VMEM((rows, cols), F32),
            pltpu.VMEM((heads, rows, rows), BF),
            pltpu.VMEM((2, rows, width), BF),
            pltpu.VMEM((2, width, rows), BF),
        ]
        + [pltpu.VMEM((2, width, w.shape[1]), BF) for w in weights]
        + [pltpu.SemaphoreType.DMA((16,))],
        compiler_params=params(),
        cost_estimate=cost(
            4 * rows * width * cols + 4 * heads * rows * rows * HD, 4 * width * (2 * rows + cols)
        ),
        name="attend",
    )(idx, *pieces, gain, *weights, *extras)


def back_near_kernel(*refs):
    idx_ref, pieces = refs[0], refs[1:7]
    wo_ref, acc_ref, buffer, held, sems = refs[7:]
    width = buffer.shape[2]
    copies = Copies(sems)
    arrivals = fetch_near(copies, pieces, buffer)
    for n, (step, other) in enumerate(NEAR):
        part = part_of(idx_ref, step, other, width)
        arrivals[n].append(copies.start(wo_ref.at[:, part], held.at[n]))
    for n in range(len(NEAR)):
        for copy in arrivals[n]:
            copy.wait()
        if n == 0:
            acc_ref[...] = nt(buffer[n], held[n])
        else:
            acc_ref[...] += nt(buffer[n], held[n])


def back_near(idx, pieces, wo):
    rows, width = pieces[0].shape
    cols = wo.shape[0]
    return pl.pallas_call(
        back_near_kernel,
        grid=(1,),
        in_specs=[SMEM_SPEC] + [HBM_SPEC] * 7,
        out_specs=whole((rows, cols)),
        out_shape=jax.ShapeDtypeStruct((rows, cols), F32),
        scratch_shapes=[
            pltpu.VMEM((6, rows, width), BF),
            pltpu.VMEM((6, cols, width), BF),
            pltpu.SemaphoreType.DMA((12,)),
        ],
        compiler_params=params(),
        cost_estimate=cost(12 * rows * width * cols, 12 * width * (rows + cols)),
        name="back_near",
    )(idx, *pieces, wo)


def back_kernel(*refs, scale):
    idx_ref, pieces = refs[0], refs[1:5]
    inputs = refs[5:16]
    grad_ref, dots_ref, gq_ref, gk_ref, gv_ref = refs[16:21]
    buffer, held, scaled_ref, gq, gk, gv, sems = refs[21:28]
    targets = refs[28:]
    wo_ref, near_ref, far_turned, near_turned = inputs[:4]
    copies = Copies(sems)
    arrivals = fetch_far(copies, pieces, buffer)
    rows, width = buffer.shape[1:]
    for n, (step, other) in enumerate(FAR):
        part = part_of(idx_ref, step, other, width)
        arrivals[n].append(copies.start(wo_ref.at[:, part], held.at[n]))
    acc_ref, turned_ref = targets[:2]
    acc_copy = copies.start(near_ref, acc_ref)
    loads = [copies.start(source, target) for source, target in zip(inputs[4:], targets[2:])]
    turned_loads = [
        copies.start(near_turned, turned_ref.at[:3]),
        copies.start(far_turned, turned_ref.at[3:]),
    ]
    q_ref, k_ref, k_turned_ref, v_ref, shares_ref, inverse_ref, rotary_ref = targets[2:]
    acc_copy.wait()
    for n in range(2):
        for copy in arrivals[n]:
            copy.wait()
        acc_ref[...] += nt(buffer[n], held[n])
    for copy in loads:
        copy.wait()

    cosine = rotary_ref[0]
    sine = rotary_ref[1]
    heads = shares_ref.shape[0]
    factor = inverse_ref[:, 0:1] * scale

    def rotate_back(u):
        return u * cosine - pltpu.roll(u, HD // 2, 1) * sine

    products = jnp.zeros((rows, HD), F32)

    def emit(at, grad):
        cols = slice(at * HD, (at + 1) * HD)
        grad_ref[:, cols] = grad.astype(BF)
        scaled_ref[:, cols] = (grad * factor).astype(BF)

    parts = turned_ref.shape[0]
    outs = []

    def send(held_ref, out_ref, at):
        tall = turned_ref.shape[1]
        wide = held_ref.shape[2]
        for j in range(parts):
            held_ref[j] = nn(turned_ref[j], scaled_ref[:, at : at + wide]).astype(BF)
            start = pl.multiple_of(idx_ref[j] * width, tall)
            outs.append(copies.start(held_ref.at[j], out_ref.at[pl.ds(start, tall)]))

    key_grad = jnp.zeros((rows, HD), F32)
    value_grad = jnp.zeros((rows, HD), F32)
    for h in range(heads):
        cols = slice(h * HD, (h + 1) * HD)
        grad_attended = acc_ref[:, cols].astype(BF)
        shares = shares_ref[h]
        share_grad = nt(v_ref[...], grad_attended)
        wide = shares.astype(F32)
        row_dot = jnp.sum(share_grad * wide, axis=0, keepdims=True)
        dscore = (wide * (share_grad - row_dot) * SCORE_SCALE).astype(BF)
        key_grad += nn(dscore, q_ref[:, cols])
        value_grad += nn(shares, grad_attended)
        query_grad = nn(k_turned_ref[...], dscore).T
        products += query_grad * q_ref[:, cols].astype(F32)
        emit(h, rotate_back(query_grad))
    products += key_grad * k_ref[...].astype(F32) + value_grad * v_ref[...].astype(F32)
    emit(heads, rotate_back(key_grad))
    emit(heads + 1, value_grad)
    for copy in turned_loads:
        copy.wait()
    send(gq, gq_ref, 0)
    kv = gk.shape[2]
    for j in range(parts):
        both = nn(turned_ref[j], scaled_ref[:, heads * HD :]).astype(BF)
        gk[j] = both[:, :kv]
        gv[j] = both[:, kv:]
        tall = turned_ref.shape[1]
        start = pl.multiple_of(idx_ref[j] * width, tall)
        outs.append(copies.start(gk.at[j], gk_ref.at[pl.ds(start, tall)]))
        outs.append(copies.start(gv.at[j], gv_ref.at[pl.ds(start, tall)]))
    dots_ref[...] = lax.dot_general(
        jnp.ones((8, HD), F32), products, (((1,), (1,)), ((), ())),
        preferred_element_type=F32, precision=lax.Precision.HIGHEST,
    )
    for copy in outs:
        copy.wait()


def back(idx, pieces, wo, near, far_turned, near_turned, q, k, k_turned, v, shares, inverse, rotary, scale):
    width = pieces[0].shape[1]
    cols, features = wo.shape
    rows = near.shape[0]
    kv_cols = k.shape[1]
    grad_shape = (rows, cols + 2 * kv_cols)
    inputs = (wo, near, far_turned, near_turned, q, k, k_turned, v, shares, inverse, rotary)
    loaded = (q, k, k_turned, v, shares, inverse, rotary)
    weight_shapes = [
        jax.ShapeDtypeStruct((features, w), BF) for w in (cols, kv_cols, kv_cols)
    ]
    shapes = [jax.ShapeDtypeStruct(grad_shape, BF), jax.ShapeDtypeStruct((8, rows), F32)]
    return pl.pallas_call(
        functools.partial(back_kernel, scale=scale),
        grid=(1,),
        in_specs=[SMEM_SPEC] + [HBM_SPEC] * 15,
        out_specs=[whole(a.shape) for a in shapes] + [HBM_SPEC] * 3,
        out_shape=shapes + weight_shapes,
        scratch_shapes=[
            pltpu.VMEM((2, rows, width), BF),
            pltpu.VMEM((2, cols, width), BF),
            pltpu.VMEM(grad_shape, BF),
        ]
        + [pltpu.VMEM((4, features // 4, w.shape[1]), BF) for w in weight_shapes]
        + [
            pltpu.SemaphoreType.DMA((40,)),
            pltpu.VMEM(near.shape, F32),
            pltpu.VMEM((4, features // 4, rows), BF),
        ]
        + [pltpu.VMEM(a.shape, a.dtype) for a in loaded],
        compiler_params=params(),
        cost_estimate=cost(
            4 * rows * width * cols + 8 * cols * rows * rows + 2 * rows * features * (cols + 2 * kv_cols),
            2 * features * (rows + cols),
        ),
        name="back",
    )(idx, *pieces, *inputs)


def finish_kernel(*refs):
    for source, target in zip(refs[:3], refs[3:]):
        target[...] = source[...]


def finish(arrays):
    parts = 4
    specs = [pl.BlockSpec((a.shape[0] // parts, a.shape[1]), lambda j: (j, 0)) for a in arrays]
    return pl.pallas_call(
        finish_kernel,
        grid=(parts,),
        in_specs=specs,
        out_specs=specs,
        out_shape=[jax.ShapeDtypeStruct(a.shape, a.dtype) for a in arrays],
        compiler_params=params(),
        cost_estimate=cost(0, 4 * sum(a.size for a in arrays)),
        name="finish",
    )(*arrays)


def out_term_kernel(idx_ref, _, attended_ref, wo_ref, out_ref):
    out_ref[0] = nn(attended_ref[...], wo_ref[...]).astype(BF)


def out_terms(idx, after, attended, wo, width):
    rows, cols = attended.shape
    parts = 4
    grid_spec = pltpu.PrefetchScalarGridSpec(
        num_scalar_prefetch=1,
        grid=(parts,),
        in_specs=[
            HBM_SPEC,
            pl.BlockSpec((rows, cols), lambda j, idx: (0, 0)),
            pl.BlockSpec((cols, width), lambda j, idx: (0, idx[j])),
        ],
        out_specs=pl.BlockSpec((1, rows, width), lambda j, idx: (j, 0, 0)),
    )
    return pl.pallas_call(
        out_term_kernel,
        grid_spec=grid_spec,
        out_shape=jax.ShapeDtypeStruct((parts, rows, width), BF),
        compiler_params=params(),
        cost_estimate=cost(40 * parts * rows * cols * width, 40 * parts * width * (rows + cols)),
        name="out_terms",
    )(idx, after, attended, wo)


def input_term_kernel(idx_ref, _, grad_ref, dots_ref, wq_ref, wk_ref, wv_ref, out_ref):
    q_cols = wq_ref.shape[1]
    kv_cols = wk_ref.shape[1]
    rows = grad_ref.shape[0]
    dots = dots_ref[0:1, :]
    high = dots.astype(BF).astype(F32)
    line = lax.broadcasted_iota(jnp.int32, (16, dots.shape[1]), 0)
    extra = jnp.where(line == 0, high, jnp.where(line == 1, dots - high, 0.0))
    term = nt(grad_ref[:, :q_cols], wq_ref[...])
    term += nt(grad_ref[:, q_cols : q_cols + kv_cols], wk_ref[...])
    term += nt(grad_ref[:, q_cols + kv_cols :], wv_ref[...])
    out_ref[0, :rows] = term.astype(BF)
    out_ref[0, rows:] = extra.astype(BF)


def input_terms(idx, after, grad, dots, wq, wk, wv, width):
    rows, cols = grad.shape
    parts = 4
    grid_spec = pltpu.PrefetchScalarGridSpec(
        num_scalar_prefetch=1,
        grid=(parts,),
        in_specs=[
            HBM_SPEC,
            pl.BlockSpec((rows, cols), lambda j, idx: (0, 0)),
            pl.BlockSpec(dots.shape, lambda j, idx: (0, 0)),
        ]
        + [
            pl.BlockSpec((width, w.shape[1]), lambda j, idx: (idx[j], 0))
            for w in (wq, wk, wv)
        ],
        out_specs=pl.BlockSpec((1, rows + 16, width), lambda j, idx: (j, 0, 0)),
    )
    return pl.pallas_call(
        input_term_kernel,
        grid_spec=grid_spec,
        out_shape=jax.ShapeDtypeStruct((parts, rows + 16, width), BF),
        compiler_params=params(),
        cost_estimate=cost(40 * parts * rows * cols * width, 40 * parts * width * (rows + cols)),
        name="input_terms",
    )(idx, after, grad, dots, wq, wk, wv)


def shift(array, step, axis="y"):
    size = lax.axis_size(axis)
    return lax.ppermute(array, axis, [(i, (i + step) % size) for i in range(size)])


def swap(array):
    return lax.ppermute(array, "core", [(0, 1), (1, 0)])


def gather_near(piece):
    return piece, shift(piece, 1), shift(piece, -1)


def gather_far(near):
    _, below, above = near
    half = below.shape[0] // 2
    return shift(below[:half], 1), shift(above[half:], -1)


def both_cores(pieces):
    return tuple(pieces) + tuple(swap(a) for a in pieces)


def sum_pieces(mine_terms, other_terms):
    wide = lambda a: a.astype(F32)
    sums = (wide(mine_terms) + wide(swap(other_terms))).astype(BF)
    rows = sums.shape[1]
    half = rows // 32 * 16
    relay_top = shift(sums[3, :half], 1)
    relay_end = shift(sums[3, half:], -1)
    up = jnp.concatenate([(wide(sums[2, :half]) + wide(relay_top)).astype(BF), sums[2, half:]], axis=0)
    down = jnp.concatenate([sums[1, :half], (wide(sums[1, half:]) + wide(relay_end)).astype(BF)], axis=0)
    return wide(sums[0]) + wide(shift(up, 1)) + wide(shift(down, -1))


def exchange(panels):
    return lax.all_to_all(panels, ("x", "z"), split_axis=0, concat_axis=0, tiled=True)


def per_device(
    tokens, norm_gain, doc_ids, panel_plan, wq, wk, wv, wo, cotangent,
):
    y, core = lax.axis_index("y"), lax.axis_index("core")
    ys, cores = lax.axis_size("y"), lax.axis_size("core")
    block = lax.axis_index("x") * lax.axis_size("z") + lax.axis_index("z")
    dp = lax.axis_size("x") * lax.axis_size("z")
    count = panel_plan.shape[0]
    rows, width = tokens.shape
    panel = rows // count
    features = norm_gain.shape[0]

    around = (y + jnp.array(STEPS, jnp.int32)) % ys
    steps = jnp.array(STEPS, jnp.int32)
    idx = jnp.concatenate(
        [around * cores, core[None], (lax.axis_index("x") + steps) % 4, (lax.axis_index("z") + steps) % 4]
    )

    here_tokens = exchange(place(panel_plan, tokens.reshape(count, panel, width))).reshape(rows, width)
    arrived = exchange(
        place_meta(panel_plan, cotangent.reshape(count, panel, width), doc_ids.reshape(count, panel))
    )
    here_cot = arrived[:, :, :width].reshape(rows, width)
    meta = arrived[:, :, width : width + 3].reshape(rows, 3).astype(jnp.int32)
    docs = meta[:, 0] * 128 + meta[:, 1]
    at = block * rows + meta[:, 2] * panel + jnp.arange(rows, dtype=jnp.int32) % panel
    positions = (at - docs).astype(F32)
    frequency = ROPE_THETA ** (-2.0 * jnp.arange(HD // 2, dtype=F32) / HD)
    angles = positions[:, None] * frequency[None, :]
    cosine, sine = jnp.cos(angles), jnp.sin(angles)
    rotary = jnp.stack(
        [jnp.concatenate([cosine, cosine], axis=1), jnp.concatenate([-sine, sine], axis=1)]
    )
    where = jnp.pad(jnp.stack([docs, at]).astype(F32), ((0, 6), (0, 0)))

    tok_near = gather_near(here_tokens)
    cot_near = gather_near(here_cot)
    tok_far = gather_far(tok_near)
    gain = norm_gain.reshape(features // width, width)
    near_turned, near_raw, near_squares = project_near(idx, both_cores(tok_near), gain, wq, wk, wv)
    tok_far, cot_near, near_raw = lax.optimization_barrier((tok_far, cot_near, near_raw))
    cot_far = gather_far(cot_near)
    far_turned, inverse, q, k, k_turned, v, shares, attended = attend(
        idx, both_cores(tok_far), gain, wq, wk, wv, near_raw, near_squares, rotary, where
    )

    scale = (rows * dp) ** (-0.5)
    cot_near, shares = lax.optimization_barrier((both_cores(cot_near), shares))
    near = back_near(idx, cot_near, wo)
    cot_far, near = lax.optimization_barrier((cot_far, near))
    grad, dots, *grads = back(
        idx, both_cores(cot_far), wo, near, far_turned, near_turned, q, k, k_turned, v, shares,
        inverse, rotary, scale,
    )
    grad_query, grad_key, grad_value = finish(lax.psum(tuple(grads), ("x", "z")))
    after = swap(dots)
    idx_mine, idx_other = around * cores + core, around * cores + (1 - core)
    out_sum = sum_pieces(
        *[out_terms(i, after, attended, wo, width) for i in (idx_mine, idx_other)]
    )
    output_rows = (here_tokens.astype(F32) + out_sum).astype(BF)
    in_sum = sum_pieces(
        *[input_terms(i, after, grad, dots, wq, wk, wv, width) for i in (idx_mine, idx_other)]
    )
    inverse = inverse[:, 0:1]
    mean_term = ((in_sum[rows] + in_sum[rows + 1]) / features)[:, None]
    own = y * cores + core
    own_gain = lax.dynamic_slice_in_dim(norm_gain, own * width, width, 0)
    own_scaled = here_tokens.astype(F32) * inverse
    grad_rows = here_cot.astype(F32) + inverse * (in_sum[:rows] * own_gain - own_scaled * mean_term)
    grad_rows = grad_rows.astype(BF)

    targets = panel_plan // count
    output = exchange(output_rows.reshape(dp, panel, width))[targets].reshape(rows, width)
    grad_tokens = exchange(grad_rows.reshape(dp, panel, width))[targets].reshape(rows, width)
    return output, grad_tokens, grad_query, grad_key, grad_value


def solution(mesh):
    axes = ("x", "z", "y", "core")
    split = Mesh(mesh.devices.reshape(4, 4, 4, 2), axes)
    dp, tensor = ("x", "z"), ("y", "core")
    in_specs = (
        P(dp, tensor),
        P(),
        P(dp),
        P(dp),
        P(None, tensor),
        P(None, tensor),
        P(None, tensor),
        P(tensor, None),
        P(dp, tensor),
    )
    out_specs = (
        P(dp, tensor),
        P(dp, tensor),
        P(None, tensor),
        P(None, tensor),
        P(None, tensor),
    )
    return jax.shard_map(
        per_device, mesh=split, in_specs=in_specs, out_specs=out_specs, check_vma=False
    )
```

```python
import functools

import jax
import jax.numpy as jnp
from jax import lax
from jax.experimental import pallas as pl
from jax.experimental.pallas import tpu as pltpu
from jax.sharding import Mesh
from jax.sharding import PartitionSpec as P

HD = 128
NORM_EPSILON = 1e-05
ROPE_THETA = 500000.0
SCORE_SCALE = HD ** (-0.5)
STEPS = (0, -1, 1, 2)
BF = jnp.bfloat16
F32 = jnp.float32
COSTLY = 40
VMEM_LIMIT = 56 * 1024 * 1024


def params():
    return pltpu.CompilerParams(vmem_limit_bytes=VMEM_LIMIT)


def cost(flops, moved):
    return pl.CostEstimate(flops=int(flops), bytes_accessed=int(moved), transcendentals=0)


def nn(a, b):
    return lax.dot_general(a, b, (((1,), (0,)), ((), ())), preferred_element_type=F32)


def nt(a, b):
    return lax.dot_general(a, b, (((1,), (1,)), ((), ())), preferred_element_type=F32)


def place_kernel(plan_ref, rows_ref, out_ref):
    count = rows_ref.shape[0]
    for panel in range(count):
        out_ref[plan_ref[panel] // count] = rows_ref[panel]


def place(plan, panels):
    return pl.pallas_call(
        place_kernel,
        out_shape=jax.ShapeDtypeStruct(panels.shape, panels.dtype),
        in_specs=[
            pl.BlockSpec(memory_space=pltpu.SMEM),
            pl.BlockSpec(memory_space=pltpu.VMEM),
        ],
        out_specs=pl.BlockSpec(memory_space=pltpu.VMEM),
        compiler_params=params(),
        cost_estimate=cost(0, 2 * panels.size * 2),
        name="place",
    )(plan, panels)


def place_meta_kernel(plan_ref, rows_ref, docs_ref, out_ref):
    count, rows, width = rows_ref.shape
    for panel in range(count):
        target = plan_ref[panel] // count
        slot = plan_ref[panel] % count
        out_ref[target, :, :width] = rows_ref[panel]
        doc = docs_ref[panel]
        high = (doc // 128).astype(F32)
        low = (doc % 128).astype(F32)
        lane = lax.broadcasted_iota(jnp.int32, (rows, 128), 1)
        extra = jnp.where(lane == 0, high, 0.0)
        extra = jnp.where(lane == 1, low, extra)
        extra = jnp.where(lane == 2, slot.astype(F32), extra)
        out_ref[target, :, width:] = extra.astype(BF)


def place_meta(plan, panels, docs):
    count, rows, width = panels.shape
    return pl.pallas_call(
        place_meta_kernel,
        out_shape=jax.ShapeDtypeStruct((count, rows, width + 128), panels.dtype),
        in_specs=[
            pl.BlockSpec(memory_space=pltpu.SMEM),
            pl.BlockSpec(memory_space=pltpu.VMEM),
            pl.BlockSpec(memory_space=pltpu.VMEM),
        ],
        out_specs=pl.BlockSpec(memory_space=pltpu.VMEM),
        compiler_params=params(),
        cost_estimate=cost(0, 2 * panels.size * 2),
        name="place_meta",
    )(plan, panels, docs.reshape(count, rows, 1))


NEAR = tuple((step, other) for step in range(3) for other in (0, 1))
FAR = ((3, 0), (3, 1))

SMEM_SPEC = pl.BlockSpec(memory_space=pltpu.SMEM)
HBM_SPEC = pl.BlockSpec(memory_space=pltpu.HBM)


def whole(shape):
    return pl.BlockSpec(tuple(shape), lambda j: (0,) * len(shape))


def part_of(idx_ref, step, other, width):
    at = idx_ref[step] + (idx_ref[4] if not other else 1 - idx_ref[4])
    return pl.ds(pl.multiple_of(at * width, width), width)


class Copies:
    def __init__(self, sems):
        self.sems = sems
        self.count = 0

    def start(self, source, target):
        copy = pltpu.make_async_copy(source, target, self.sems.at[self.count])
        self.count += 1
        copy.start()
        return copy


def fetch_near(copies, pieces, buffer):
    return [[copies.start(pieces[3 * o + s], buffer.at[n])] for n, (s, o) in enumerate(NEAR)]


def fetch_far(copies, pieces, buffer):
    half = buffer.shape[1] // 2
    return [
        [
            copies.start(pieces[2 * n], buffer.at[n, :half]),
            copies.start(pieces[2 * n + 1], buffer.at[n, half:]),
        ]
        for n in range(2)
    ]


def project_steps(
    idx_ref, places, arrivals, copies, buffer, gain_ref, weights, held, stage, turned_ref, raw_ref, fresh
):
    rows, width = buffer.shape[1:]
    for n, (step, other) in enumerate(places):
        part = part_of(idx_ref, step, other, width)
        for ref, target in zip(weights, held):
            arrivals[n].append(copies.start(ref.at[part], target.at[n]))
    squares = jnp.zeros((rows, 1), F32)
    sent = []
    for n, (step, other) in enumerate(places):
        core = idx_ref[4] if not other else 1 - idx_ref[4]
        for copy in arrivals[n]:
            copy.wait()
        wide = buffer[n].astype(F32)
        squares += jnp.sum(wide * wide, axis=1, keepdims=True)
        gained = (wide * gain_ref[pl.ds(idx_ref[step] + core, 1)]).astype(BF)
        stage[n] = gained.T
        here = pl.ds(pl.multiple_of(core * width, width), width)
        sent.append(copies.start(stage.at[n], turned_ref.at[step % 3, here]))
        at = 0
        for target in held:
            cols = slice(at, at + target.shape[2])
            at += target.shape[2]
            if fresh and n == 0:
                raw_ref[:, cols] = nn(gained, target[n])
            else:
                raw_ref[:, cols] += nn(gained, target[n])
    return squares, sent


def project_near_kernel(*refs):
    idx_ref, pieces = refs[0], refs[1:7]
    gain_ref, wq, wk, wv, turned_ref, raw_ref, squares_ref, buffer, stage, hq, hk, hv, sems = refs[7:]
    copies = Copies(sems)
    arrivals = fetch_near(copies, pieces, buffer)
    squares, sent = project_steps(
        idx_ref, NEAR, arrivals, copies, buffer, gain_ref, (wq, wk, wv), (hq, hk, hv),
        stage, turned_ref, raw_ref, True,
    )
    squares_ref[...] = jnp.broadcast_to(squares, squares_ref.shape)
    for copy in sent:
        copy.wait()


def project_near(idx, pieces, gain, wq, wk, wv):
    rows, width = pieces[0].shape
    weights = (wq, wk, wv)
    cols = sum(w.shape[1] for w in weights)
    shapes = [
        jax.ShapeDtypeStruct((3, 2 * width, rows), BF),
        jax.ShapeDtypeStruct((rows, cols), F32),
        jax.ShapeDtypeStruct((rows, HD), F32),
    ]
    return pl.pallas_call(
        project_near_kernel,
        grid=(1,),
        in_specs=[SMEM_SPEC] + [HBM_SPEC] * 6 + [whole(gain.shape)] + [HBM_SPEC] * 3,
        out_specs=[HBM_SPEC] + [whole(a.shape) for a in shapes[1:]],
        out_shape=shapes,
        scratch_shapes=[pltpu.VMEM((6, rows, width), BF), pltpu.VMEM((6, width, rows), BF)]
        + [pltpu.VMEM((6, width, w.shape[1]), BF) for w in weights]
        + [pltpu.SemaphoreType.DMA((30,))],
        compiler_params=params(),
        cost_estimate=cost(12 * rows * width * cols, 12 * width * (2 * rows + cols)),
        name="project_near",
    )(idx, *pieces, gain, *weights)


def attend_kernel(*refs):
    idx_ref, pieces = refs[0], refs[1:5]
    (
        gain_ref, wq, wk, wv, near_raw_ref, near_squares_ref, rotary_ref, where_ref,
        turned_ref, inverse_ref, q_ref, k_ref, k_turned_ref, v_ref, shares_ref, attended_ref,
        raw_ref, shares_stage, buffer, stage, hq, hk, hv, sems,
    ) = refs[5:]
    rows, width = buffer.shape[1:]
    copies = Copies(sems)
    arrivals = fetch_far(copies, pieces, buffer)
    raw_ref[...] = near_raw_ref[...]
    squares, sent = project_steps(
        idx_ref, FAR, arrivals, copies, buffer, gain_ref, (wq, wk, wv), (hq, hk, hv),
        stage, turned_ref, raw_ref, False,
    )
    features = wq.shape[0]
    inverse = lax.rsqrt((squares + near_squares_ref[:, 0:1]) / features + NORM_EPSILON)
    inverse_ref[...] = jnp.broadcast_to(inverse, inverse_ref.shape)

    cosine = rotary_ref[0] * inverse
    sine = rotary_ref[1] * inverse
    heads = shares_stage.shape[0]

    def rotate(u):
        return u * cosine + pltpu.roll(u, HD // 2, 1) * sine

    key = rotate(raw_ref[:, heads * HD : (heads + 1) * HD])
    k_ref[...] = key.astype(BF)
    k_turned_ref[...] = key.T.astype(BF)
    value = raw_ref[:, (heads + 1) * HD :] * inverse
    v_ref[...] = value.astype(BF)
    v_turned = value.T.astype(BF)
    down = where_ref[...].T
    doc_s = down[:, 0:1]
    at_s = down[:, 1:2]
    doc_g = where_ref[0:1, :]
    at_g = where_ref[1:2, :]
    allowed = (doc_s == doc_g) & (at_s <= at_g)
    for h in range(heads):
        cols = slice(h * HD, (h + 1) * HD)
        query = rotate(raw_ref[:, cols]).astype(BF)
        q_ref[:, cols] = query
        scores = nt(k_ref[...], query) * SCORE_SCALE
        weights = jnp.where(allowed, jnp.exp(scores), 0.0)
        total = jnp.sum(weights, axis=0, keepdims=True)
        shares = (weights * (1.0 / total)).astype(BF)
        shares_stage[h] = shares
        sent.append(copies.start(shares_stage.at[h], shares_ref.at[h]))
        attended_ref[:, cols] = nn(v_turned, shares).T.astype(BF)
    for copy in sent:
        copy.wait()


def attend(idx, pieces, gain, wq, wk, wv, near_raw, near_squares, rotary, where):
    width = pieces[0].shape[1]
    rows, cols = near_raw.shape
    weights = (wq, wk, wv)
    heads = wq.shape[1] // HD
    shapes = [
        jax.ShapeDtypeStruct((1, 2 * width, rows), BF),
        jax.ShapeDtypeStruct((rows, HD), F32),
        jax.ShapeDtypeStruct((rows, heads * HD), BF),
        jax.ShapeDtypeStruct((rows, HD), BF),
        jax.ShapeDtypeStruct((HD, rows), BF),
        jax.ShapeDtypeStruct((rows, HD), BF),
        jax.ShapeDtypeStruct((heads, rows, rows), BF),
        jax.ShapeDtypeStruct((rows, heads * HD), BF),
    ]
    extras = (near_raw, near_squares, rotary, where)
    out_specs = [whole(a.shape) for a in shapes]
    out_specs[0] = out_specs[6] = HBM_SPEC
    return pl.pallas_call(
        attend_kernel,
        grid=(1,),
        in_specs=[SMEM_SPEC] + [HBM_SPEC] * 4 + [whole(gain.shape)] + [HBM_SPEC] * 3
        + [whole(a.shape) for a in extras],
        out_specs=out_specs,
        out_shape=shapes,
        scratch_shapes=[
            pltpu.VMEM((rows, cols), F32),
            pltpu.VMEM((heads, rows, rows), BF),
            pltpu.VMEM((2, rows, width), BF),
            pltpu.VMEM((2, width, rows), BF),
        ]
        + [pltpu.VMEM((2, width, w.shape[1]), BF) for w in weights]
        + [pltpu.SemaphoreType.DMA((16,))],
        compiler_params=params(),
        cost_estimate=cost(
            4 * rows * width * cols + 4 * heads * rows * rows * HD, 4 * width * (2 * rows + cols)
        ),
        name="attend",
    )(idx, *pieces, gain, *weights, *extras)


def back_near_kernel(*refs):
    idx_ref, pieces = refs[0], refs[1:7]
    wo_ref, acc_ref, buffer, held, sems = refs[7:]
    width = buffer.shape[2]
    copies = Copies(sems)
    arrivals = fetch_near(copies, pieces, buffer)
    for n, (step, other) in enumerate(NEAR):
        part = part_of(idx_ref, step, other, width)
        arrivals[n].append(copies.start(wo_ref.at[:, part], held.at[n]))
    for n in range(len(NEAR)):
        for copy in arrivals[n]:
            copy.wait()
        if n == 0:
            acc_ref[...] = nt(buffer[n], held[n])
        else:
            acc_ref[...] += nt(buffer[n], held[n])


def back_near(idx, pieces, wo):
    rows, width = pieces[0].shape
    cols = wo.shape[0]
    return pl.pallas_call(
        back_near_kernel,
        grid=(1,),
        in_specs=[SMEM_SPEC] + [HBM_SPEC] * 7,
        out_specs=whole((rows, cols)),
        out_shape=jax.ShapeDtypeStruct((rows, cols), F32),
        scratch_shapes=[
            pltpu.VMEM((6, rows, width), BF),
            pltpu.VMEM((6, cols, width), BF),
            pltpu.SemaphoreType.DMA((12,)),
        ],
        compiler_params=params(),
        cost_estimate=cost(12 * rows * width * cols, 12 * width * (rows + cols)),
        name="back_near",
    )(idx, *pieces, wo)


def back_kernel(*refs, scale):
    idx_ref, pieces = refs[0], refs[1:5]
    inputs = refs[5:16]
    grad_ref, dots_ref, gq_ref, gkv_ref = refs[16:20]
    buffer, held, scaled_ref, gq, gkv, sems = refs[20:26]
    targets = refs[26:]
    wo_ref, near_ref, far_turned, near_turned = inputs[:4]
    copies = Copies(sems)
    arrivals = fetch_far(copies, pieces, buffer)
    rows, width = buffer.shape[1:]
    for n, (step, other) in enumerate(FAR):
        part = part_of(idx_ref, step, other, width)
        arrivals[n].append(copies.start(wo_ref.at[:, part], held.at[n]))
    acc_ref, turned_ref = targets[:2]
    acc_copy = copies.start(near_ref, acc_ref)
    loads = [copies.start(source, target) for source, target in zip(inputs[4:], targets[2:])]
    tall = 2 * width
    turned_loads = [
        copies.start(near_turned.at[n], turned_ref.at[n * tall : (n + 1) * tall]) for n in range(3)
    ] + [copies.start(far_turned.at[0], turned_ref.at[3 * tall :])]
    q_ref, k_ref, k_turned_ref, v_ref, shares_ref, inverse_ref, rotary_ref = targets[2:]
    acc_copy.wait()
    for n in range(2):
        for copy in arrivals[n]:
            copy.wait()
        acc_ref[...] += nt(buffer[n], held[n])
    for copy in loads:
        copy.wait()

    cosine = rotary_ref[0]
    sine = rotary_ref[1]
    heads = shares_ref.shape[0]
    factor = inverse_ref[:, 0:1] * scale

    def rotate_back(u):
        return u * cosine - pltpu.roll(u, HD // 2, 1) * sine

    products = jnp.zeros((rows, HD), F32)

    def emit(at, grad):
        cols = slice(at * HD, (at + 1) * HD)
        grad_ref[:, cols] = grad.astype(BF)
        scaled_ref[:, cols] = (grad * factor).astype(BF)

    key_grad = jnp.zeros((rows, HD), F32)
    value_grad = jnp.zeros((rows, HD), F32)
    for h in range(heads):
        cols = slice(h * HD, (h + 1) * HD)
        grad_attended = acc_ref[:, cols].astype(BF)
        shares = shares_ref[h]
        share_grad = nt(v_ref[...], grad_attended)
        wide = shares.astype(F32)
        row_dot = jnp.sum(share_grad * wide, axis=0, keepdims=True)
        dscore = (wide * (share_grad - row_dot) * SCORE_SCALE).astype(BF)
        key_grad += nn(dscore, q_ref[:, cols])
        value_grad += nn(shares, grad_attended)
        query_grad = nn(k_turned_ref[...], dscore).T
        products += query_grad * q_ref[:, cols].astype(F32)
        emit(h, rotate_back(query_grad))
    products += key_grad * k_ref[...].astype(F32) + value_grad * v_ref[...].astype(F32)
    emit(heads, rotate_back(key_grad))
    emit(heads + 1, value_grad)
    for copy in turned_loads:
        copy.wait()
    outs = []
    q_cols = gq.shape[2]
    share = gkv.shape[2]
    for j in range(4):
        gq[j] = nn(turned_ref[j * tall : (j + 1) * tall], scaled_ref[:, :q_cols]).astype(BF)
        start = pl.multiple_of(idx_ref[j] * width, tall)
        outs.append(copies.start(gq.at[j], gq_ref.at[pl.ds(start, tall)]))
    for first in range(4):
        for n in range(4):
            at = (idx_ref[5 + first] * 4 + idx_ref[9 + n]) * share
            block = turned_ref[pl.ds(pl.multiple_of(at, share), share)]
            gkv[first, n] = nn(block, scaled_ref[:, q_cols:]).astype(BF)
        outs.append(copies.start(gkv.at[first], gkv_ref.at[first]))
    dots_ref[...] = lax.dot_general(
        jnp.ones((8, HD), F32), products, (((1,), (1,)), ((), ())),
        preferred_element_type=F32, precision=lax.Precision.HIGHEST,
    )
    for copy in outs:
        copy.wait()


def back(idx, pieces, wo, near, far_turned, near_turned, q, k, k_turned, v, shares, inverse, rotary, scale):
    width = pieces[0].shape[1]
    cols, features = wo.shape
    rows = near.shape[0]
    kv_cols = k.shape[1]
    grad_shape = (rows, cols + 2 * kv_cols)
    inputs = (wo, near, far_turned, near_turned, q, k, k_turned, v, shares, inverse, rotary)
    loaded = (q, k, k_turned, v, shares, inverse, rotary)
    weight_shapes = [
        jax.ShapeDtypeStruct((features, cols), BF),
        jax.ShapeDtypeStruct((4, 4, features // 16, 2 * kv_cols), BF),
    ]
    shapes = [jax.ShapeDtypeStruct(grad_shape, BF), jax.ShapeDtypeStruct((8, rows), F32)]
    return pl.pallas_call(
        functools.partial(back_kernel, scale=scale),
        grid=(1,),
        in_specs=[SMEM_SPEC] + [HBM_SPEC] * 15,
        out_specs=[whole(a.shape) for a in shapes] + [HBM_SPEC] * 2,
        out_shape=shapes + weight_shapes,
        scratch_shapes=[
            pltpu.VMEM((2, rows, width), BF),
            pltpu.VMEM((2, cols, width), BF),
            pltpu.VMEM(grad_shape, BF),
        ]
        + [
            pltpu.VMEM((4, features // 4, cols), BF),
            pltpu.VMEM(weight_shapes[1].shape, BF),
            pltpu.SemaphoreType.DMA((40,)),
            pltpu.VMEM(near.shape, F32),
            pltpu.VMEM((features, rows), BF),
        ]
        + [pltpu.VMEM(a.shape, a.dtype) for a in loaded],
        compiler_params=params(),
        cost_estimate=cost(
            4 * rows * width * cols + 8 * cols * rows * rows + 2 * rows * features * (cols + 2 * kv_cols),
            2 * features * (rows + cols),
        ),
        name="back",
    )(idx, *pieces, *inputs)


def sum_wide(chunks, axis):
    total = chunks[0].astype(F32)
    for n, step in ((1, -1), (2, 1), (3, 2)):
        total = total + shift(chunks[n], step, axis).astype(F32)
    return total


def sum_direct(chunks, axis):
    return sum_wide(chunks, axis).astype(BF)


def spread_direct(piece, axis):
    return [piece, shift(piece, 1, axis), shift(piece, -1, axis), shift(piece, 2, axis)]


def assemble_kernel(*refs):
    idx_ref, pieces, k_ref, v_ref = refs[0], refs[1:5], refs[5], refs[6]
    share = pieces[0].shape[1]
    kv = k_ref.shape[1]
    for first in range(4):
        for n in range(4):
            owner = idx_ref[5 + first] * 4 + idx_ref[9 + n]
            row = idx_ref[owner // 4] * 2 * share + owner % 4 * share
            rows = pl.ds(pl.multiple_of(row, share), share)
            k_ref[rows] = pieces[first][n, :, :kv]
            v_ref[rows] = pieces[first][n, :, kv:]


def assemble(idx, pieces, features, kv):
    return pl.pallas_call(
        assemble_kernel,
        grid=(1,),
        in_specs=[SMEM_SPEC] + [whole(a.shape) for a in pieces],
        out_specs=[whole((features, kv))] * 2,
        out_shape=[jax.ShapeDtypeStruct((features, kv), BF)] * 2,
        compiler_params=params(),
        cost_estimate=cost(0, 8 * features * kv),
        name="assemble",
    )(idx, *pieces)


def finish_kernel(*refs):
    refs[-1][...] = refs[-2][...]


def finish(after, array):
    parts = 4
    spec = pl.BlockSpec((array.shape[0] // parts, array.shape[1]), lambda j: (j, 0))
    return pl.pallas_call(
        finish_kernel,
        grid=(parts,),
        in_specs=[HBM_SPEC] * len(after) + [spec],
        out_specs=spec,
        out_shape=jax.ShapeDtypeStruct(array.shape, array.dtype),
        compiler_params=params(),
        cost_estimate=cost(0, 4 * array.size),
        name="finish",
    )(*after, array)


def term_kernel(
    idx_ref, _, attended_ref, wo_ref, grad_ref, dots_ref, wq_ref, wk_ref, wv_ref, out_ref
):
    q_cols = wq_ref.shape[1]
    kv_cols = wk_ref.shape[1]
    rows = grad_ref.shape[0]
    out_ref[0, :rows] = nn(attended_ref[...], wo_ref[...]).astype(BF)
    dots = dots_ref[0:1, :]
    high = dots.astype(BF).astype(F32)
    line = lax.broadcasted_iota(jnp.int32, (16, dots.shape[1]), 0)
    extra = jnp.where(line == 0, high, jnp.where(line == 1, dots - high, 0.0))
    term = nt(grad_ref[:, :q_cols], wq_ref[...])
    term += nt(grad_ref[:, q_cols : q_cols + kv_cols], wk_ref[...])
    term += nt(grad_ref[:, q_cols + kv_cols :], wv_ref[...])
    out_ref[0, rows : 2 * rows] = term.astype(BF)
    out_ref[0, 2 * rows :] = extra.astype(BF)


def terms(idx, after, attended, wo, grad, dots, wq, wk, wv, width):
    rows, cols = grad.shape
    heads = attended.shape[1]
    parts = 4
    grid_spec = pltpu.PrefetchScalarGridSpec(
        num_scalar_prefetch=1,
        grid=(parts,),
        in_specs=[
            HBM_SPEC,
            pl.BlockSpec((rows, heads), lambda j, idx: (0, 0)),
            pl.BlockSpec((heads, width), lambda j, idx: (0, idx[j])),
            pl.BlockSpec((rows, cols), lambda j, idx: (0, 0)),
            pl.BlockSpec(dots.shape, lambda j, idx: (0, 0)),
        ]
        + [pl.BlockSpec((width, w.shape[1]), lambda j, idx: (idx[j], 0)) for w in (wq, wk, wv)],
        out_specs=pl.BlockSpec((1, 2 * rows + 16, width), lambda j, idx: (j, 0, 0)),
    )
    return pl.pallas_call(
        term_kernel,
        grid_spec=grid_spec,
        out_shape=jax.ShapeDtypeStruct((parts, 2 * rows + 16, width), BF),
        compiler_params=params(),
        cost_estimate=cost(
            COSTLY * parts * rows * (cols + heads) * width, COSTLY * parts * width * (rows + cols)
        ),
        name="terms",
    )(idx, after, attended, wo, grad, dots, wq, wk, wv)


def shift(array, step, axis="y"):
    size = lax.axis_size(axis)
    return lax.ppermute(array, axis, [(i, (i + step) % size) for i in range(size)])


def swap(array):
    return lax.ppermute(array, "core", [(0, 1), (1, 0)])


def gather_near(piece):
    return piece, shift(piece, 1), shift(piece, -1)


def gather_far(near):
    _, below, above = near
    half = below.shape[0] // 2
    return shift(below[:half], 1), shift(above[half:], -1)


def both_cores(pieces):
    return tuple(pieces) + tuple(swap(a) for a in pieces)


def add_cores(mine_terms, other_terms):
    return (mine_terms.astype(F32) + swap(other_terms).astype(F32)).astype(BF)


def exchange(panels):
    return lax.all_to_all(panels, ("x", "z"), split_axis=0, concat_axis=0, tiled=True)


def per_device(
    tokens, norm_gain, doc_ids, panel_plan, wq, wk, wv, wo, cotangent,
):
    y, core = lax.axis_index("y"), lax.axis_index("core")
    ys, cores = lax.axis_size("y"), lax.axis_size("core")
    block = lax.axis_index("x") * lax.axis_size("z") + lax.axis_index("z")
    dp = lax.axis_size("x") * lax.axis_size("z")
    count = panel_plan.shape[0]
    rows, width = tokens.shape
    panel = rows // count
    features = norm_gain.shape[0]

    around = (y + jnp.array(STEPS, jnp.int32)) % ys
    steps = jnp.array(STEPS, jnp.int32)
    idx = jnp.concatenate(
        [around * cores, core[None], (lax.axis_index("x") + steps) % 4, (lax.axis_index("z") + steps) % 4]
    )

    here_tokens = exchange(place(panel_plan, tokens.reshape(count, panel, width))).reshape(rows, width)
    arrived = exchange(
        place_meta(panel_plan, cotangent.reshape(count, panel, width), doc_ids.reshape(count, panel))
    )
    here_cot = arrived[:, :, :width].reshape(rows, width)
    meta = arrived[:, :, width : width + 3].reshape(rows, 3).astype(jnp.int32)
    docs = meta[:, 0] * 128 + meta[:, 1]
    at = block * rows + meta[:, 2] * panel + jnp.arange(rows, dtype=jnp.int32) % panel
    positions = (at - docs).astype(F32)
    frequency = ROPE_THETA ** (-2.0 * jnp.arange(HD // 2, dtype=F32) / HD)
    angles = positions[:, None] * frequency[None, :]
    cosine, sine = jnp.cos(angles), jnp.sin(angles)
    rotary = jnp.stack(
        [jnp.concatenate([cosine, cosine], axis=1), jnp.concatenate([-sine, sine], axis=1)]
    )
    where = jnp.pad(jnp.stack([docs, at]).astype(F32), ((0, 6), (0, 0)))

    tok_near = gather_near(here_tokens)
    cot_near = gather_near(here_cot)
    tok_far = gather_far(tok_near)
    gain = norm_gain.reshape(features // width, width)
    near_turned, near_raw, near_squares = project_near(idx, both_cores(tok_near), gain, wq, wk, wv)
    tok_far, cot_near, near_raw = lax.optimization_barrier((tok_far, cot_near, near_raw))
    cot_far = gather_far(cot_near)
    far_turned, inverse, q, k, k_turned, v, shares, attended = attend(
        idx, both_cores(tok_far), gain, wq, wk, wv, near_raw, near_squares, rotary, where
    )

    scale = (rows * dp) ** (-0.5)
    cot_near, shares = lax.optimization_barrier((both_cores(cot_near), shares))
    near = back_near(idx, cot_near, wo)
    cot_far, near = lax.optimization_barrier((cot_far, near))
    grad, dots, grad_q, grad_kv = back(
        idx, both_cores(cot_far), wo, near, far_turned, near_turned, q, k, k_turned, v, shares,
        inverse, rotary, scale,
    )
    grad_query = lax.psum(grad_q, ("x", "z"))
    tie = lax.optimization_barrier

    after = swap(dots)
    grad_kv = sum_direct(grad_kv, "x")
    idx_mine, idx_other = around * cores + core, around * cores + (1 - core)
    sums = add_cores(
        *[terms(i, after, attended, wo, grad, dots, wq, wk, wv, width) for i in (idx_mine, idx_other)]
    )
    grad_kv, sums = tie((grad_kv, sums))
    grad_kv = sum_direct(grad_kv, "z")
    sums = sum_wide(sums, "y")
    grad_kv, sums = tie((grad_kv, sums))
    grad_kv = jnp.stack(spread_direct(grad_kv, "z"))
    grad_key, grad_value = assemble(idx, spread_direct(grad_kv, "x"), features, wk.shape[1])

    output_rows = (here_tokens.astype(F32) + sums[:rows]).astype(BF)
    in_sum = sums[rows:]
    inverse = inverse[:, 0:1]
    mean_term = ((in_sum[rows] + in_sum[rows + 1]) / features)[:, None]
    own = y * cores + core
    own_gain = lax.dynamic_slice_in_dim(norm_gain, own * width, width, 0)
    own_scaled = here_tokens.astype(F32) * inverse
    grad_rows = here_cot.astype(F32) + inverse * (in_sum[:rows] * own_gain - own_scaled * mean_term)
    grad_rows = grad_rows.astype(BF)

    targets = panel_plan // count
    both = jnp.concatenate([output_rows, grad_rows], axis=1).reshape(dp, panel, 2 * width)
    both = exchange(both)[targets].reshape(rows, 2 * width)
    output, grad_tokens = both[:, :width], both[:, width:]
    grad_query = finish((output, grad_tokens, grad_key), grad_query)
    return output, grad_tokens, grad_query, grad_key, grad_value


def solution(mesh):
    axes = ("x", "z", "y", "core")
    split = Mesh(mesh.devices.reshape(4, 4, 4, 2), axes)
    dp, tensor = ("x", "z"), ("y", "core")
    in_specs = (
        P(dp, tensor),
        P(),
        P(dp),
        P(dp),
        P(None, tensor),
        P(None, tensor),
        P(None, tensor),
        P(tensor, None),
        P(dp, tensor),
    )
    out_specs = (
        P(dp, tensor),
        P(dp, tensor),
        P(None, tensor),
        P(None, tensor),
        P(None, tensor),
    )
    return jax.shard_map(
        per_device, mesh=split, in_specs=in_specs, out_specs=out_specs, check_vma=False
    )
```

```python
import functools

import jax
import jax.numpy as jnp
from jax import lax
from jax.experimental import pallas as pl
from jax.experimental.pallas import tpu as pltpu
from jax.sharding import Mesh
from jax.sharding import PartitionSpec as P

HD = 128
NORM_EPSILON = 1e-05
ROPE_THETA = 500000.0
SCORE_SCALE = HD ** (-0.5)
STEPS = (0, -1, 1, 2)
BF = jnp.bfloat16
F32 = jnp.float32
VMEM_LIMIT = 56 * 1024 * 1024


def params():
    return pltpu.CompilerParams(vmem_limit_bytes=VMEM_LIMIT)


def cost(flops, moved):
    return pl.CostEstimate(flops=int(flops), bytes_accessed=int(moved), transcendentals=0)


def nn(a, b):
    return lax.dot_general(a, b, (((1,), (0,)), ((), ())), preferred_element_type=F32)


def nt(a, b):
    return lax.dot_general(a, b, (((1,), (1,)), ((), ())), preferred_element_type=F32)


def place_kernel(plan_ref, rows_ref, out_ref):
    count = rows_ref.shape[0]
    for panel in range(count):
        out_ref[plan_ref[panel] // count] = rows_ref[panel]


def place(plan, panels):
    return pl.pallas_call(
        place_kernel,
        out_shape=jax.ShapeDtypeStruct(panels.shape, panels.dtype),
        in_specs=[
            pl.BlockSpec(memory_space=pltpu.SMEM),
            pl.BlockSpec(memory_space=pltpu.VMEM),
        ],
        out_specs=pl.BlockSpec(memory_space=pltpu.VMEM),
        compiler_params=params(),
        cost_estimate=cost(0, 2 * panels.size * 2),
        name="place",
    )(plan, panels)


def place_meta_kernel(plan_ref, _, rows_ref, docs_ref, out_ref):
    count, rows, width = rows_ref.shape
    for panel in range(count):
        target = plan_ref[panel] // count
        slot = plan_ref[panel] % count
        out_ref[target, :, :width] = rows_ref[panel]
        doc = docs_ref[panel]
        high = (doc // 128).astype(F32)
        low = (doc % 128).astype(F32)
        lane = lax.broadcasted_iota(jnp.int32, (rows, 128), 1)
        extra = jnp.where(lane == 0, high, 0.0)
        extra = jnp.where(lane == 1, low, extra)
        extra = jnp.where(lane == 2, slot.astype(F32), extra)
        out_ref[target, :, width:] = extra.astype(BF)


def place_meta(plan, after, panels, docs):
    count, rows, width = panels.shape
    return pl.pallas_call(
        place_meta_kernel,
        out_shape=jax.ShapeDtypeStruct((count, rows, width + 128), panels.dtype),
        in_specs=[
            pl.BlockSpec(memory_space=pltpu.SMEM),
            pl.BlockSpec(memory_space=pltpu.HBM),
            pl.BlockSpec(memory_space=pltpu.VMEM),
            pl.BlockSpec(memory_space=pltpu.VMEM),
        ],
        out_specs=pl.BlockSpec(memory_space=pltpu.VMEM),
        compiler_params=params(),
        cost_estimate=cost(0, 2 * panels.size * 2),
        name="place_meta",
    )(plan, after, panels, docs.reshape(count, rows, 1))


NEAR = tuple((step, other) for step in range(3) for other in (0, 1))
FAR = ((3, 0), (3, 1))

SMEM_SPEC = pl.BlockSpec(memory_space=pltpu.SMEM)
HBM_SPEC = pl.BlockSpec(memory_space=pltpu.HBM)


def whole(shape):
    return pl.BlockSpec(tuple(shape), lambda j: (0,) * len(shape))


def part_of(idx_ref, step, other, width):
    at = idx_ref[step] + (idx_ref[4] if not other else 1 - idx_ref[4])
    return pl.ds(pl.multiple_of(at * width, width), width)


class Copies:
    def __init__(self, sems):
        self.sems = sems
        self.count = 0

    def start(self, source, target):
        copy = pltpu.make_async_copy(source, target, self.sems.at[self.count])
        self.count += 1
        copy.start()
        return copy


def fetch_near(copies, pieces, buffer):
    return [[copies.start(pieces[3 * o + s], buffer.at[n])] for n, (s, o) in enumerate(NEAR)]


def fetch_far(copies, pieces, buffer):
    half = buffer.shape[1] // 2
    return [
        [
            copies.start(pieces[2 * n], buffer.at[n, :half]),
            copies.start(pieces[2 * n + 1], buffer.at[n, half:]),
        ]
        for n in range(2)
    ]


def project_steps(
    idx_ref, places, arrivals, copies, buffer, gain_ref, weights, held, stage, turned_ref, raw_ref, fresh
):
    rows, width = buffer.shape[1:]
    for n, (step, other) in enumerate(places):
        part = part_of(idx_ref, step, other, width)
        for ref, target in zip(weights, held):
            arrivals[n].append(copies.start(ref.at[part], target.at[n]))
    squares = jnp.zeros((rows, 1), F32)
    sent = []
    for n, (step, other) in enumerate(places):
        core = idx_ref[4] if not other else 1 - idx_ref[4]
        for copy in arrivals[n]:
            copy.wait()
        wide = buffer[n].astype(F32)
        squares += jnp.sum(wide * wide, axis=1, keepdims=True)
        gained = (wide * gain_ref[pl.ds(idx_ref[step] + core, 1)]).astype(BF)
        stage[n] = gained.T
        here = pl.ds(pl.multiple_of(core * width, width), width)
        sent.append(copies.start(stage.at[n], turned_ref.at[step % 3, here]))
        at = 0
        for target in held:
            cols = slice(at, at + target.shape[2])
            at += target.shape[2]
            if fresh and n == 0:
                raw_ref[:, cols] = nn(gained, target[n])
            else:
                raw_ref[:, cols] += nn(gained, target[n])
    return squares, sent


def project_near_kernel(*refs):
    idx_ref, pieces = refs[0], refs[1:7]
    gain_ref, wq, wk, wv, turned_ref, raw_ref, squares_ref, buffer, stage, hq, hk, hv, sems = refs[7:]
    copies = Copies(sems)
    arrivals = fetch_near(copies, pieces, buffer)
    squares, sent = project_steps(
        idx_ref, NEAR, arrivals, copies, buffer, gain_ref, (wq, wk, wv), (hq, hk, hv),
        stage, turned_ref, raw_ref, True,
    )
    squares_ref[...] = jnp.broadcast_to(squares, squares_ref.shape)
    for copy in sent:
        copy.wait()


def project_near(idx, pieces, gain, wq, wk, wv):
    rows, width = pieces[0].shape
    weights = (wq, wk, wv)
    cols = sum(w.shape[1] for w in weights)
    shapes = [
        jax.ShapeDtypeStruct((3, 2 * width, rows), BF),
        jax.ShapeDtypeStruct((rows, cols), F32),
        jax.ShapeDtypeStruct((rows, HD), F32),
    ]
    return pl.pallas_call(
        project_near_kernel,
        grid=(1,),
        in_specs=[SMEM_SPEC] + [HBM_SPEC] * 6 + [whole(gain.shape)] + [HBM_SPEC] * 3,
        out_specs=[HBM_SPEC] + [whole(a.shape) for a in shapes[1:]],
        out_shape=shapes,
        scratch_shapes=[pltpu.VMEM((6, rows, width), BF), pltpu.VMEM((6, width, rows), BF)]
        + [pltpu.VMEM((6, width, w.shape[1]), BF) for w in weights]
        + [pltpu.SemaphoreType.DMA((30,))],
        compiler_params=params(),
        cost_estimate=cost(12 * rows * width * cols, 12 * width * (2 * rows + cols)),
        name="project_near",
    )(idx, *pieces, gain, *weights)


def attend_kernel(*refs):
    idx_ref, pieces = refs[0], refs[1:5]
    (
        gain_ref, wq, wk, wv, near_raw_ref, near_squares_ref, rotary_ref, where_ref,
        turned_ref, inverse_ref, q_ref, k_ref, k_turned_ref, v_ref, shares_ref, attended_ref,
        raw_ref, shares_stage, buffer, stage, hq, hk, hv, sems,
    ) = refs[5:]
    rows, width = buffer.shape[1:]
    copies = Copies(sems)
    arrivals = fetch_far(copies, pieces, buffer)
    raw_ref[...] = near_raw_ref[...]
    squares, sent = project_steps(
        idx_ref, FAR, arrivals, copies, buffer, gain_ref, (wq, wk, wv), (hq, hk, hv),
        stage, turned_ref, raw_ref, False,
    )
    features = wq.shape[0]
    inverse = lax.rsqrt((squares + near_squares_ref[:, 0:1]) / features + NORM_EPSILON)
    inverse_ref[...] = jnp.broadcast_to(inverse, inverse_ref.shape)

    cosine = rotary_ref[0] * inverse
    sine = rotary_ref[1] * inverse
    heads = shares_stage.shape[0]

    def rotate(u):
        return u * cosine + pltpu.roll(u, HD // 2, 1) * sine

    key = rotate(raw_ref[:, heads * HD : (heads + 1) * HD])
    k_ref[...] = key.astype(BF)
    k_turned_ref[...] = key.T.astype(BF)
    value = raw_ref[:, (heads + 1) * HD :] * inverse
    v_ref[...] = value.astype(BF)
    v_turned = value.T.astype(BF)
    down = where_ref[...].T
    doc_s = down[:, 0:1]
    at_s = down[:, 1:2]
    doc_g = where_ref[0:1, :]
    at_g = where_ref[1:2, :]
    allowed = (doc_s == doc_g) & (at_s <= at_g)
    for h in range(heads):
        cols = slice(h * HD, (h + 1) * HD)
        query = rotate(raw_ref[:, cols]).astype(BF)
        q_ref[:, cols] = query
        scores = nt(k_ref[...], query) * SCORE_SCALE
        weights = jnp.where(allowed, jnp.exp(scores), 0.0)
        total = jnp.sum(weights, axis=0, keepdims=True)
        shares = (weights * (1.0 / total)).astype(BF)
        shares_stage[h] = shares
        sent.append(copies.start(shares_stage.at[h], shares_ref.at[h]))
        attended_ref[:, cols] = nn(v_turned, shares).T.astype(BF)
    for copy in sent:
        copy.wait()


def attend(idx, pieces, gain, wq, wk, wv, near_raw, near_squares, rotary, where):
    width = pieces[0].shape[1]
    rows, cols = near_raw.shape
    weights = (wq, wk, wv)
    heads = wq.shape[1] // HD
    shapes = [
        jax.ShapeDtypeStruct((1, 2 * width, rows), BF),
        jax.ShapeDtypeStruct((rows, HD), F32),
        jax.ShapeDtypeStruct((rows, heads * HD), BF),
        jax.ShapeDtypeStruct((rows, HD), BF),
        jax.ShapeDtypeStruct((HD, rows), BF),
        jax.ShapeDtypeStruct((rows, HD), BF),
        jax.ShapeDtypeStruct((heads, rows, rows), BF),
        jax.ShapeDtypeStruct((rows, heads * HD), BF),
    ]
    extras = (near_raw, near_squares, rotary, where)
    out_specs = [whole(a.shape) for a in shapes]
    out_specs[0] = out_specs[6] = HBM_SPEC
    return pl.pallas_call(
        attend_kernel,
        grid=(1,),
        in_specs=[SMEM_SPEC] + [HBM_SPEC] * 4 + [whole(gain.shape)] + [HBM_SPEC] * 3
        + [whole(a.shape) for a in extras],
        out_specs=out_specs,
        out_shape=shapes,
        scratch_shapes=[
            pltpu.VMEM((rows, cols), F32),
            pltpu.VMEM((heads, rows, rows), BF),
            pltpu.VMEM((2, rows, width), BF),
            pltpu.VMEM((2, width, rows), BF),
        ]
        + [pltpu.VMEM((2, width, w.shape[1]), BF) for w in weights]
        + [pltpu.SemaphoreType.DMA((16,))],
        compiler_params=params(),
        cost_estimate=cost(
            4 * rows * width * cols + 4 * heads * rows * rows * HD, 4 * width * (2 * rows + cols)
        ),
        name="attend",
    )(idx, *pieces, gain, *weights, *extras)


def back_near_kernel(*refs):
    idx_ref, pieces = refs[0], refs[1:7]
    wo_ref, acc_ref, buffer, held, sems = refs[7:]
    width = buffer.shape[2]
    copies = Copies(sems)
    arrivals = fetch_near(copies, pieces, buffer)
    for n, (step, other) in enumerate(NEAR):
        part = part_of(idx_ref, step, other, width)
        arrivals[n].append(copies.start(wo_ref.at[:, part], held.at[n]))
    for n in range(len(NEAR)):
        for copy in arrivals[n]:
            copy.wait()
        if n == 0:
            acc_ref[...] = nt(buffer[n], held[n])
        else:
            acc_ref[...] += nt(buffer[n], held[n])


def back_near(idx, pieces, wo):
    rows, width = pieces[0].shape
    cols = wo.shape[0]
    return pl.pallas_call(
        back_near_kernel,
        grid=(1,),
        in_specs=[SMEM_SPEC] + [HBM_SPEC] * 7,
        out_specs=whole((rows, cols)),
        out_shape=jax.ShapeDtypeStruct((rows, cols), F32),
        scratch_shapes=[
            pltpu.VMEM((6, rows, width), BF),
            pltpu.VMEM((6, cols, width), BF),
            pltpu.SemaphoreType.DMA((12,)),
        ],
        compiler_params=params(),
        cost_estimate=cost(12 * rows * width * cols, 12 * width * (rows + cols)),
        name="back_near",
    )(idx, *pieces, wo)


def back_kernel(*refs, scale):
    idx_ref, pieces = refs[0], refs[1:5]
    inputs = refs[5:16]
    grad_ref, dots_ref, gq_ref, gk_ref, gv_ref = refs[16:21]
    buffer, held, scaled_ref, gq, gk, gv, sems = refs[21:28]
    targets = refs[28:]
    wo_ref, near_ref, far_turned, near_turned = inputs[:4]
    copies = Copies(sems)
    arrivals = fetch_far(copies, pieces, buffer)
    rows, width = buffer.shape[1:]
    for n, (step, other) in enumerate(FAR):
        part = part_of(idx_ref, step, other, width)
        arrivals[n].append(copies.start(wo_ref.at[:, part], held.at[n]))
    acc_ref, turned_ref = targets[:2]
    acc_copy = copies.start(near_ref, acc_ref)
    loads = [copies.start(source, target) for source, target in zip(inputs[4:], targets[2:])]
    turned_loads = [
        copies.start(near_turned, turned_ref.at[:3]),
        copies.start(far_turned, turned_ref.at[3:]),
    ]
    q_ref, k_ref, k_turned_ref, v_ref, shares_ref, inverse_ref, rotary_ref = targets[2:]
    acc_copy.wait()
    for n in range(2):
        for copy in arrivals[n]:
            copy.wait()
        acc_ref[...] += nt(buffer[n], held[n])
    for copy in loads:
        copy.wait()

    cosine = rotary_ref[0]
    sine = rotary_ref[1]
    heads = shares_ref.shape[0]
    factor = inverse_ref[:, 0:1] * scale

    def rotate_back(u):
        return u * cosine - pltpu.roll(u, HD // 2, 1) * sine

    products = jnp.zeros((rows, HD), F32)

    def emit(at, grad):
        cols = slice(at * HD, (at + 1) * HD)
        grad_ref[:, cols] = grad.astype(BF)
        scaled_ref[:, cols] = (grad * factor).astype(BF)

    parts = turned_ref.shape[0]
    outs = []

    def send(held_ref, out_ref, at):
        tall = turned_ref.shape[1]
        wide = held_ref.shape[2]
        for j in range(parts):
            held_ref[j] = nn(turned_ref[j], scaled_ref[:, at : at + wide]).astype(BF)
            start = pl.multiple_of(idx_ref[j] * width, tall)
            outs.append(copies.start(held_ref.at[j], out_ref.at[pl.ds(start, tall)]))

    key_grad = jnp.zeros((rows, HD), F32)
    value_grad = jnp.zeros((rows, HD), F32)
    for h in range(heads):
        cols = slice(h * HD, (h + 1) * HD)
        grad_attended = acc_ref[:, cols].astype(BF)
        shares = shares_ref[h]
        share_grad = nt(v_ref[...], grad_attended)
        wide = shares.astype(F32)
        row_dot = jnp.sum(share_grad * wide, axis=0, keepdims=True)
        dscore = (wide * (share_grad - row_dot) * SCORE_SCALE).astype(BF)
        key_grad += nn(dscore, q_ref[:, cols])
        value_grad += nn(shares, grad_attended)
        query_grad = nn(k_turned_ref[...], dscore).T
        products += query_grad * q_ref[:, cols].astype(F32)
        emit(h, rotate_back(query_grad))
    products += key_grad * k_ref[...].astype(F32) + value_grad * v_ref[...].astype(F32)
    emit(heads, rotate_back(key_grad))
    emit(heads + 1, value_grad)
    for copy in turned_loads:
        copy.wait()
    send(gq, gq_ref, 0)
    kv = gk.shape[2]
    for j in range(parts):
        both = nn(turned_ref[j], scaled_ref[:, heads * HD :]).astype(BF)
        gk[j] = both[:, :kv]
        gv[j] = both[:, kv:]
        tall = turned_ref.shape[1]
        start = pl.multiple_of(idx_ref[j] * width, tall)
        outs.append(copies.start(gk.at[j], gk_ref.at[pl.ds(start, tall)]))
        outs.append(copies.start(gv.at[j], gv_ref.at[pl.ds(start, tall)]))
    dots_ref[...] = lax.dot_general(
        jnp.ones((8, HD), F32), products, (((1,), (1,)), ((), ())),
        preferred_element_type=F32, precision=lax.Precision.HIGHEST,
    )
    for copy in outs:
        copy.wait()


def back(idx, pieces, wo, near, far_turned, near_turned, q, k, k_turned, v, shares, inverse, rotary, scale):
    width = pieces[0].shape[1]
    cols, features = wo.shape
    rows = near.shape[0]
    kv_cols = k.shape[1]
    grad_shape = (rows, cols + 2 * kv_cols)
    inputs = (wo, near, far_turned, near_turned, q, k, k_turned, v, shares, inverse, rotary)
    loaded = (q, k, k_turned, v, shares, inverse, rotary)
    weight_shapes = [
        jax.ShapeDtypeStruct((features, w), BF) for w in (cols, kv_cols, kv_cols)
    ]
    shapes = [jax.ShapeDtypeStruct(grad_shape, BF), jax.ShapeDtypeStruct((8, rows), F32)]
    return pl.pallas_call(
        functools.partial(back_kernel, scale=scale),
        grid=(1,),
        in_specs=[SMEM_SPEC] + [HBM_SPEC] * 15,
        out_specs=[whole(a.shape) for a in shapes] + [HBM_SPEC] * 3,
        out_shape=shapes + weight_shapes,
        scratch_shapes=[
            pltpu.VMEM((2, rows, width), BF),
            pltpu.VMEM((2, cols, width), BF),
            pltpu.VMEM(grad_shape, BF),
        ]
        + [pltpu.VMEM((4, features // 4, w.shape[1]), BF) for w in weight_shapes]
        + [
            pltpu.SemaphoreType.DMA((40,)),
            pltpu.VMEM(near.shape, F32),
            pltpu.VMEM((4, features // 4, rows), BF),
        ]
        + [pltpu.VMEM(a.shape, a.dtype) for a in loaded],
        compiler_params=params(),
        cost_estimate=cost(
            4 * rows * width * cols + 8 * cols * rows * rows + 2 * rows * features * (cols + 2 * kv_cols),
            2 * features * (rows + cols),
        ),
        name="back",
    )(idx, *pieces, *inputs)


def finish_kernel(*refs):
    for source, target in zip(refs[:3], refs[3:]):
        target[...] = source[...]


def finish(arrays):
    parts = 4
    specs = [pl.BlockSpec((a.shape[0] // parts, a.shape[1]), lambda j: (j, 0)) for a in arrays]
    return pl.pallas_call(
        finish_kernel,
        grid=(parts,),
        in_specs=specs,
        out_specs=specs,
        out_shape=[jax.ShapeDtypeStruct(a.shape, a.dtype) for a in arrays],
        compiler_params=params(),
        cost_estimate=cost(0, 4 * sum(a.size for a in arrays)),
        name="finish",
    )(*arrays)


def out_term_kernel(idx_ref, _, attended_ref, wo_ref, out_ref):
    out_ref[0] = nn(attended_ref[...], wo_ref[...]).astype(BF)


def place_of(other):
    if other:
        return lambda j, idx: idx[j] + 1 - idx[4]
    return lambda j, idx: idx[j] + idx[4]


def out_terms(idx, other, after, attended, wo, width):
    rows, cols = attended.shape
    parts = 4
    at = place_of(other)
    grid_spec = pltpu.PrefetchScalarGridSpec(
        num_scalar_prefetch=1,
        grid=(parts,),
        in_specs=[
            HBM_SPEC,
            pl.BlockSpec((rows, cols), lambda j, idx: (0, 0)),
            pl.BlockSpec((cols, width), lambda j, idx: (0, at(j, idx))),
        ],
        out_specs=pl.BlockSpec((1, rows, width), lambda j, idx: (j, 0, 0)),
    )
    return pl.pallas_call(
        out_term_kernel,
        grid_spec=grid_spec,
        out_shape=jax.ShapeDtypeStruct((parts, rows, width), BF),
        compiler_params=params(),
        cost_estimate=cost(40 * parts * rows * cols * width, 40 * parts * width * (rows + cols)),
        name="out_terms",
    )(idx, after, attended, wo)


def input_term_kernel(idx_ref, _, grad_ref, dots_ref, wq_ref, wk_ref, wv_ref, out_ref):
    q_cols = wq_ref.shape[1]
    kv_cols = wk_ref.shape[1]
    rows = grad_ref.shape[0]
    dots = dots_ref[0:1, :]
    high = dots.astype(BF).astype(F32)
    line = lax.broadcasted_iota(jnp.int32, (16, dots.shape[1]), 0)
    extra = jnp.where(line == 0, high, jnp.where(line == 1, dots - high, 0.0))
    term = nt(grad_ref[:, :q_cols], wq_ref[...])
    term += nt(grad_ref[:, q_cols : q_cols + kv_cols], wk_ref[...])
    term += nt(grad_ref[:, q_cols + kv_cols :], wv_ref[...])
    out_ref[0, :rows] = term.astype(BF)
    out_ref[0, rows:] = extra.astype(BF)


def input_terms(idx, other, after, grad, dots, wq, wk, wv, width):
    rows, cols = grad.shape
    parts = 4
    at = place_of(other)
    grid_spec = pltpu.PrefetchScalarGridSpec(
        num_scalar_prefetch=1,
        grid=(parts,),
        in_specs=[
            HBM_SPEC,
            pl.BlockSpec((rows, cols), lambda j, idx: (0, 0)),
            pl.BlockSpec(dots.shape, lambda j, idx: (0, 0)),
        ]
        + [
            pl.BlockSpec((width, w.shape[1]), lambda j, idx: (at(j, idx), 0))
            for w in (wq, wk, wv)
        ],
        out_specs=pl.BlockSpec((1, rows + 16, width), lambda j, idx: (j, 0, 0)),
    )
    return pl.pallas_call(
        input_term_kernel,
        grid_spec=grid_spec,
        out_shape=jax.ShapeDtypeStruct((parts, rows + 16, width), BF),
        compiler_params=params(),
        cost_estimate=cost(40 * parts * rows * cols * width, 40 * parts * width * (rows + cols)),
        name="input_terms",
    )(idx, after, grad, dots, wq, wk, wv)


def shift(array, step, axis="y"):
    size = lax.axis_size(axis)
    return lax.ppermute(array, axis, [(i, (i + step) % size) for i in range(size)])


def swap(array):
    return lax.ppermute(array, "core", [(0, 1), (1, 0)])


def gather_near(piece):
    return piece, shift(piece, 1), shift(piece, -1)


def gather_far(near):
    _, below, above = near
    half = below.shape[0] // 2
    return shift(below[:half], 1), shift(above[half:], -1)


def both_cores(pieces):
    return tuple(pieces) + tuple(swap(a) for a in pieces)


def sum_pieces(mine_terms, other_terms):
    wide = lambda a: a.astype(F32)
    sums = (wide(mine_terms) + wide(swap(other_terms))).astype(BF)
    rows = sums.shape[1]
    half = rows // 32 * 16
    relay_top = shift(sums[3, :half], 1)
    relay_end = shift(sums[3, half:], -1)
    up = jnp.concatenate([(wide(sums[2, :half]) + wide(relay_top)).astype(BF), sums[2, half:]], axis=0)
    down = jnp.concatenate([sums[1, :half], (wide(sums[1, half:]) + wide(relay_end)).astype(BF)], axis=0)
    return wide(sums[0]) + wide(shift(up, 1)) + wide(shift(down, -1))


def exchange(panels):
    return lax.all_to_all(panels, ("x", "z"), split_axis=0, concat_axis=0, tiled=True)


def per_device(
    tokens, norm_gain, doc_ids, panel_plan, wq, wk, wv, wo, cotangent,
):
    y, core = lax.axis_index("y"), lax.axis_index("core")
    ys, cores = lax.axis_size("y"), lax.axis_size("core")
    block = lax.axis_index("x") * lax.axis_size("z") + lax.axis_index("z")
    dp = lax.axis_size("x") * lax.axis_size("z")
    count = panel_plan.shape[0]
    rows, width = tokens.shape
    panel = rows // count
    features = norm_gain.shape[0]

    around = (y + jnp.array(STEPS, jnp.int32)) % ys
    steps = jnp.array(STEPS, jnp.int32)
    idx = jnp.concatenate(
        [around * cores, core[None], (lax.axis_index("x") + steps) % 4, (lax.axis_index("z") + steps) % 4]
    )

    here_tokens = exchange(place(panel_plan, tokens.reshape(count, panel, width))).reshape(rows, width)
    arrived = exchange(
        place_meta(
            panel_plan, here_tokens, cotangent.reshape(count, panel, width), doc_ids.reshape(count, panel)
        )
    )
    here_cot = arrived[:, :, :width].reshape(rows, width)
    meta = arrived[:, :, width : width + 3].reshape(rows, 3).astype(jnp.int32)
    docs = meta[:, 0] * 128 + meta[:, 1]
    at = block * rows + meta[:, 2] * panel + jnp.arange(rows, dtype=jnp.int32) % panel
    positions = (at - docs).astype(F32)
    frequency = ROPE_THETA ** (-2.0 * jnp.arange(HD // 2, dtype=F32) / HD)
    angles = positions[:, None] * frequency[None, :]
    cosine, sine = jnp.cos(angles), jnp.sin(angles)
    rotary = jnp.stack(
        [jnp.concatenate([cosine, cosine], axis=1), jnp.concatenate([-sine, sine], axis=1)]
    )
    where = jnp.pad(jnp.stack([docs, at]).astype(F32), ((0, 6), (0, 0)))

    tok_near = gather_near(here_tokens)
    cot_near = gather_near(here_cot)
    tok_far = gather_far(tok_near)
    gain = norm_gain.reshape(features // width, width)
    near_turned, near_raw, near_squares = project_near(idx, both_cores(tok_near), gain, wq, wk, wv)
    tok_far, cot_near, near_raw = lax.optimization_barrier((tok_far, cot_near, near_raw))
    cot_far = gather_far(cot_near)
    far_turned, inverse, q, k, k_turned, v, shares, attended = attend(
        idx, both_cores(tok_far), gain, wq, wk, wv, near_raw, near_squares, rotary, where
    )

    scale = (rows * dp) ** (-0.5)
    cot_near, shares = lax.optimization_barrier((both_cores(cot_near), shares))
    near = back_near(idx, cot_near, wo)
    cot_far, near = lax.optimization_barrier((cot_far, near))
    grad, dots, *grads = back(
        idx, both_cores(cot_far), wo, near, far_turned, near_turned, q, k, k_turned, v, shares,
        inverse, rotary, scale,
    )
    grad_query, grad_key, grad_value = finish(lax.psum(tuple(grads), ("x", "z")))
    after = swap(dots)
    out_sum = sum_pieces(
        *[out_terms(idx, other, after, attended, wo, width) for other in (False, True)]
    )
    output_rows = (here_tokens.astype(F32) + out_sum).astype(BF)
    in_sum = sum_pieces(
        *[input_terms(idx, other, after, grad, dots, wq, wk, wv, width) for other in (False, True)]
    )
    inverse = inverse[:, 0:1]
    mean_term = ((in_sum[rows] + in_sum[rows + 1]) / features)[:, None]
    own = y * cores + core
    own_gain = lax.dynamic_slice_in_dim(norm_gain, own * width, width, 0)
    own_scaled = here_tokens.astype(F32) * inverse
    grad_rows = here_cot.astype(F32) + inverse * (in_sum[:rows] * own_gain - own_scaled * mean_term)
    grad_rows = grad_rows.astype(BF)

    targets = panel_plan // count
    output = exchange(output_rows.reshape(dp, panel, width))[targets].reshape(rows, width)
    grad_tokens = exchange(grad_rows.reshape(dp, panel, width))[targets].reshape(rows, width)
    return output, grad_tokens, grad_query, grad_key, grad_value


def solution(mesh):
    axes = ("x", "z", "y", "core")
    split = Mesh(mesh.devices.reshape(4, 4, 4, 2), axes)
    dp, tensor = ("x", "z"), ("y", "core")
    in_specs = (
        P(dp, tensor),
        P(),
        P(dp),
        P(dp),
        P(None, tensor),
        P(None, tensor),
        P(None, tensor),
        P(tensor, None),
        P(dp, tensor),
    )
    out_specs = (
        P(dp, tensor),
        P(dp, tensor),
        P(None, tensor),
        P(None, tensor),
        P(None, tensor),
    )
    return jax.shard_map(
        per_device, mesh=split, in_specs=in_specs, out_specs=out_specs, check_vma=False
    )
```

```python
import functools

import jax
import jax.numpy as jnp
from jax import lax
from jax.experimental import pallas as pl
from jax.experimental.pallas import tpu as pltpu
from jax.sharding import Mesh
from jax.sharding import PartitionSpec as P

HD = 128
NORM_EPSILON = 1e-05
ROPE_THETA = 500000.0
SCORE_SCALE = HD ** (-0.5)
STEPS = (0, -1, 1, 2)
BF = jnp.bfloat16
F32 = jnp.float32
VMEM_LIMIT = 60 * 1024 * 1024


def params():
    return pltpu.CompilerParams(vmem_limit_bytes=VMEM_LIMIT)


def cost(flops, moved):
    return pl.CostEstimate(flops=int(flops), bytes_accessed=int(moved), transcendentals=0)


def nn(a, b):
    return lax.dot_general(a, b, (((1,), (0,)), ((), ())), preferred_element_type=F32)


def nt(a, b):
    return lax.dot_general(a, b, (((1,), (1,)), ((), ())), preferred_element_type=F32)


def place_kernel(plan_ref, rows_ref, out_ref):
    count = rows_ref.shape[0]
    for panel in range(count):
        out_ref[plan_ref[panel] // count] = rows_ref[panel]


def place(plan, panels):
    return pl.pallas_call(
        place_kernel,
        out_shape=jax.ShapeDtypeStruct(panels.shape, panels.dtype),
        in_specs=[
            pl.BlockSpec(memory_space=pltpu.SMEM),
            pl.BlockSpec(memory_space=pltpu.VMEM),
        ],
        out_specs=pl.BlockSpec(memory_space=pltpu.VMEM),
        compiler_params=params(),
        cost_estimate=cost(0, 2 * panels.size * 2),
        name="place",
    )(plan, panels)


def place_meta_kernel(plan_ref, rows_ref, docs_ref, out_ref):
    count, rows, width = rows_ref.shape
    for panel in range(count):
        target = plan_ref[panel] // count
        slot = plan_ref[panel] % count
        out_ref[target, :, :width] = rows_ref[panel]
        doc = docs_ref[panel]
        high = (doc // 128).astype(F32)
        low = (doc % 128).astype(F32)
        lane = lax.broadcasted_iota(jnp.int32, (rows, 128), 1)
        extra = jnp.where(lane == 0, high, 0.0)
        extra = jnp.where(lane == 1, low, extra)
        extra = jnp.where(lane == 2, slot.astype(F32), extra)
        out_ref[target, :, width:] = extra.astype(BF)


def place_meta(plan, panels, docs):
    count, rows, width = panels.shape
    return pl.pallas_call(
        place_meta_kernel,
        out_shape=jax.ShapeDtypeStruct((count, rows, width + 128), panels.dtype),
        in_specs=[
            pl.BlockSpec(memory_space=pltpu.SMEM),
            pl.BlockSpec(memory_space=pltpu.VMEM),
            pl.BlockSpec(memory_space=pltpu.VMEM),
        ],
        out_specs=pl.BlockSpec(memory_space=pltpu.VMEM),
        compiler_params=params(),
        cost_estimate=cost(0, 2 * panels.size * 2),
        name="place_meta",
    )(plan, panels, docs.reshape(count, rows, 1))


NEAR = tuple((step, other) for step in range(3) for other in (0, 1))
FAR = ((3, 0), (3, 1))

SMEM_SPEC = pl.BlockSpec(memory_space=pltpu.SMEM)
HBM_SPEC = pl.BlockSpec(memory_space=pltpu.HBM)


def whole(shape):
    return pl.BlockSpec(tuple(shape), lambda j: (0,) * len(shape))


def part_of(idx_ref, step, other, width):
    at = idx_ref[step] + (idx_ref[4] if not other else 1 - idx_ref[4])
    return pl.ds(pl.multiple_of(at * width, width), width)


class Copies:
    def __init__(self, sems):
        self.sems = sems
        self.count = 0

    def start(self, source, target):
        copy = pltpu.make_async_copy(source, target, self.sems.at[self.count])
        self.count += 1
        copy.start()
        return copy


def fetch_near(copies, pieces, buffer):
    return [[copies.start(pieces[3 * o + s], buffer.at[n])] for n, (s, o) in enumerate(NEAR)]


def fetch_far(copies, pieces, buffer):
    half = buffer.shape[1] // 2
    return [
        [
            copies.start(pieces[2 * n], buffer.at[n, :half]),
            copies.start(pieces[2 * n + 1], buffer.at[n, half:]),
        ]
        for n in range(2)
    ]


def project_steps(
    idx_ref, places, arrivals, copies, buffer, gain_ref, weights, held, stage, turned_ref, raw_ref, fresh
):
    rows, width = buffer.shape[1:]
    for n, (step, other) in enumerate(places):
        part = part_of(idx_ref, step, other, width)
        for ref, target in zip(weights, held):
            arrivals[n].append(copies.start(ref.at[part], target.at[n]))
    squares = jnp.zeros((rows, 1), F32)
    sent = []
    for n, (step, other) in enumerate(places):
        core = idx_ref[4] if not other else 1 - idx_ref[4]
        for copy in arrivals[n]:
            copy.wait()
        wide = buffer[n].astype(F32)
        squares += jnp.sum(wide * wide, axis=1, keepdims=True)
        gained = (wide * gain_ref[pl.ds(idx_ref[step] + core, 1)]).astype(BF)
        stage[n] = gained.T
        here = pl.ds(pl.multiple_of(core * width, width), width)
        sent.append(copies.start(stage.at[n], turned_ref.at[step % 3, here]))
        at = 0
        for target in held:
            cols = slice(at, at + target.shape[2])
            at += target.shape[2]
            if fresh and n == 0:
                raw_ref[:, cols] = nn(gained, target[n])
            else:
                raw_ref[:, cols] += nn(gained, target[n])
    return squares, sent


def project_near_kernel(*refs):
    idx_ref, pieces = refs[0], refs[1:7]
    gain_ref, wq, wk, wv, turned_ref, raw_ref, squares_ref, buffer, stage, hq, hk, hv, sems = refs[7:]
    copies = Copies(sems)
    arrivals = fetch_near(copies, pieces, buffer)
    squares, sent = project_steps(
        idx_ref, NEAR, arrivals, copies, buffer, gain_ref, (wq, wk, wv), (hq, hk, hv),
        stage, turned_ref, raw_ref, True,
    )
    squares_ref[...] = jnp.broadcast_to(squares, squares_ref.shape)
    for copy in sent:
        copy.wait()


def project_near(idx, pieces, gain, wq, wk, wv):
    rows, width = pieces[0].shape
    weights = (wq, wk, wv)
    cols = sum(w.shape[1] for w in weights)
    shapes = [
        jax.ShapeDtypeStruct((3, 2 * width, rows), BF),
        jax.ShapeDtypeStruct((rows, cols), F32),
        jax.ShapeDtypeStruct((rows, HD), F32),
    ]
    return pl.pallas_call(
        project_near_kernel,
        grid=(1,),
        in_specs=[SMEM_SPEC] + [HBM_SPEC] * 6 + [whole(gain.shape)] + [HBM_SPEC] * 3,
        out_specs=[HBM_SPEC] + [whole(a.shape) for a in shapes[1:]],
        out_shape=shapes,
        scratch_shapes=[pltpu.VMEM((6, rows, width), BF), pltpu.VMEM((6, width, rows), BF)]
        + [pltpu.VMEM((6, width, w.shape[1]), BF) for w in weights]
        + [pltpu.SemaphoreType.DMA((30,))],
        compiler_params=params(),
        cost_estimate=cost(12 * rows * width * cols, 12 * width * (2 * rows + cols)),
        name="project_near",
    )(idx, *pieces, gain, *weights)


def attend_kernel(*refs):
    idx_ref, pieces = refs[0], refs[1:5]
    (
        gain_ref, wq, wk, wv, near_raw_ref, near_squares_ref, rotary_ref, where_ref,
        turned_ref, inverse_ref, q_ref, k_ref, k_turned_ref, v_ref, shares_ref, attended_ref,
        raw_ref, shares_stage, buffer, stage, hq, hk, hv, sems,
    ) = refs[5:]
    rows, width = buffer.shape[1:]
    copies = Copies(sems)
    arrivals = fetch_far(copies, pieces, buffer)
    raw_ref[...] = near_raw_ref[...]
    squares, sent = project_steps(
        idx_ref, FAR, arrivals, copies, buffer, gain_ref, (wq, wk, wv), (hq, hk, hv),
        stage, turned_ref, raw_ref, False,
    )
    features = wq.shape[0]
    inverse = lax.rsqrt((squares + near_squares_ref[:, 0:1]) / features + NORM_EPSILON)
    inverse_ref[...] = jnp.broadcast_to(inverse, inverse_ref.shape)

    cosine = rotary_ref[0] * inverse
    sine = rotary_ref[1] * inverse
    heads = shares_stage.shape[0]

    def rotate(u):
        return u * cosine + pltpu.roll(u, HD // 2, 1) * sine

    key = rotate(raw_ref[:, heads * HD : (heads + 1) * HD])
    k_ref[...] = key.astype(BF)
    k_turned_ref[...] = key.T.astype(BF)
    value = raw_ref[:, (heads + 1) * HD :] * inverse
    v_ref[...] = value.astype(BF)
    v_turned = value.T.astype(BF)
    down = where_ref[...].T
    doc_s = down[:, 0:1]
    at_s = down[:, 1:2]
    doc_g = where_ref[0:1, :]
    at_g = where_ref[1:2, :]
    allowed = (doc_s == doc_g) & (at_s <= at_g)
    for h in range(heads):
        cols = slice(h * HD, (h + 1) * HD)
        query = rotate(raw_ref[:, cols]).astype(BF)
        q_ref[:, cols] = query
        scores = nt(k_ref[...], query) * SCORE_SCALE
        weights = jnp.where(allowed, jnp.exp(scores), 0.0)
        total = jnp.sum(weights, axis=0, keepdims=True)
        shares = (weights * (1.0 / total)).astype(BF)
        shares_stage[h] = shares
        sent.append(copies.start(shares_stage.at[h], shares_ref.at[h]))
        attended_ref[:, cols] = nn(v_turned, shares).T.astype(BF)
    for copy in sent:
        copy.wait()


def attend(idx, pieces, gain, wq, wk, wv, near_raw, near_squares, rotary, where):
    width = pieces[0].shape[1]
    rows, cols = near_raw.shape
    weights = (wq, wk, wv)
    heads = wq.shape[1] // HD
    shapes = [
        jax.ShapeDtypeStruct((1, 2 * width, rows), BF),
        jax.ShapeDtypeStruct((rows, HD), F32),
        jax.ShapeDtypeStruct((rows, heads * HD), BF),
        jax.ShapeDtypeStruct((rows, HD), BF),
        jax.ShapeDtypeStruct((HD, rows), BF),
        jax.ShapeDtypeStruct((rows, HD), BF),
        jax.ShapeDtypeStruct((heads, rows, rows), BF),
        jax.ShapeDtypeStruct((rows, heads * HD), BF),
    ]
    extras = (near_raw, near_squares, rotary, where)
    out_specs = [whole(a.shape) for a in shapes]
    out_specs[0] = out_specs[6] = HBM_SPEC
    return pl.pallas_call(
        attend_kernel,
        grid=(1,),
        in_specs=[SMEM_SPEC] + [HBM_SPEC] * 4 + [whole(gain.shape)] + [HBM_SPEC] * 3
        + [whole(a.shape) for a in extras],
        out_specs=out_specs,
        out_shape=shapes,
        scratch_shapes=[
            pltpu.VMEM((rows, cols), F32),
            pltpu.VMEM((heads, rows, rows), BF),
            pltpu.VMEM((2, rows, width), BF),
            pltpu.VMEM((2, width, rows), BF),
        ]
        + [pltpu.VMEM((2, width, w.shape[1]), BF) for w in weights]
        + [pltpu.SemaphoreType.DMA((16,))],
        compiler_params=params(),
        cost_estimate=cost(
            4 * rows * width * cols + 4 * heads * rows * rows * HD, 4 * width * (2 * rows + cols)
        ),
        name="attend",
    )(idx, *pieces, gain, *weights, *extras)


def back_near_kernel(*refs):
    idx_ref, pieces = refs[0], refs[1:7]
    wo_ref, acc_ref, buffer, held, sems = refs[7:]
    width = buffer.shape[2]
    copies = Copies(sems)
    arrivals = fetch_near(copies, pieces, buffer)
    for n, (step, other) in enumerate(NEAR):
        part = part_of(idx_ref, step, other, width)
        arrivals[n].append(copies.start(wo_ref.at[:, part], held.at[n]))
    for n in range(len(NEAR)):
        for copy in arrivals[n]:
            copy.wait()
        if n == 0:
            acc_ref[...] = nt(buffer[n], held[n])
        else:
            acc_ref[...] += nt(buffer[n], held[n])


def back_near(idx, pieces, wo):
    rows, width = pieces[0].shape
    cols = wo.shape[0]
    return pl.pallas_call(
        back_near_kernel,
        grid=(1,),
        in_specs=[SMEM_SPEC] + [HBM_SPEC] * 7,
        out_specs=whole((rows, cols)),
        out_shape=jax.ShapeDtypeStruct((rows, cols), F32),
        scratch_shapes=[
            pltpu.VMEM((6, rows, width), BF),
            pltpu.VMEM((6, cols, width), BF),
            pltpu.SemaphoreType.DMA((12,)),
        ],
        compiler_params=params(),
        cost_estimate=cost(12 * rows * width * cols, 12 * width * (rows + cols)),
        name="back_near",
    )(idx, *pieces, wo)


def back_kernel(*refs, scale):
    idx_ref, pieces = refs[0], refs[1:5]
    inputs = refs[5:16]
    grad_ref, dots_ref, gq_ref, gk_ref, gv_ref = refs[16:21]
    buffer, held, scaled_ref, gq, gk, gv, sems = refs[21:28]
    targets = refs[28:]
    wo_ref, near_ref, far_turned, near_turned = inputs[:4]
    copies = Copies(sems)
    arrivals = fetch_far(copies, pieces, buffer)
    rows, width = buffer.shape[1:]
    for n, (step, other) in enumerate(FAR):
        part = part_of(idx_ref, step, other, width)
        arrivals[n].append(copies.start(wo_ref.at[:, part], held.at[n]))
    acc_ref, turned_ref = targets[:2]
    acc_copy = copies.start(near_ref, acc_ref)
    loads = [copies.start(source, target) for source, target in zip(inputs[4:], targets[2:])]
    turned_loads = [
        copies.start(near_turned, turned_ref.at[:3]),
        copies.start(far_turned, turned_ref.at[3:]),
    ]
    q_ref, k_ref, k_turned_ref, v_ref, shares_ref, inverse_ref, rotary_ref = targets[2:]
    acc_copy.wait()
    for n in range(2):
        for copy in arrivals[n]:
            copy.wait()
        acc_ref[...] += nt(buffer[n], held[n])
    for copy in loads:
        copy.wait()

    cosine = rotary_ref[0]
    sine = rotary_ref[1]
    heads = shares_ref.shape[0]
    factor = inverse_ref[:, 0:1] * scale

    def rotate_back(u):
        return u * cosine - pltpu.roll(u, HD // 2, 1) * sine

    products = jnp.zeros((rows, HD), F32)

    def emit(at, grad):
        cols = slice(at * HD, (at + 1) * HD)
        grad_ref[:, cols] = grad.astype(BF)
        scaled_ref[:, cols] = (grad * factor).astype(BF)

    parts = turned_ref.shape[0]
    outs = []

    def send(held_ref, out_ref, at):
        tall = turned_ref.shape[1]
        wide = held_ref.shape[2]
        for j in range(parts):
            held_ref[j] = nn(turned_ref[j], scaled_ref[:, at : at + wide]).astype(BF)
            start = pl.multiple_of(idx_ref[j] * width, tall)
            outs.append(copies.start(held_ref.at[j], out_ref.at[pl.ds(start, tall)]))

    key_grad = jnp.zeros((rows, HD), F32)
    value_grad = jnp.zeros((rows, HD), F32)
    for h in range(heads):
        cols = slice(h * HD, (h + 1) * HD)
        grad_attended = acc_ref[:, cols].astype(BF)
        shares = shares_ref[h]
        share_grad = nt(v_ref[...], grad_attended)
        wide = shares.astype(F32)
        row_dot = jnp.sum(share_grad * wide, axis=0, keepdims=True)
        dscore = (wide * (share_grad - row_dot) * SCORE_SCALE).astype(BF)
        key_grad += nn(dscore, q_ref[:, cols])
        value_grad += nn(shares, grad_attended)
        query_grad = nn(k_turned_ref[...], dscore).T
        products += query_grad * q_ref[:, cols].astype(F32)
        emit(h, rotate_back(query_grad))
    products += key_grad * k_ref[...].astype(F32) + value_grad * v_ref[...].astype(F32)
    emit(heads, rotate_back(key_grad))
    emit(heads + 1, value_grad)
    for copy in turned_loads:
        copy.wait()
    send(gq, gq_ref, 0)
    kv = gk.shape[2]
    for j in range(parts):
        both = nn(turned_ref[j], scaled_ref[:, heads * HD :]).astype(BF)
        gk[j] = both[:, :kv]
        gv[j] = both[:, kv:]
        tall = turned_ref.shape[1]
        start = pl.multiple_of(idx_ref[j] * width, tall)
        outs.append(copies.start(gk.at[j], gk_ref.at[pl.ds(start, tall)]))
        outs.append(copies.start(gv.at[j], gv_ref.at[pl.ds(start, tall)]))
    dots_ref[...] = lax.dot_general(
        jnp.ones((8, HD), F32), products, (((1,), (1,)), ((), ())),
        preferred_element_type=F32, precision=lax.Precision.HIGHEST,
    )
    for copy in outs:
        copy.wait()


def back(idx, pieces, wo, near, far_turned, near_turned, q, k, k_turned, v, shares, inverse, rotary, scale):
    width = pieces[0].shape[1]
    cols, features = wo.shape
    rows = near.shape[0]
    kv_cols = k.shape[1]
    grad_shape = (rows, cols + 2 * kv_cols)
    inputs = (wo, near, far_turned, near_turned, q, k, k_turned, v, shares, inverse, rotary)
    loaded = (q, k, k_turned, v, shares, inverse, rotary)
    weight_shapes = [
        jax.ShapeDtypeStruct((features, w), BF) for w in (cols, kv_cols, kv_cols)
    ]
    shapes = [jax.ShapeDtypeStruct(grad_shape, BF), jax.ShapeDtypeStruct((8, rows), F32)]
    return pl.pallas_call(
        functools.partial(back_kernel, scale=scale),
        grid=(1,),
        in_specs=[SMEM_SPEC] + [HBM_SPEC] * 15,
        out_specs=[whole(a.shape) for a in shapes] + [HBM_SPEC] * 3,
        out_shape=shapes + weight_shapes,
        scratch_shapes=[
            pltpu.VMEM((2, rows, width), BF),
            pltpu.VMEM((2, cols, width), BF),
            pltpu.VMEM(grad_shape, BF),
        ]
        + [pltpu.VMEM((4, features // 4, w.shape[1]), BF) for w in weight_shapes]
        + [
            pltpu.SemaphoreType.DMA((40,)),
            pltpu.VMEM(near.shape, F32),
            pltpu.VMEM((4, features // 4, rows), BF),
        ]
        + [pltpu.VMEM(a.shape, a.dtype) for a in loaded],
        compiler_params=params(),
        cost_estimate=cost(
            4 * rows * width * cols + 8 * cols * rows * rows + 2 * rows * features * (cols + 2 * kv_cols),
            2 * features * (rows + cols),
        ),
        name="back",
    )(idx, *pieces, *inputs)


def finish_kernel(*refs):
    for source, target in zip(refs[:3], refs[3:]):
        target[...] = source[...]


def finish(arrays):
    parts = 4
    specs = [pl.BlockSpec((a.shape[0] // parts, a.shape[1]), lambda j: (j, 0)) for a in arrays]
    return pl.pallas_call(
        finish_kernel,
        grid=(parts,),
        in_specs=specs,
        out_specs=specs,
        out_shape=[jax.ShapeDtypeStruct(a.shape, a.dtype) for a in arrays],
        compiler_params=params(),
        cost_estimate=cost(0, 4 * sum(a.size for a in arrays)),
        name="finish",
    )(*arrays)


def out_term_kernel(idx_ref, _, attended_ref, wo_ref, out_ref):
    out_ref[0] = nn(attended_ref[...], wo_ref[...]).astype(BF)


def place_of(other):
    if other:
        return lambda j, idx: idx[j] + 1 - idx[4]
    return lambda j, idx: idx[j] + idx[4]


def out_terms(idx, other, after, attended, wo, width):
    rows, cols = attended.shape
    parts = 4
    at = place_of(other)
    grid_spec = pltpu.PrefetchScalarGridSpec(
        num_scalar_prefetch=1,
        grid=(parts,),
        in_specs=[
            HBM_SPEC,
            pl.BlockSpec((rows, cols), lambda j, idx: (0, 0)),
            pl.BlockSpec((cols, width), lambda j, idx: (0, at(j, idx))),
        ],
        out_specs=pl.BlockSpec((1, rows, width), lambda j, idx: (j, 0, 0)),
    )
    return pl.pallas_call(
        out_term_kernel,
        grid_spec=grid_spec,
        out_shape=jax.ShapeDtypeStruct((parts, rows, width), BF),
        compiler_params=params(),
        cost_estimate=cost(40 * parts * rows * cols * width, 40 * parts * width * (rows + cols)),
        name="out_terms",
    )(idx, after, attended, wo)


def input_term_kernel(idx_ref, _, grad_ref, dots_ref, wq_ref, wk_ref, wv_ref, out_ref):
    q_cols = wq_ref.shape[1]
    kv_cols = wk_ref.shape[1]
    rows = grad_ref.shape[0]
    dots = dots_ref[0:1, :]
    high = dots.astype(BF).astype(F32)
    line = lax.broadcasted_iota(jnp.int32, (16, dots.shape[1]), 0)
    extra = jnp.where(line == 0, high, jnp.where(line == 1, dots - high, 0.0))
    term = nt(grad_ref[:, :q_cols], wq_ref[...])
    term += nt(grad_ref[:, q_cols : q_cols + kv_cols], wk_ref[...])
    term += nt(grad_ref[:, q_cols + kv_cols :], wv_ref[...])
    out_ref[0, :rows] = term.astype(BF)
    out_ref[0, rows:] = extra.astype(BF)


def input_terms(idx, other, after, grad, dots, wq, wk, wv, width):
    rows, cols = grad.shape
    parts = 4
    at = place_of(other)
    grid_spec = pltpu.PrefetchScalarGridSpec(
        num_scalar_prefetch=1,
        grid=(parts,),
        in_specs=[
            HBM_SPEC,
            pl.BlockSpec((rows, cols), lambda j, idx: (0, 0)),
            pl.BlockSpec(dots.shape, lambda j, idx: (0, 0)),
        ]
        + [
            pl.BlockSpec((width, w.shape[1]), lambda j, idx: (at(j, idx), 0))
            for w in (wq, wk, wv)
        ],
        out_specs=pl.BlockSpec((1, rows + 16, width), lambda j, idx: (j, 0, 0)),
    )
    return pl.pallas_call(
        input_term_kernel,
        grid_spec=grid_spec,
        out_shape=jax.ShapeDtypeStruct((parts, rows + 16, width), BF),
        compiler_params=params(),
        cost_estimate=cost(40 * parts * rows * cols * width, 40 * parts * width * (rows + cols)),
        name="input_terms",
    )(idx, after, grad, dots, wq, wk, wv)


def shift(array, step, axis="y"):
    size = lax.axis_size(axis)
    return lax.ppermute(array, axis, [(i, (i + step) % size) for i in range(size)])


def swap(array):
    return lax.ppermute(array, "core", [(0, 1), (1, 0)])


def gather_near(piece):
    return piece, shift(piece, 1), shift(piece, -1)


def gather_far(near):
    _, below, above = near
    half = below.shape[0] // 2
    return shift(below[:half], 1), shift(above[half:], -1)


def both_cores(pieces):
    return tuple(pieces) + tuple(swap(a) for a in pieces)


def sum_pieces(mine_terms, other_terms):
    wide = lambda a: a.astype(F32)
    sums = (wide(mine_terms) + wide(swap(other_terms))).astype(BF)
    rows = sums.shape[1]
    half = rows // 32 * 16
    relay_top = shift(sums[3, :half], 1)
    relay_end = shift(sums[3, half:], -1)
    up = jnp.concatenate([(wide(sums[2, :half]) + wide(relay_top)).astype(BF), sums[2, half:]], axis=0)
    down = jnp.concatenate([sums[1, :half], (wide(sums[1, half:]) + wide(relay_end)).astype(BF)], axis=0)
    return wide(sums[0]) + wide(shift(up, 1)) + wide(shift(down, -1))


def exchange(panels):
    return lax.all_to_all(panels, ("x", "z"), split_axis=0, concat_axis=0, tiled=True)


def per_device(
    tokens, norm_gain, doc_ids, panel_plan, wq, wk, wv, wo, cotangent,
):
    y, core = lax.axis_index("y"), lax.axis_index("core")
    ys, cores = lax.axis_size("y"), lax.axis_size("core")
    block = lax.axis_index("x") * lax.axis_size("z") + lax.axis_index("z")
    dp = lax.axis_size("x") * lax.axis_size("z")
    count = panel_plan.shape[0]
    rows, width = tokens.shape
    panel = rows // count
    features = norm_gain.shape[0]

    around = (y + jnp.array(STEPS, jnp.int32)) % ys
    steps = jnp.array(STEPS, jnp.int32)
    idx = jnp.concatenate(
        [around * cores, core[None], (lax.axis_index("x") + steps) % 4, (lax.axis_index("z") + steps) % 4]
    )

    here_tokens = exchange(place(panel_plan, tokens.reshape(count, panel, width))).reshape(rows, width)
    arrived = exchange(
        place_meta(panel_plan, cotangent.reshape(count, panel, width), doc_ids.reshape(count, panel))
    )
    here_cot = arrived[:, :, :width].reshape(rows, width)
    meta = arrived[:, :, width : width + 3].reshape(rows, 3).astype(jnp.int32)
    docs = meta[:, 0] * 128 + meta[:, 1]
    at = block * rows + meta[:, 2] * panel + jnp.arange(rows, dtype=jnp.int32) % panel
    positions = (at - docs).astype(F32)
    frequency = ROPE_THETA ** (-2.0 * jnp.arange(HD // 2, dtype=F32) / HD)
    angles = positions[:, None] * frequency[None, :]
    cosine, sine = jnp.cos(angles), jnp.sin(angles)
    rotary = jnp.stack(
        [jnp.concatenate([cosine, cosine], axis=1), jnp.concatenate([-sine, sine], axis=1)]
    )
    where = jnp.pad(jnp.stack([docs, at]).astype(F32), ((0, 6), (0, 0)))

    tok_near = gather_near(here_tokens)
    cot_near = gather_near(here_cot)
    tok_far = gather_far(tok_near)
    gain = norm_gain.reshape(features // width, width)
    near_turned, near_raw, near_squares = project_near(idx, both_cores(tok_near), gain, wq, wk, wv)
    tok_far, cot_near, near_raw = lax.optimization_barrier((tok_far, cot_near, near_raw))
    cot_far = gather_far(cot_near)
    far_turned, inverse, q, k, k_turned, v, shares, attended = attend(
        idx, both_cores(tok_far), gain, wq, wk, wv, near_raw, near_squares, rotary, where
    )

    scale = (rows * dp) ** (-0.5)
    cot_near, shares = lax.optimization_barrier((both_cores(cot_near), shares))
    near = back_near(idx, cot_near, wo)
    cot_far, near = lax.optimization_barrier((cot_far, near))
    grad, dots, *grads = back(
        idx, both_cores(cot_far), wo, near, far_turned, near_turned, q, k, k_turned, v, shares,
        inverse, rotary, scale,
    )
    grad_query, grad_key, grad_value = finish(lax.psum(tuple(grads), ("x", "z")))
    after = swap(dots)
    out_sum = sum_pieces(
        *[out_terms(idx, other, after, attended, wo, width) for other in (False, True)]
    )
    output_rows = (here_tokens.astype(F32) + out_sum).astype(BF)
    in_sum = sum_pieces(
        *[input_terms(idx, other, after, grad, dots, wq, wk, wv, width) for other in (False, True)]
    )
    inverse = inverse[:, 0:1]
    mean_term = ((in_sum[rows] + in_sum[rows + 1]) / features)[:, None]
    own = y * cores + core
    own_gain = lax.dynamic_slice_in_dim(norm_gain, own * width, width, 0)
    own_scaled = here_tokens.astype(F32) * inverse
    grad_rows = here_cot.astype(F32) + inverse * (in_sum[:rows] * own_gain - own_scaled * mean_term)
    grad_rows = grad_rows.astype(BF)

    targets = panel_plan // count
    output = exchange(output_rows.reshape(dp, panel, width))[targets].reshape(rows, width)
    grad_tokens = exchange(grad_rows.reshape(dp, panel, width))[targets].reshape(rows, width)
    return output, grad_tokens, grad_query, grad_key, grad_value


def solution(mesh):
    axes = ("x", "z", "y", "core")
    split = Mesh(mesh.devices.reshape(4, 4, 4, 2), axes)
    dp, tensor = ("x", "z"), ("y", "core")
    in_specs = (
        P(dp, tensor),
        P(),
        P(dp),
        P(dp),
        P(None, tensor),
        P(None, tensor),
        P(None, tensor),
        P(tensor, None),
        P(dp, tensor),
    )
    out_specs = (
        P(dp, tensor),
        P(dp, tensor),
        P(None, tensor),
        P(None, tensor),
        P(None, tensor),
    )
    return jax.shard_map(
        per_device, mesh=split, in_specs=in_specs, out_specs=out_specs, check_vma=False
    )
```
